512 devices in a mesh: tm: 64 (over y, z), space: 8 (over x, core).
Axes of the slice: x: 4, y: 4, z: 16, core: 2. Of those that a mesh axis runs over, the one named last changes fastest.
Arguments:
- initial: float32 [4, 65536], P(None, 'space'), may hold values from -6 to 6
- guess: float32 [64, 4, 65536], P('tm', None, 'space'), may hold values from -6 to 6
- speeds: float32 [65536], P('space'), may hold values from 0.02 to 0.5
- flags: int32 [65536], P('space'), may hold values 0 or 1
Outputs:
- corrected: float32 [64, 4, 65536], P('tm', None, 'space')
The draws below stay inside these ranges and needn't reach their ends.
All inputs are finite; a program needn't handle non-finite values. No bound on the sum of `flags` on one device may be relied on, other than what follows from the above.
Results may differ from the reference program's by a relative error of at most 0.0003.
Values sent between devices are 32-bit elements; how exact they have to be, the bound alone decides.
No kernel may reach another device: no remote copies, remote signals or barrier semaphores. Data moves between devices by JAX's collectives and lax.ppermute only.
A program may use at most 128 MiB of HBM per device.

```python
import math
import jax
import jax.numpy as jnp
import numpy as np
from jax import lax

MODES = 4
STEPS = 8
ELEMS = 65536
SLABS = 64


def set_ends(entries, rng, low, high):
    dims = entries.shape
    index_at = [jax.random.randint(jax.random.fold_in(rng, axis), (), 0, dims[axis]) for axis in range(len(dims))]
    entries = entries.at[tuple(index_at)].set(low)
    longest = dims.index(max(dims))
    index_at[longest] = (index_at[longest] + 1) % dims[longest]
    return entries.at[tuple(index_at)].set(high)


def steps_of(stream_key, shape, pieces, low, high):
    loudness = 1.0
    for axis_at, shards_of in pieces:
        draws = jax.random.uniform(jax.random.fold_in(jax.random.fold_in(stream_key, 6), axis_at), (shards_of,), jnp.float32, low / len(pieces), high / len(pieces))
        loudness = loudness * jnp.repeat(jnp.exp(draws), shape[axis_at] // shards_of).reshape((-1,) + (1,) * (len(shape) - 1 - axis_at))
    return loudness


def normal_values(stream_key, shape, width, bound, cuts=(), kind=jnp.bfloat16):
    array = jax.random.normal(stream_key, shape, jnp.float32) * width
    if len(cuts) > 0:
        array = steps_of(stream_key, shape, cuts, -0.22, 0.18) * array
    return jnp.clip(array, min=-bound, max=bound).astype(kind)


def setup_inputs(seed: int = 0) -> dict:
    splits = jax.random.split(jax.random.key(seed), 5)
    return {
        "initial": normal_values(splits[0], (MODES, ELEMS), 1.0, 6.0, ((1, 8),), jnp.float32),
        "guess": normal_values(splits[1], (SLABS, MODES, ELEMS), 1.0, 6.0, ((0, 64), (2, 8)), jnp.float32),
        "speeds": jnp.clip(jnp.exp(math.log(0.5) - 3.218876 * jax.random.uniform(splits[2], (ELEMS,), jnp.float32) ** steps_of(splits[2], (ELEMS,), ((0, 8),), -0.2, 0.2)), 0.02, 0.5),
        "flags": set_ends((jax.random.randint(splits[3], (ELEMS,), 0, 16) < 1).astype(jnp.int32), jax.random.fold_in(splits[3], 1), 0, 1),
    }


viscosity = 0.02
penalty = 10.0
step_size = 0.015625
jacobian = 8.0


def basis_tables(count):
    order = np.arange(count)
    right_vals = np.ones(count)
    left_vals = (-1.0) ** order
    right_slope = order * (order + 1) / 2.0
    left_slope = -left_vals * right_slope
    inv_mass = (2.0 * order + 1.0) / 2.0
    row_index = order[:, None]
    col_index = order[None, :]
    odd_sum = (row_index + col_index) % 2
    advect = np.where((row_index > col_index) & (odd_sum == 1), 2.0, 0.0)
    lesser = np.minimum(row_index, col_index)
    stiffness = np.where(odd_sum == 0, lesser * (lesser + 1.0), 0.0)
    return right_vals, left_vals, right_slope, left_slope, inv_mass, advect, stiffness


def column(values, dtype):
    return jnp.asarray(values, dtype)[:, None]


def multiply(table, field):
    return jnp.einsum("ij,je->ie", jnp.asarray(table, field.dtype), field, precision=lax.Precision.HIGHEST)


def spatial_rhs(padded, speed_pad, open_pad):
    dtype = padded.dtype
    right_vals, left_vals, right_slope, left_slope, inv_mass, advect, stiffness = basis_tables(padded.shape[0])
    trace_r = jnp.sum(column(right_vals, dtype) * padded, 0)
    trace_l = jnp.sum(column(left_vals, dtype) * padded, 0)
    slope_r = jnp.sum(column(right_slope, dtype) * padded, 0)
    slope_l = jnp.sum(column(left_slope, dtype) * padded, 0)
    jumps = trace_r[:-1] - trace_l[1:]
    means = 0.5 * (slope_r[:-1] + slope_l[1:])
    gates = open_pad[1:]
    inflow = speed_pad[:-1] * trace_r[:-1] * gates
    center = padded[:, 1:-1]
    speeds = speed_pad[1:-1]
    volume = speeds * multiply(advect, center) - column(right_vals, dtype) * (speeds * trace_r[1:-1])
    volume = volume - viscosity * multiply(stiffness, center) + column(left_vals, dtype) * inflow[:-1]
    right_terms = gates[1:] * (means[1:] * column(right_vals, dtype) + 0.5 * jumps[1:] * column(right_slope, dtype)
                               - penalty * jumps[1:] * column(right_vals, dtype))
    left_terms = gates[:-1] * (-means[:-1] * column(left_vals, dtype) + 0.5 * jumps[:-1] * column(left_slope, dtype)
                               + penalty * jumps[:-1] * column(left_vals, dtype))
    return jacobian * column(inv_mass, dtype) * (volume + viscosity * (right_terms + left_terms))


def local_rhs(state, speeds):
    dtype = state.dtype
    right_vals, left_vals, right_slope, left_slope, inv_mass, advect, stiffness = basis_tables(state.shape[0])
    trace_r = jnp.sum(column(right_vals, dtype) * state, 0)
    volume = speeds * multiply(advect, state) - column(right_vals, dtype) * (speeds * trace_r)
    volume = volume - viscosity * multiply(stiffness, state)
    return jacobian * column(inv_mass, dtype) * volume


def runge_kutta(state, tendency, delta):
    section_one = state + delta * tendency(state)
    section_two = 0.75 * state + 0.25 * (section_one + delta * tendency(section_one))
    return state / 3.0 + (2.0 / 3.0) * (section_two + delta * tendency(section_two))


def coarse_matrices(speeds, count):
    units = jnp.eye(count, dtype=speeds.dtype)[:, :, None] * jnp.ones_like(speeds)[None, None, :]
    columns = jax.vmap(lambda unit: runge_kutta(unit, lambda s: local_rhs(s, speeds), STEPS * step_size))(units)
    return jnp.transpose(columns, (1, 0, 2))


def apply_map(matrices, field):
    return jnp.sum(matrices * field[None, :, :], axis=1)


def reference(initial, guess, speeds, flags):
    dtype = initial.dtype
    place = lax.iota(jnp.int32, speeds.shape[0])
    open_faces = (1 - flags).astype(dtype) * (place > 0).astype(dtype)
    speed_pad = jnp.pad(speeds, 1)
    open_pad = jnp.pad(open_faces, 1)

    def tendency(state):
        return spatial_rhs(jnp.pad(state, ((0, 0), (1, 1))), speed_pad, open_pad)

    def propagate(state):
        return lax.fori_loop(0, STEPS, lambda i, s: runge_kutta(s, tendency, step_size), state)

    starts = jnp.concatenate([initial[None], guess[:-1]], axis=0)
    finals = lax.map(propagate, starts)
    residual = finals - guess
    matrices = coarse_matrices(speeds, initial.shape[0])

    def chain(carry, term):
        result = apply_map(matrices, carry) + term
        return result, result

    zeros = jnp.zeros_like(initial)
    _, correction = lax.scan(chain, zeros, residual)
    return guess + correction
```

```python
import functools

import jax
import jax.numpy as jnp
from jax import lax
from jax.experimental import pallas as pl
from jax.experimental.pallas import tpu as pltpu
from jax.sharding import PartitionSpec as P

MODES = 4
STEPS = 8
LANES = 128
VISCOSITY = 0.02
PENALTY = 10.0
STEP = 0.015625
JACOBIAN = 8.0
INV_MASS = (0.5, 1.5, 2.5, 3.5)


def column_scales(delta):
    return [JACOBIAN * m * delta for m in INV_MASS]


def before(x):
    rolled = pltpu.roll(x, 1, 1)
    lane = lax.broadcasted_iota(jnp.int32, x.shape, 1)
    return jnp.where(lane == 0, pltpu.roll(rolled, 1, 0), rolled)


def after(x):
    rows, lanes = x.shape
    rolled = pltpu.roll(x, lanes - 1, 1)
    lane = lax.broadcasted_iota(jnp.int32, x.shape, 1)
    return jnp.where(lane == lanes - 1, pltpu.roll(rolled, rows - 1, 0), rolled)


def volume_terms(u, speed2, drain, p, q):
    a, b, c, d = u
    vq = (2.0 * VISCOSITY) * q
    m1 = speed2 * a - vq
    m2 = speed2 * b - (6.0 * VISCOSITY) * c
    m3 = speed2 * p - vq - (10.0 * VISCOSITY) * d
    return m1, m2, m3


def local_rhs(u, speed, speed2):
    a, b, c, d = u
    p, q = a + c, b + d
    out = -(speed * (p + q))
    m1, m2, m3 = volume_terms(u, speed2, out, p, q)
    return out, out + m1, out + m2, out + m3


def full_rhs(u, speed, speed2, inflow, gate, gate_after):
    a, b, c, d = u
    p, q = a + c, b + d
    tr, tl = p + q, p - q
    odd, even = b + 6.0 * d, 3.0 * c
    sr, sl = odd + even, odd - even
    tr_b, sr_b = before(tr), before(sr)
    tl_a, sl_a = after(tl), after(sl)
    jump = tr_b - tl
    k_l = gate * jump
    h_l = gate * (sr_b + sl - (2.0 * PENALTY) * jump)
    g_l = inflow * tr_b - h_l
    jump_a = tr - tl_a
    k_r = gate_after * jump_a
    h_r = gate_after * (sr + sl_a - (2.0 * PENALTY) * jump_a)
    base = h_r - speed * tr
    plus, minus = base + g_l, base - g_l
    k_sum, k_dif = k_r + k_l, k_r - k_l
    m1, m2, m3 = volume_terms(u, speed2, base, p, q)
    return plus, minus + k_sum + m1, plus + 3.0 * k_dif + m2, minus + 6.0 * k_sum + m3


def three_sections(u, rhs, delta):
    v = u
    for share in (3.0, 2.0, 1.0):
        scale = column_scales(delta / share)
        v = [x + f * r for x, f, r in zip(u, scale, rhs(v))]
    return v


def fine_kernel(slabs, blocks, guess_ref, initial_ref, left_ref, right_ref, speed_ref, flag_ref, out_ref):
    rows = speed_ref.shape[0]
    wide = rows + 8
    slab, block = lax.axis_index("tm"), lax.axis_index("space")
    last = slab == slabs - 1

    def ring(main, k):
        unused = jnp.zeros((6, LANES), jnp.float32)
        return jnp.concatenate([main, right_ref[pl.ds(k, 1), :], unused, left_ref[pl.ds(k, 1), :]], 0)

    own = []
    for k in range(MODES):
        here = pl.ds(k, rows, stride=MODES)
        own.append(jnp.where(last, initial_ref[here, :], guess_ref[here, :]))
    start = [ring(x, k) for k, x in enumerate(own)]
    speed_own = speed_ref[...]
    open_own = 1.0 - flag_ref[...].astype(jnp.float32)
    speed = ring(speed_own, MODES)
    opened = ring(open_own, MODES + 1)
    row = lax.broadcasted_iota(jnp.int32, (wide, LANES), 0)
    lane = lax.broadcasted_iota(jnp.int32, (wide, LANES), 1)
    first = jnp.logical_and(jnp.logical_and(row == 0, lane == 0), block == 0)
    opened = jnp.where(first, 0.0, opened)
    gate = (0.5 * VISCOSITY) * opened
    gate_after = after(gate)
    inflow = opened * before(speed)
    speed2 = 2.0 * speed

    def rhs(u):
        return full_rhs(u, speed, speed2, inflow, gate, gate_after)

    final = lax.fori_loop(0, STEPS, lambda i, u: tuple(three_sections(u, rhs, STEP)), tuple(start))
    speed2_own = 2.0 * speed_own
    coarse = three_sections(own, lambda u: local_rhs(u, speed_own, speed2_own), STEPS * STEP)
    for k in range(MODES):
        share = jnp.where(last, 0.0, coarse[k])
        out_ref[pl.ds(k, rows, stride=MODES), :] = final[k][:rows] - share


def fine_part(guess, initial, left, right, speeds, flags, slabs, blocks):
    return pl.pallas_call(
        functools.partial(fine_kernel, slabs, blocks),
        out_shape=jax.ShapeDtypeStruct(guess.shape, jnp.float32),
        in_specs=[pl.BlockSpec(memory_space=pltpu.VMEM)] * 6,
        out_specs=pl.BlockSpec(memory_space=pltpu.VMEM),
        compiler_params=pltpu.CompilerParams(vmem_limit_bytes=16 * 1024 * 1024),
        cost_estimate=pl.CostEstimate(flops=24 * 60 * 8192, bytes_accessed=4 * guess.size * 4, transcendentals=0),
        name="fine_steps",
    )(guess, initial, left, right, speeds, flags)


def times(matrix, field):
    return [sum(matrix[i][j] * field[j] for j in range(1, MODES)) + matrix[i][0] * field[0] for i in range(MODES)]


def square(matrix):
    columns = [times(matrix, [matrix[i][j] for i in range(MODES)]) for j in range(MODES)]
    return [[columns[j][i] for j in range(MODES)] for i in range(MODES)]


def scan_kernel(group, term_ref, speed_ref, out_ref):
    slabs = term_ref.shape[0] // MODES
    groups = slabs // group
    shape = (groups, LANES)
    row = lax.broadcasted_iota(jnp.int32, shape, 0)
    speed = jnp.broadcast_to(speed_ref[pl.ds(lax.axis_index("tm"), 1), :], shape)
    speed2 = 2.0 * speed
    zero, one = jnp.zeros(shape, jnp.float32), jnp.ones(shape, jnp.float32)
    columns = [
        three_sections([one if i == j else zero for i in range(MODES)], lambda u: local_rhs(u, speed, speed2), STEPS * STEP)
        for j in range(MODES)
    ]
    matrix = [[columns[j][i] for j in range(MODES)] for i in range(MODES)]

    def term(i):
        source = (i - 1) % group
        read = [term_ref[pl.ds(source * MODES + k, groups, stride=group * MODES), :] for k in range(MODES)]
        return [pltpu.roll(x, 1, 0) for x in read] if i == 0 else read

    sums = [term(0)]
    for i in range(1, group):
        sums.append([x + y for x, y in zip(times(matrix, sums[-1]), term(i))])
    power, size = matrix, 1
    while size < group:
        power, size = square(power), 2 * size
    total, reach = sums[-1], 1
    while reach < groups:
        earlier = [jnp.where(row >= reach, pltpu.roll(x, reach, 0), 0.0) for x in total]
        total = [x + y for x, y in zip(total, times(power, earlier))]
        reach *= 2
        if reach < groups:
            power = square(power)
    carry = [jnp.where(row >= 1, pltpu.roll(x, 1, 0), 0.0) for x in total]
    for i in range(group):
        carry = times(matrix, carry)
        for k in range(MODES):
            out_ref[pl.ds(i * MODES + k, groups, stride=group * MODES), :] = sums[i][k] + carry[k]


def scan_part(terms, speeds):
    return pl.pallas_call(
        functools.partial(scan_kernel, 8),
        out_shape=jax.ShapeDtypeStruct(terms.shape, jnp.float32),
        in_specs=[pl.BlockSpec(memory_space=pltpu.VMEM)] * 2,
        out_specs=pl.BlockSpec(memory_space=pltpu.VMEM),
        name="slab_scan",
    )(terms, speeds)


def body(initial, guess, speeds, flags):
    slabs, blocks = lax.axis_size("tm"), lax.axis_size("space")
    count = initial.shape[1]
    rows = count // LANES

    def by_row(x):
        return x.reshape(MODES, rows, LANES).transpose(1, 0, 2).reshape(rows * MODES, LANES)

    last = lax.axis_index("tm") == slabs - 1

    def strip(lo):
        cut = slice(lo, lo + LANES)
        state = jnp.where(last, initial[:, cut], guess[0][:, cut])
        coefs = jnp.stack([speeds[cut], (1 - flags[cut]).astype(jnp.float32)])
        return jnp.concatenate([state, coefs, jnp.zeros((2, LANES), jnp.float32)], 0)

    left = lax.ppermute(strip(count - LANES), "space", [(i, i + 1) for i in range(blocks - 1)])
    right = lax.ppermute(strip(0), "space", [(i + 1, i) for i in range(blocks - 1)])
    speed_rows = speeds.reshape(rows, LANES)
    terms = fine_part(
        by_row(guess[0]), by_row(initial), left, right, speed_rows, flags.reshape(rows, LANES), slabs, blocks
    )
    terms = lax.all_to_all(terms.reshape(rows, MODES, LANES), "tm", 0, 0, tiled=True)
    sums = scan_part(terms.reshape(rows * MODES, LANES), speed_rows)
    sums = lax.all_to_all(sums.reshape(rows, MODES, LANES), "tm", 0, 0, tiled=True)
    return sums.transpose(1, 0, 2).reshape(1, MODES, count)


def solution(mesh):
    return jax.shard_map(
        body,
        mesh=mesh,
        in_specs=(P(None, "space"), P("tm", None, "space"), P("space"), P("space")),
        out_specs=P("tm", None, "space"),
        check_vma=False,
    )
```

```python
import functools

import jax
import jax.numpy as jnp
from jax import lax
from jax.experimental import pallas as pl
from jax.experimental.pallas import tpu as pltpu
from jax.sharding import PartitionSpec as P

MODES = 4
STEPS = 8
LANES = 128
VISCOSITY = 0.02
PENALTY = 10.0
STEP = 0.015625
JACOBIAN = 8.0
INV_MASS = (0.5, 1.5, 2.5, 3.5)


def column_scales(delta):
    return [JACOBIAN * m * delta for m in INV_MASS]


def before(x):
    rolled = pltpu.roll(x, 1, 1)
    lane = lax.broadcasted_iota(jnp.int32, x.shape, 1)
    return jnp.where(lane == 0, pltpu.roll(rolled, 1, 0), rolled)


def after(x):
    rows, lanes = x.shape
    rolled = pltpu.roll(x, lanes - 1, 1)
    lane = lax.broadcasted_iota(jnp.int32, x.shape, 1)
    return jnp.where(lane == lanes - 1, pltpu.roll(rolled, rows - 1, 0), rolled)


def volume_terms(u, speed2, drain, p, q):
    a, b, c, d = u
    vq = (2.0 * VISCOSITY) * q
    m1 = speed2 * a - vq
    m2 = speed2 * b - (6.0 * VISCOSITY) * c
    m3 = speed2 * p - vq - (10.0 * VISCOSITY) * d
    return m1, m2, m3


def local_rhs(u, speed, speed2):
    a, b, c, d = u
    p, q = a + c, b + d
    out = -(speed * (p + q))
    m1, m2, m3 = volume_terms(u, speed2, out, p, q)
    return out, out + m1, out + m2, out + m3


def full_rhs(u, speed, speed2, inflow, gate, gate_after):
    a, b, c, d = u
    p, q = a + c, b + d
    tr, tl = p + q, p - q
    odd, even = b + 6.0 * d, 3.0 * c
    sr, sl = odd + even, odd - even
    tr_b, sr_b = before(tr), before(sr)
    tl_a, sl_a = after(tl), after(sl)
    jump = tr_b - tl
    k_l = gate * jump
    h_l = gate * (sr_b + sl - (2.0 * PENALTY) * jump)
    g_l = inflow * tr_b - h_l
    jump_a = tr - tl_a
    k_r = gate_after * jump_a
    h_r = gate_after * (sr + sl_a - (2.0 * PENALTY) * jump_a)
    base = h_r - speed * tr
    plus, minus = base + g_l, base - g_l
    k_sum, k_dif = k_r + k_l, k_r - k_l
    m1, m2, m3 = volume_terms(u, speed2, base, p, q)
    return plus, minus + k_sum + m1, plus + 3.0 * k_dif + m2, minus + 6.0 * k_sum + m3


def three_sections(u, rhs, delta):
    v = u
    for share in (3.0, 2.0, 1.0):
        scale = column_scales(delta / share)
        v = [x + f * r for x, f, r in zip(u, scale, rhs(v))]
    return v


def strip_kernel(state_ref, speed_ref, flag_ref, head_ref, tail_ref):
    rows = speed_ref.shape[0]
    for ref, row in ((head_ref, 0), (tail_ref, rows - 1)):
        ref[pl.ds(0, MODES), :] = state_ref[pl.ds(row * MODES, MODES), :]
        ref[pl.ds(MODES, 1), :] = speed_ref[pl.ds(row, 1), :]
        ref[pl.ds(MODES + 1, 1), :] = 1.0 - flag_ref[pl.ds(row, 1), :].astype(jnp.float32)
        ref[pl.ds(MODES + 2, 2), :] = jnp.zeros((2, LANES), jnp.float32)


def strip_part(state, speeds, flags):
    strip = jax.ShapeDtypeStruct((8, LANES), jnp.float32)
    return pl.pallas_call(
        strip_kernel,
        out_shape=[strip, strip],
        in_specs=[pl.BlockSpec(memory_space=pltpu.VMEM)] * 3,
        out_specs=[pl.BlockSpec(memory_space=pltpu.VMEM)] * 2,
        name="end_strips",
    )(state, speeds, flags)


def fine_kernel(slabs, state_ref, speed_ref, flag_ref, left_ref, right_ref, out_ref):
    rows = speed_ref.shape[0]
    wide = rows + 8
    last = lax.axis_index("tm") == slabs - 1
    block = lax.axis_index("space")

    def ring(main, k):
        unused = jnp.zeros((6, LANES), jnp.float32)
        return jnp.concatenate([main, right_ref[pl.ds(k, 1), :], unused, left_ref[pl.ds(k, 1), :]], 0)

    own = [state_ref[pl.ds(k, rows, stride=MODES), :] for k in range(MODES)]
    start = [ring(x, k) for k, x in enumerate(own)]
    speed_own = speed_ref[...]
    speed = ring(speed_own, MODES)
    opened = ring(1.0 - flag_ref[...].astype(jnp.float32), MODES + 1)
    row = lax.broadcasted_iota(jnp.int32, (wide, LANES), 0)
    lane = lax.broadcasted_iota(jnp.int32, (wide, LANES), 1)
    first = jnp.logical_and(jnp.logical_and(row == 0, lane == 0), block == 0)
    opened = jnp.where(first, 0.0, opened)
    gate = (0.5 * VISCOSITY) * opened
    gate_after = after(gate)
    inflow = opened * before(speed)
    speed2 = 2.0 * speed

    def rhs(u):
        return full_rhs(u, speed, speed2, inflow, gate, gate_after)

    final = lax.fori_loop(0, STEPS, lambda i, u: tuple(three_sections(u, rhs, STEP)), tuple(start))
    speed2_own = 2.0 * speed_own
    coarse = three_sections(own, lambda u: local_rhs(u, speed_own, speed2_own), STEPS * STEP)
    for k in range(MODES):
        share = jnp.where(last, 0.0, coarse[k])
        out_ref[pl.ds(k, rows, stride=MODES), :] = final[k][:rows] - share


def fine_part(state, speeds, flags, left, right, slabs):
    return pl.pallas_call(
        functools.partial(fine_kernel, slabs),
        out_shape=jax.ShapeDtypeStruct(state.shape, jnp.float32),
        in_specs=[pl.BlockSpec(memory_space=pltpu.VMEM)] * 5,
        out_specs=pl.BlockSpec(memory_space=pltpu.VMEM),
        compiler_params=pltpu.CompilerParams(vmem_limit_bytes=16 * 1024 * 1024),
        cost_estimate=pl.CostEstimate(flops=24 * 60 * 8192, bytes_accessed=2 * state.size * 4, transcendentals=0),
        name="fine_steps",
    )(state, speeds, flags, left, right)


def times(matrix, field):
    return [sum(matrix[i][j] * field[j] for j in range(1, MODES)) + matrix[i][0] * field[0] for i in range(MODES)]


def square(matrix):
    columns = [times(matrix, [matrix[i][j] for i in range(MODES)]) for j in range(MODES)]
    return [[columns[j][i] for j in range(MODES)] for i in range(MODES)]


def scan_kernel(group, term_ref, speed_ref, out_ref):
    slabs = term_ref.shape[0] // MODES
    groups = slabs // group
    shape = (groups, LANES)
    row = lax.broadcasted_iota(jnp.int32, shape, 0)
    speed = jnp.broadcast_to(speed_ref[pl.ds(lax.axis_index("tm"), 1), :], shape)
    speed2 = 2.0 * speed
    zero, one = jnp.zeros(shape, jnp.float32), jnp.ones(shape, jnp.float32)
    columns = [
        three_sections([one if i == j else zero for i in range(MODES)], lambda u: local_rhs(u, speed, speed2), STEPS * STEP)
        for j in range(MODES)
    ]
    matrix = [[columns[j][i] for j in range(MODES)] for i in range(MODES)]

    def term(i):
        source = (i - 1) % group
        read = [term_ref[pl.ds(source * MODES + k, groups, stride=group * MODES), :] for k in range(MODES)]
        return [pltpu.roll(x, 1, 0) for x in read] if i == 0 else read

    sums = [term(0)]
    for i in range(1, group):
        sums.append([x + y for x, y in zip(times(matrix, sums[-1]), term(i))])
    power, size = matrix, 1
    while size < group:
        power, size = square(power), 2 * size
    total, reach = sums[-1], 1
    while reach < groups:
        earlier = [jnp.where(row >= reach, pltpu.roll(x, reach, 0), 0.0) for x in total]
        total = [x + y for x, y in zip(total, times(power, earlier))]
        reach *= 2
        if reach < groups:
            power = square(power)
    carry = [jnp.where(row >= 1, pltpu.roll(x, 1, 0), 0.0) for x in total]
    for i in range(group):
        carry = times(matrix, carry)
        for k in range(MODES):
            out_ref[pl.ds(i * MODES + k, groups, stride=group * MODES), :] = sums[i][k] + carry[k]


def scan_part(terms, speeds):
    return pl.pallas_call(
        functools.partial(scan_kernel, 8),
        out_shape=jax.ShapeDtypeStruct(terms.shape, jnp.float32),
        in_specs=[pl.BlockSpec(memory_space=pltpu.VMEM)] * 2,
        out_specs=pl.BlockSpec(memory_space=pltpu.VMEM),
        name="slab_scan",
    )(terms, speeds)


def body(initial, guess, speeds, flags):
    slabs, blocks = lax.axis_size("tm"), lax.axis_size("space")
    count = initial.shape[1]
    rows = count // LANES

    def by_row(x):
        return x.reshape(MODES, rows, LANES).transpose(1, 0, 2).reshape(rows * MODES, LANES)

    speed_rows, flag_rows = speeds.reshape(rows, LANES), flags.reshape(rows, LANES)
    last = lax.axis_index("tm") == slabs - 1
    state = by_row(jnp.where(last, initial, guess[0]))
    head, tail = strip_part(state, speed_rows, flag_rows)
    left = lax.ppermute(tail, "space", [(i, i + 1) for i in range(blocks - 1)])
    right = lax.ppermute(head, "space", [(i + 1, i) for i in range(blocks - 1)])
    terms = fine_part(state, speed_rows, flag_rows, left, right, slabs)
    terms = lax.all_to_all(terms.reshape(rows, MODES, LANES), "tm", 0, 0, tiled=True)
    sums = scan_part(terms.reshape(rows * MODES, LANES), speed_rows)
    sums = lax.all_to_all(sums.reshape(rows, MODES, LANES), "tm", 0, 0, tiled=True)
    return sums.transpose(1, 0, 2).reshape(1, MODES, count)


def solution(mesh):
    return jax.shard_map(
        body,
        mesh=mesh,
        in_specs=(P(None, "space"), P("tm", None, "space"), P("space"), P("space")),
        out_specs=P("tm", None, "space"),
        check_vma=False,
    )
```

```python
import functools

import jax
import jax.numpy as jnp
from jax import lax
from jax.experimental import pallas as pl
from jax.experimental.pallas import tpu as pltpu
from jax.sharding import PartitionSpec as P

MODES = 4
STEPS = 8
LANES = 128
ROWS = 8
VISCOSITY = 0.02
PENALTY = 10.0
STEP = 0.015625
JACOBIAN = 8.0
INV_MASS = (0.5, 1.5, 2.5, 3.5)


def column_scales(delta):
    return [JACOBIAN * m * delta for m in INV_MASS]


def before(x):
    rolled = pltpu.roll(x, 1, 1)
    lane = lax.broadcasted_iota(jnp.int32, x.shape, 1)
    return jnp.where(lane == 0, pltpu.roll(rolled, 1, 0), rolled)


def after(x):
    rows, lanes = x.shape
    rolled = pltpu.roll(x, lanes - 1, 1)
    lane = lax.broadcasted_iota(jnp.int32, x.shape, 1)
    return jnp.where(lane == lanes - 1, pltpu.roll(rolled, rows - 1, 0), rolled)


def volume_terms(u, speed2, drain, p, q):
    a, b, c, d = u
    vq = (2.0 * VISCOSITY) * q
    m1 = speed2 * a - vq
    m2 = speed2 * b - (6.0 * VISCOSITY) * c
    m3 = speed2 * p - vq - (10.0 * VISCOSITY) * d
    return m1, m2, m3


def local_rhs(u, speed, speed2):
    a, b, c, d = u
    p, q = a + c, b + d
    out = -(speed * (p + q))
    m1, m2, m3 = volume_terms(u, speed2, out, p, q)
    return out, out + m1, out + m2, out + m3


def full_rhs(u, speed, speed2, inflow, gate, gate_after):
    a, b, c, d = u
    p, q = a + c, b + d
    tr, tl = p + q, p - q
    odd, even = b + 6.0 * d, 3.0 * c
    sr, sl = odd + even, odd - even
    tr_b, sr_b = before(tr), before(sr)
    tl_a, sl_a = after(tl), after(sl)
    jump = tr_b - tl
    k_l = gate * jump
    h_l = gate * (sr_b + sl - (2.0 * PENALTY) * jump)
    g_l = inflow * tr_b - h_l
    jump_a = tr - tl_a
    k_r = gate_after * jump_a
    h_r = gate_after * (sr + sl_a - (2.0 * PENALTY) * jump_a)
    base = h_r - speed * tr
    plus, minus = base + g_l, base - g_l
    k_sum, k_dif = k_r + k_l, k_r - k_l
    m1, m2, m3 = volume_terms(u, speed2, base, p, q)
    return plus, minus + k_sum + m1, plus + 3.0 * k_dif + m2, minus + 6.0 * k_sum + m3


def three_sections(u, rhs, delta):
    v = u
    for share in (3.0, 2.0, 1.0):
        scale = column_scales(delta / share)
        v = [x + f * r for x, f, r in zip(u, scale, rhs(v))]
    return v


def strip_kernel(slabs, guess_ref, initial_ref, speed_ref, flag_ref, near_ref, far_ref, states, speeds, flags, sems):
    rows = speed_ref.shape[0]
    last = lax.axis_index("tm") == slabs - 1
    ends = (0, 1)

    def tile(ref, end):
        return ref.at[pl.ds(end * (ref.shape[0] - ROWS), ROWS)]

    def copies(source):
        return [pltpu.make_async_copy(tile(source, e), states.at[e], sems.at[e]) for e in ends]

    others = [pltpu.make_async_copy(tile(speed_ref, e), speeds.at[e], sems.at[2 + e]) for e in ends]
    others += [pltpu.make_async_copy(tile(flag_ref, e), flags.at[e], sems.at[4 + e]) for e in ends]

    @pl.when(last)
    def _():
        for copy in copies(initial_ref):
            copy.start()

    @pl.when(jnp.logical_not(last))
    def _():
        for copy in copies(guess_ref):
            copy.start()

    for copy in others:
        copy.start()
    for copy in others + copies(guess_ref):
        copy.wait()
    strips = []
    for end in ends:
        row = end * (ROWS - 1)
        state = states[end, pl.ds(end * (ROWS - MODES), MODES), :]
        opened = 1.0 - flags[end, pl.ds(row, 1), :].astype(jnp.float32)
        unused = jnp.zeros((2, LANES), jnp.float32)
        strips.append(jnp.concatenate([state, speeds[end, pl.ds(row, 1), :], opened, unused], 0))
    head, tail = strips
    even = lax.axis_index("space") % 2 == 0
    near_ref[...] = jnp.where(even, tail, head)
    far_ref[...] = jnp.where(even, head, tail)


def strip_part(guess, initial, speeds, flags, slabs):
    strip = jax.ShapeDtypeStruct((ROWS, LANES), jnp.float32)
    return pl.pallas_call(
        functools.partial(strip_kernel, slabs),
        out_shape=[strip, strip],
        in_specs=[pl.BlockSpec(memory_space=pltpu.HBM)] * 4,
        out_specs=[pl.BlockSpec(memory_space=pltpu.VMEM)] * 2,
        scratch_shapes=[
            pltpu.VMEM((2, ROWS, LANES), jnp.float32),
            pltpu.VMEM((2, ROWS, LANES), jnp.float32),
            pltpu.VMEM((2, ROWS, LANES), jnp.int32),
            pltpu.SemaphoreType.DMA((6,)),
        ],
        compiler_params=pltpu.CompilerParams(vmem_limit_bytes=60 * 1024 * 1024),
        name="end_strips",
    )(guess, initial, speeds, flags)


def fine_kernel(slabs, state_ref, speed_ref, flag_ref, near_ref, far_ref, out_ref):
    rows = speed_ref.shape[0]
    wide = rows + 8
    last = lax.axis_index("tm") == slabs - 1
    block = lax.axis_index("space")
    even = block % 2 == 0
    near, far = near_ref[...], far_ref[...]
    left, right = jnp.where(even, far, near), jnp.where(even, near, far)

    def ring(main, k):
        unused = jnp.zeros((6, LANES), jnp.float32)
        return jnp.concatenate([main, right[k : k + 1], unused, left[k : k + 1]], 0)

    own = [state_ref[pl.ds(k, rows, stride=MODES), :] for k in range(MODES)]
    start = [ring(x, k) for k, x in enumerate(own)]
    speed_own = speed_ref[...]
    speed = ring(speed_own, MODES)
    opened = ring(1.0 - flag_ref[...].astype(jnp.float32), MODES + 1)
    row = lax.broadcasted_iota(jnp.int32, (wide, LANES), 0)
    lane = lax.broadcasted_iota(jnp.int32, (wide, LANES), 1)
    first = jnp.logical_and(jnp.logical_and(row == 0, lane == 0), block == 0)
    opened = jnp.where(first, 0.0, opened)
    gate = (0.5 * VISCOSITY) * opened
    gate_after = after(gate)
    inflow = opened * before(speed)
    speed2 = 2.0 * speed

    def rhs(u):
        return full_rhs(u, speed, speed2, inflow, gate, gate_after)

    final = lax.fori_loop(0, STEPS, lambda i, u: tuple(three_sections(u, rhs, STEP)), tuple(start))
    speed2_own = 2.0 * speed_own
    coarse = three_sections(own, lambda u: local_rhs(u, speed_own, speed2_own), STEPS * STEP)
    for k in range(MODES):
        share = jnp.where(last, 0.0, coarse[k])
        out_ref[pl.ds(k, rows, stride=MODES), :] = final[k][:rows] - share


def fine_part(state, speeds, flags, near, far, slabs):
    return pl.pallas_call(
        functools.partial(fine_kernel, slabs),
        out_shape=jax.ShapeDtypeStruct(state.shape, jnp.float32),
        in_specs=[pl.BlockSpec(memory_space=pltpu.VMEM)] * 5,
        out_specs=pl.BlockSpec(memory_space=pltpu.VMEM),
        compiler_params=pltpu.CompilerParams(vmem_limit_bytes=16 * 1024 * 1024),
        cost_estimate=pl.CostEstimate(flops=24 * 60 * 8192, bytes_accessed=2 * state.size * 4, transcendentals=0),
        name="fine_steps",
    )(state, speeds, flags, near, far)


def times(matrix, field):
    return [sum(matrix[i][j] * field[j] for j in range(1, MODES)) + matrix[i][0] * field[0] for i in range(MODES)]


def square(matrix):
    columns = [times(matrix, [matrix[i][j] for i in range(MODES)]) for j in range(MODES)]
    return [[columns[j][i] for j in range(MODES)] for i in range(MODES)]


def scan_kernel(group, term_ref, speed_ref, out_ref):
    slabs = term_ref.shape[0] // MODES
    groups = slabs // group
    shape = (groups, LANES)
    row = lax.broadcasted_iota(jnp.int32, shape, 0)
    speed = jnp.broadcast_to(speed_ref[pl.ds(lax.axis_index("tm"), 1), :], shape)
    speed2 = 2.0 * speed
    zero, one = jnp.zeros(shape, jnp.float32), jnp.ones(shape, jnp.float32)
    columns = [
        three_sections([one if i == j else zero for i in range(MODES)], lambda u: local_rhs(u, speed, speed2), STEPS * STEP)
        for j in range(MODES)
    ]
    matrix = [[columns[j][i] for j in range(MODES)] for i in range(MODES)]

    def term(i):
        source = (i - 1) % group
        read = [term_ref[pl.ds(source * MODES + k, groups, stride=group * MODES), :] for k in range(MODES)]
        return [pltpu.roll(x, 1, 0) for x in read] if i == 0 else read

    sums = [term(0)]
    for i in range(1, group):
        sums.append([x + y for x, y in zip(times(matrix, sums[-1]), term(i))])
    power, size = matrix, 1
    while size < group:
        power, size = square(power), 2 * size
    total, reach = sums[-1], 1
    while reach < groups:
        earlier = [jnp.where(row >= reach, pltpu.roll(x, reach, 0), 0.0) for x in total]
        total = [x + y for x, y in zip(total, times(power, earlier))]
        reach *= 2
        if reach < groups:
            power = square(power)
    carry = [jnp.where(row >= 1, pltpu.roll(x, 1, 0), 0.0) for x in total]
    for i in range(group):
        carry = times(matrix, carry)
        for k in range(MODES):
            out_ref[pl.ds(i * MODES + k, groups, stride=group * MODES), :] = sums[i][k] + carry[k]


def scan_part(terms, speeds):
    return pl.pallas_call(
        functools.partial(scan_kernel, 8),
        out_shape=jax.ShapeDtypeStruct(terms.shape, jnp.float32),
        in_specs=[pl.BlockSpec(memory_space=pltpu.VMEM)] * 2,
        out_specs=pl.BlockSpec(memory_space=pltpu.VMEM),
        name="slab_scan",
    )(terms, speeds)


def body(initial, guess, speeds, flags):
    slabs, blocks = lax.axis_size("tm"), lax.axis_size("space")
    count = initial.shape[1]
    rows = count // LANES

    def by_row(x):
        return x.reshape(MODES, rows, LANES).transpose(1, 0, 2).reshape(rows * MODES, LANES)

    speed_rows, flag_rows = speeds.reshape(rows, LANES), flags.reshape(rows, LANES)
    near, far = strip_part(by_row(guess[0]), by_row(initial), speed_rows, flag_rows, slabs)
    ours, _ = lax.optimization_barrier((guess[0], near))
    far = lax.ppermute(far, "space", [p for i in range(1, blocks - 1, 2) for p in ((i, i + 1), (i + 1, i))])
    near = lax.ppermute(near, "space", [p for i in range(0, blocks, 2) for p in ((i, i + 1), (i + 1, i))])
    state = by_row(jnp.where(lax.axis_index("tm") == slabs - 1, initial, ours))
    terms = fine_part(state, speed_rows, flag_rows, near, far, slabs)
    terms = lax.all_to_all(terms.reshape(rows, MODES, LANES), "tm", 0, 0, tiled=True)
    sums = scan_part(terms.reshape(rows * MODES, LANES), speed_rows)
    sums = lax.all_to_all(sums.reshape(rows, MODES, LANES), "tm", 0, 0, tiled=True)
    return sums.transpose(1, 0, 2).reshape(1, MODES, count)


def solution(mesh):
    return jax.shard_map(
        body,
        mesh=mesh,
        in_specs=(P(None, "space"), P("tm", None, "space"), P("space"), P("space")),
        out_specs=P("tm", None, "space"),
        check_vma=False,
    )
```

```python
import functools

import jax
import jax.numpy as jnp
from jax import lax
from jax.experimental import pallas as pl
from jax.experimental.pallas import tpu as pltpu
from jax.sharding import PartitionSpec as P

MODES = 4
STEPS = 8
LANES = 128
ROWS = 8
VISCOSITY = 0.02
PENALTY = 10.0
STEP = 0.015625
JACOBIAN = 8.0
INV_MASS = (0.5, 1.5, 2.5, 3.5)


def column_scales(delta):
    return [JACOBIAN * m * delta for m in INV_MASS]


def before(x):
    rolled = pltpu.roll(x, 1, 1)
    lane = lax.broadcasted_iota(jnp.int32, x.shape, 1)
    return jnp.where(lane == 0, pltpu.roll(rolled, 1, 0), rolled)


def after(x):
    rows, lanes = x.shape
    rolled = pltpu.roll(x, lanes - 1, 1)
    lane = lax.broadcasted_iota(jnp.int32, x.shape, 1)
    return jnp.where(lane == lanes - 1, pltpu.roll(rolled, rows - 1, 0), rolled)


def volume_terms(u, speed2, drain, p, q):
    a, b, c, d = u
    vq = (2.0 * VISCOSITY) * q
    m1 = speed2 * a - vq
    m2 = speed2 * b - (6.0 * VISCOSITY) * c
    m3 = speed2 * p - vq - (10.0 * VISCOSITY) * d
    return m1, m2, m3


def local_rhs(u, speed, speed2):
    a, b, c, d = u
    p, q = a + c, b + d
    out = -(speed * (p + q))
    m1, m2, m3 = volume_terms(u, speed2, out, p, q)
    return out, out + m1, out + m2, out + m3


def full_rhs(u, speed, speed2, inflow, gate, gate_after):
    a, b, c, d = u
    p, q = a + c, b + d
    tr, tl = p + q, p - q
    odd, even = b + 6.0 * d, 3.0 * c
    sr, sl = odd + even, odd - even
    tr_b, sr_b = before(tr), before(sr)
    tl_a, sl_a = after(tl), after(sl)
    jump = tr_b - tl
    k_l = gate * jump
    h_l = gate * (sr_b + sl - (2.0 * PENALTY) * jump)
    g_l = inflow * tr_b - h_l
    jump_a = tr - tl_a
    k_r = gate_after * jump_a
    h_r = gate_after * (sr + sl_a - (2.0 * PENALTY) * jump_a)
    base = h_r - speed * tr
    plus, minus = base + g_l, base - g_l
    k_sum, k_dif = k_r + k_l, k_r - k_l
    m1, m2, m3 = volume_terms(u, speed2, base, p, q)
    return plus, minus + k_sum + m1, plus + 3.0 * k_dif + m2, minus + 6.0 * k_sum + m3


def three_sections(u, rhs, delta):
    v = u
    for share in (3.0, 2.0, 1.0):
        scale = column_scales(delta / share)
        v = [x + f * r for x, f, r in zip(u, scale, rhs(v))]
    return v


def strip_kernel(slabs, guess_ref, initial_ref, speed_ref, flag_ref, near_ref, far_ref, states, speeds, flags, sems):
    rows = speed_ref.shape[0]
    last = lax.axis_index("tm") == slabs - 1
    ends = (0, 1)

    def tile(ref, end):
        return ref.at[pl.ds(end * (ref.shape[0] - ROWS), ROWS)]

    def copies(source):
        return [pltpu.make_async_copy(tile(source, e), states.at[e], sems.at[e]) for e in ends]

    others = [pltpu.make_async_copy(tile(speed_ref, e), speeds.at[e], sems.at[2 + e]) for e in ends]
    others += [pltpu.make_async_copy(tile(flag_ref, e), flags.at[e], sems.at[4 + e]) for e in ends]

    @pl.when(last)
    def _():
        for copy in copies(initial_ref):
            copy.start()

    @pl.when(jnp.logical_not(last))
    def _():
        for copy in copies(guess_ref):
            copy.start()

    for copy in others:
        copy.start()
    for copy in others + copies(guess_ref):
        copy.wait()
    strips = []
    for end in ends:
        row = end * (ROWS - 1)
        state = states[end, pl.ds(end * (ROWS - MODES), MODES), :]
        opened = 1.0 - flags[end, pl.ds(row, 1), :].astype(jnp.float32)
        unused = jnp.zeros((2, LANES), jnp.float32)
        strips.append(jnp.concatenate([state, speeds[end, pl.ds(row, 1), :], opened, unused], 0))
    head, tail = strips
    even = lax.axis_index("space") % 2 == 0
    near_ref[...] = jnp.where(even, tail, head)
    far_ref[...] = jnp.where(even, head, tail)


def strip_part(guess, initial, speeds, flags, slabs):
    strip = jax.ShapeDtypeStruct((ROWS, LANES), jnp.float32)
    return pl.pallas_call(
        functools.partial(strip_kernel, slabs),
        out_shape=[strip, strip],
        in_specs=[pl.BlockSpec(memory_space=pltpu.HBM)] * 4,
        out_specs=[pl.BlockSpec(memory_space=pltpu.VMEM)] * 2,
        scratch_shapes=[
            pltpu.VMEM((2, ROWS, LANES), jnp.float32),
            pltpu.VMEM((2, ROWS, LANES), jnp.float32),
            pltpu.VMEM((2, ROWS, LANES), jnp.int32),
            pltpu.SemaphoreType.DMA((6,)),
        ],
        compiler_params=pltpu.CompilerParams(vmem_limit_bytes=60 * 1024 * 1024),
        name="end_strips",
    )(guess, initial, speeds, flags)


def fine_kernel(slabs, state_ref, speed_ref, flag_ref, near_ref, far_ref, out_ref):
    rows = speed_ref.shape[0]
    wide = rows + 8
    last = lax.axis_index("tm") == slabs - 1
    block = lax.axis_index("space")
    even = block % 2 == 0
    near, far = near_ref[...], far_ref[...]
    left, right = jnp.where(even, far, near), jnp.where(even, near, far)

    def ring(main, k):
        unused = jnp.zeros((6, LANES), jnp.float32)
        return jnp.concatenate([main, right[k : k + 1], unused, left[k : k + 1]], 0)

    own = [state_ref[pl.ds(k, rows, stride=MODES), :] for k in range(MODES)]
    start = [ring(x, k) for k, x in enumerate(own)]
    speed_own = speed_ref[...]
    speed = ring(speed_own, MODES)
    opened = ring(1.0 - flag_ref[...].astype(jnp.float32), MODES + 1)
    row = lax.broadcasted_iota(jnp.int32, (wide, LANES), 0)
    lane = lax.broadcasted_iota(jnp.int32, (wide, LANES), 1)
    first = jnp.logical_and(jnp.logical_and(row == 0, lane == 0), block == 0)
    opened = jnp.where(first, 0.0, opened)
    gate = (0.5 * VISCOSITY) * opened
    gate_after = after(gate)
    inflow = opened * before(speed)
    speed2 = 2.0 * speed

    def rhs(u):
        return full_rhs(u, speed, speed2, inflow, gate, gate_after)

    final = lax.fori_loop(0, STEPS, lambda i, u: tuple(three_sections(u, rhs, STEP)), tuple(start))
    speed2_own = 2.0 * speed_own
    coarse = three_sections(own, lambda u: local_rhs(u, speed_own, speed2_own), STEPS * STEP)
    for k in range(MODES):
        share = jnp.where(last, 0.0, coarse[k])
        out_ref[pl.ds(k, rows, stride=MODES), :] = final[k][:rows] - share


def fine_part(state, speeds, flags, near, far, slabs):
    return pl.pallas_call(
        functools.partial(fine_kernel, slabs),
        out_shape=jax.ShapeDtypeStruct(state.shape, jnp.float32),
        in_specs=[pl.BlockSpec(memory_space=pltpu.VMEM)] * 5,
        out_specs=pl.BlockSpec(memory_space=pltpu.VMEM),
        compiler_params=pltpu.CompilerParams(vmem_limit_bytes=16 * 1024 * 1024),
        cost_estimate=pl.CostEstimate(flops=24 * 60 * 8192, bytes_accessed=2 * state.size * 4, transcendentals=0),
        name="fine_steps",
    )(state, speeds, flags, near, far)


def times(matrix, field):
    out = []
    for row in matrix:
        total = row[0] * field[0]
        for entry, value in zip(row[1:], field[1:]):
            total = total + entry * value
        out.append(total)
    return out


def square(matrix):
    columns = [times(matrix, [matrix[i][j] for i in range(MODES)]) for j in range(MODES)]
    return [[columns[j][i] for j in range(MODES)] for i in range(MODES)]


def added(xs, ys):
    return [x + y for x, y in zip(xs, ys)]


def chosen(test, xs, ys):
    return [jnp.where(test, x, y) for x, y in zip(xs, ys)]


QUAD = 4
CHUNK = 4
HALVES = 2


def place():
    slab = lax.axis_index("tm")
    y, z = slab // (QUAD * QUAD), slab % (QUAD * QUAD)
    return z // QUAD, (z % QUAD) * QUAD + y


def coarse_matrix(speed_ref, chunk):
    rows = [speed_ref[pl.ds(chunk * CHUNK + r, 1), :] for r in range(CHUNK)]
    speed = jnp.concatenate(rows * (ROWS // CHUNK), 0)
    speed2 = 2.0 * speed
    zero, one = jnp.zeros_like(speed), jnp.ones_like(speed)
    columns = [
        three_sections([one if i == j else zero for i in range(MODES)], lambda u: local_rhs(u, speed, speed2), STEPS * STEP)
        for j in range(MODES)
    ]
    return [[columns[j][i] for j in range(MODES)] for i in range(MODES)]


def term_rows(step, half, k):
    return pl.ds((step * QUAD * CHUNK + half * ROWS) * MODES + k, ROWS, stride=MODES)


def carry_rows(half, k):
    return pl.ds((k * HALVES + half) * ROWS, ROWS)


def quad_kernel(term_ref, speed_ref, carry_ref):
    quad, chunk = place()
    matrix = coarse_matrix(speed_ref, chunk)
    row = lax.broadcasted_iota(jnp.int32, (ROWS, LANES), 0)
    for half in range(HALVES):
        terms = [[term_ref[term_rows(step, half, k), :] for k in range(MODES)] for step in range(QUAD)]
        total = terms[0]
        for step in range(1, QUAD):
            total = added(times(matrix, total), terms[step])
        if half == HALVES - 1:
            total = chosen(jnp.logical_and(quad == QUAD - 1, row >= CHUNK), terms[-1], total)
        for k in range(MODES):
            carry_ref[carry_rows(half, k), :] = total[k]


def read_carry(ref, half):
    return [ref[carry_rows(half, k), :] for k in range(MODES)]


def joined(over_quad, quad, own, partner, half, row):
    odd = quad % 2 == 1
    earlier, later = chosen(odd, partner, own), chosen(odd, own, partner)
    both = added(times(over_quad, earlier), later)
    if half < HALVES - 1:
        return both
    return chosen(jnp.logical_and(quad >= 2, row >= CHUNK), later, both)


def pair_kernel(carry_ref, partner_ref, speed_ref, out_ref):
    quad, chunk = place()
    over_quad = square(square(coarse_matrix(speed_ref, chunk)))
    row = lax.broadcasted_iota(jnp.int32, (ROWS, LANES), 0)
    for half in range(HALVES):
        both = joined(over_quad, quad, read_carry(carry_ref, half), read_carry(partner_ref, half), half, row)
        for k in range(MODES):
            out_ref[carry_rows(half, k), :] = both[k]


def slab_kernel(term_ref, carry_ref, partner_ref, far_ref, speed_ref, out_ref):
    quad, chunk = place()
    matrix = coarse_matrix(speed_ref, chunk)
    over_quad = square(square(matrix))
    over_pair = square(over_quad)
    over_y = square(over_pair)
    row = lax.broadcasted_iota(jnp.int32, (ROWS, LANES), 0)
    low = row < CHUNK
    high_pair, odd = quad >= 2, quad % 2 == 1

    def swapped(xs):
        return [pltpu.roll(x, CHUNK, 0) for x in xs]

    here, total = [], []
    for half in range(HALVES):
        own, partner, far = (read_carry(ref, half) for ref in (carry_ref, partner_ref, far_ref))
        both = joined(over_quad, quad, own, partner, half, row)
        before_pair = [jnp.where(high_pair, x, 0.0) for x in far]
        here.append(chosen(odd, added(times(over_quad, before_pair), partner), before_pair))
        first_pair, second_pair = chosen(high_pair, far, both), chosen(high_pair, both, far)
        total.append(added(times(over_pair, first_pair), second_pair))
    first = swapped(second_pair)
    second = swapped(added(times(over_y, first), total[0]))
    pair = chosen(low, first, second)
    third = swapped(added(times(over_y, pair), total[0]))
    fourth = swapped(added(times(over_y, third), total[1]))
    starts = [pair, chosen(low, third, fourth)]
    for half in range(HALVES):
        state = starts[half]
        state = chosen(high_pair, times(over_pair, state), state)
        state = chosen(odd, times(over_quad, state), state)
        state = added(state, here[half])
        for step in range(QUAD):
            for k in range(MODES):
                out_ref[term_rows(step, half, k), :] = state[k]
            if step < QUAD - 1:
                terms = [term_ref[term_rows(step, half, k), :] for k in range(MODES)]
                state = added(times(matrix, state), terms)


def on_device(kernel, name, rows, *operands):
    return pl.pallas_call(
        kernel,
        out_shape=jax.ShapeDtypeStruct((rows, LANES), jnp.float32),
        in_specs=[pl.BlockSpec(memory_space=pltpu.VMEM)] * len(operands),
        out_specs=pl.BlockSpec(memory_space=pltpu.VMEM),
        compiler_params=pltpu.CompilerParams(vmem_limit_bytes=16 * 1024 * 1024),
        name=name,
    )(*operands)


def swap_blocks(x, groups):
    return lax.all_to_all(x.reshape(-1, MODES, LANES), "tm", 0, 0, axis_index_groups=groups, tiled=True).reshape(x.shape)


def body(initial, guess, speeds, flags):
    slabs, blocks = lax.axis_size("tm"), lax.axis_size("space")
    count = initial.shape[1]
    rows = count // LANES

    def by_row(x):
        return x.reshape(MODES, rows, LANES).transpose(1, 0, 2).reshape(rows * MODES, LANES)

    speed_rows, flag_rows = speeds.reshape(rows, LANES), flags.reshape(rows, LANES)
    near, far = strip_part(by_row(guess[0]), by_row(initial), speed_rows, flag_rows, slabs)
    ours, _ = lax.optimization_barrier((guess[0], near))
    far = lax.ppermute(far, "space", [p for i in range(1, blocks - 1, 2) for p in ((i, i + 1), (i + 1, i))])
    near = lax.ppermute(near, "space", [p for i in range(0, blocks, 2) for p in ((i, i + 1), (i + 1, i))])
    state = by_row(jnp.where(lax.axis_index("tm") == slabs - 1, initial, ours))
    terms = fine_part(state, speed_rows, flag_rows, near, far, slabs)
    quads, ys = range(QUAD), range(slabs // QUAD**2)
    of_quad = [[y * QUAD**2 + q * QUAD + step for step in range(QUAD) for y in ys] for q in quads]
    terms = swap_blocks(terms, of_quad)
    size = MODES * HALVES * ROWS
    carry = on_device(quad_kernel, "quad_carry", size, terms, speed_rows)
    partner = lax.ppermute(carry, "tm", [(c, c ^ QUAD) for c in range(slabs)])
    joint = on_device(pair_kernel, "pair_carry", size, carry, partner, speed_rows)
    far = lax.ppermute(joint, "tm", [(c, c ^ (3 * QUAD)) for c in range(slabs)])
    sums = on_device(slab_kernel, "slab_sums", rows * MODES, terms, carry, partner, far, speed_rows)
    sums = swap_blocks(sums, of_quad)
    sums = sums.reshape(rows, MODES, LANES)
    return sums.transpose(1, 0, 2).reshape(1, MODES, count)


def solution(mesh):
    return jax.shard_map(
        body,
        mesh=mesh,
        in_specs=(P(None, "space"), P("tm", None, "space"), P("space"), P("space")),
        out_specs=P("tm", None, "space"),
        check_vma=False,
    )
```

```python
import functools

import jax
import jax.numpy as jnp
from jax import lax
from jax.experimental import pallas as pl
from jax.experimental.pallas import tpu as pltpu
from jax.sharding import PartitionSpec as P

MODES = 4
STEPS = 8
LANES = 128
ROWS = 8
VISCOSITY = 0.02
PENALTY = 10.0
STEP = 0.015625
JACOBIAN = 8.0
INV_MASS = (0.5, 1.5, 2.5, 3.5)


def column_scales(delta):
    return [JACOBIAN * m * delta for m in INV_MASS]


def shifted(xs, step):
    n = len(xs)
    rolled = [pltpu.roll(x, step % LANES, 1) for x in xs]
    lane = lax.broadcasted_iota(jnp.int32, xs[0].shape, 1)
    edge = lane == (0 if step == 1 else LANES - 1)
    out = []
    for v in range(n):
        at = v - step
        row = rolled[at] if 0 <= at < n else pltpu.roll(rolled[at % n], step % ROWS, 0)
        out.append(jnp.where(edge, row, rolled[v]))
    return out


def volume_terms(u, speed2, drain, p, q):
    a, b, c, d = u
    vq = (2.0 * VISCOSITY) * q
    m1 = speed2 * a - vq
    m2 = speed2 * b - (6.0 * VISCOSITY) * c
    m3 = speed2 * p - vq - (10.0 * VISCOSITY) * d
    return m1, m2, m3


def local_rhs(u, speed, speed2):
    a, b, c, d = u
    p, q = a + c, b + d
    out = -(speed * (p + q))
    m1, m2, m3 = volume_terms(u, speed2, out, p, q)
    return out, out + m1, out + m2, out + m3


def traces(u):
    a, b, c, d = u
    p, q = a + c, b + d
    odd, even = b + 6.0 * d, 3.0 * c
    return p + q, p - q, odd + even, odd - even


def full_step(start, now, scale, speed, speed2, inflow, gate, gate_after):
    tr, tl, sr, sl = zip(*(traces(u) for u in now))
    tr_b, sr_b, tl_a, sl_a = shifted(tr, 1), shifted(sr, 1), shifted(tl, -1), shifted(sl, -1)
    result = []
    for v, u in enumerate(now):
        jump = tr_b[v] - tl[v]
        k_l = gate[v] * jump
        g_l = inflow[v] * tr_b[v] - gate[v] * (sr_b[v] + sl[v] - (2.0 * PENALTY) * jump)
        jump = tr[v] - tl_a[v]
        k_r = gate_after[v] * jump
        base = gate_after[v] * (sr[v] + sl_a[v] - (2.0 * PENALTY) * jump) - speed[v] * tr[v]
        plus, minus = base + g_l, base - g_l
        k_sum, k_dif = k_r + k_l, k_r - k_l
        m1, m2, m3 = volume_terms(u, speed2[v], None, u[0] + u[2], u[1] + u[3])
        rhs = plus, minus + k_sum + m1, plus + 3.0 * k_dif + m2, minus + 6.0 * k_sum + m3
        result.append([x + f * r for x, f, r in zip(start[v], scale, rhs)])
    return result


def three_sections(u, rhs, delta):
    v = u
    for share in (3.0, 2.0, 1.0):
        scale = column_scales(delta / share)
        v = [x + f * r for x, f, r in zip(u, scale, rhs(v))]
    return v


def strip_kernel(slabs, guess_ref, initial_ref, speed_ref, flag_ref, near_ref, far_ref, states, speeds, flags, sems):
    rows = speed_ref.shape[0]
    last = lax.axis_index("tm") == slabs - 1
    ends = (0, 1)

    def tile(ref, end):
        return ref.at[pl.ds(end * (ref.shape[0] - ROWS), ROWS)]

    def copies(source):
        return [pltpu.make_async_copy(tile(source, e), states.at[e], sems.at[e]) for e in ends]

    others = [pltpu.make_async_copy(tile(speed_ref, e), speeds.at[e], sems.at[2 + e]) for e in ends]
    others += [pltpu.make_async_copy(tile(flag_ref, e), flags.at[e], sems.at[4 + e]) for e in ends]

    @pl.when(last)
    def _():
        for copy in copies(initial_ref):
            copy.start()

    @pl.when(jnp.logical_not(last))
    def _():
        for copy in copies(guess_ref):
            copy.start()

    for copy in others:
        copy.start()
    for copy in others + copies(guess_ref):
        copy.wait()
    strips = []
    for end in ends:
        row = end * (ROWS - 1)
        state = states[end, pl.ds(end * (ROWS - MODES), MODES), :]
        opened = 1.0 - flags[end, pl.ds(row, 1), :].astype(jnp.float32)
        unused = jnp.zeros((2, LANES), jnp.float32)
        strips.append(jnp.concatenate([state, speeds[end, pl.ds(row, 1), :], opened, unused], 0))
    head, tail = strips
    even = lax.axis_index("space") % 2 == 0
    near_ref[...] = jnp.where(even, tail, head)
    far_ref[...] = jnp.where(even, head, tail)


def strip_part(guess, initial, speeds, flags, slabs):
    strip = jax.ShapeDtypeStruct((ROWS, LANES), jnp.float32)
    return pl.pallas_call(
        functools.partial(strip_kernel, slabs),
        out_shape=[strip, strip],
        in_specs=[pl.BlockSpec(memory_space=pltpu.HBM)] * 4,
        out_specs=[pl.BlockSpec(memory_space=pltpu.VMEM)] * 2,
        scratch_shapes=[
            pltpu.VMEM((2, ROWS, LANES), jnp.float32),
            pltpu.VMEM((2, ROWS, LANES), jnp.float32),
            pltpu.VMEM((2, ROWS, LANES), jnp.int32),
            pltpu.SemaphoreType.DMA((6,)),
        ],
        compiler_params=pltpu.CompilerParams(vmem_limit_bytes=16 * 1024 * 1024),
        name="end_strips",
    )(*(pltpu.with_memory_space_constraint(x, pltpu.HBM) for x in (guess, initial, speeds, flags)))


def fine_kernel(slabs, state_ref, speed_ref, flag_ref, near_ref, far_ref, out_ref, field, coef):
    rows = speed_ref.shape[0]
    wide = rows + ROWS
    n = wide // ROWS
    last = lax.axis_index("tm") == slabs - 1
    block = lax.axis_index("space")
    even = block % 2 == 0
    near, far = near_ref[...], far_ref[...]
    left, right = jnp.where(even, far, near), jnp.where(even, near, far)

    unused = ROWS - 2
    field[pl.ds(0, rows * MODES), :] = state_ref[...]
    field[pl.ds(rows * MODES, MODES), :] = right[:MODES]
    field[pl.ds((rows + 1) * MODES, unused * MODES), :] = jnp.zeros((unused * MODES, LANES), jnp.float32)
    field[pl.ds((wide - 1) * MODES, MODES), :] = left[:MODES]
    for part, own in ((0, speed_ref[...]), (1, 1.0 - flag_ref[...].astype(jnp.float32))):
        coef[pl.ds(part * wide, rows), :] = own
        coef[pl.ds(part * wide + rows, 1), :] = right[MODES + part : MODES + part + 1]
        coef[pl.ds(part * wide + rows + 1, unused), :] = jnp.zeros((unused, LANES), jnp.float32)
        coef[pl.ds(part * wide + wide - 1, 1), :] = left[MODES + part : MODES + part + 1]

    start = [[field[pl.ds(MODES * v + k, ROWS, stride=MODES * n), :] for k in range(MODES)] for v in range(n)]
    speed = [coef[pl.ds(v, ROWS, stride=n), :] for v in range(n)]
    opened = [coef[pl.ds(wide + v, ROWS, stride=n), :] for v in range(n)]
    row = lax.broadcasted_iota(jnp.int32, (ROWS, LANES), 0)
    lane = lax.broadcasted_iota(jnp.int32, (ROWS, LANES), 1)
    first = jnp.logical_and(jnp.logical_and(row == 0, lane == 0), block == 0)
    opened[0] = jnp.where(first, 0.0, opened[0])
    gate = [(0.5 * VISCOSITY) * x for x in opened]
    gate_after = shifted(gate, -1)
    inflow = [x * y for x, y in zip(opened, shifted(speed, 1))]
    speed2 = [2.0 * x for x in speed]

    def advance(_, u):
        now = u
        for share in (3.0, 2.0, 1.0):
            now = full_step(u, now, column_scales(STEP / share), speed, speed2, inflow, gate, gate_after)
        return now

    final = lax.fori_loop(0, STEPS, advance, start, unroll=True)
    for v in range(n):
        coarse = three_sections(start[v], lambda u: local_rhs(u, speed[v], speed2[v]), STEPS * STEP)
        for k in range(MODES):
            field[pl.ds(MODES * v + k, ROWS, stride=MODES * n), :] = final[v][k] - jnp.where(last, 0.0, coarse[k])
    out_ref[...] = field[pl.ds(0, rows * MODES), :]


def fine_part(state, speeds, flags, near, far, slabs):
    return pl.pallas_call(
        functools.partial(fine_kernel, slabs),
        out_shape=jax.ShapeDtypeStruct(state.shape, jnp.float32),
        in_specs=[pl.BlockSpec(memory_space=pltpu.VMEM)] * 5,
        out_specs=pl.BlockSpec(memory_space=pltpu.VMEM),
        scratch_shapes=[
            pltpu.VMEM(((speeds.shape[0] + ROWS) * MODES, LANES), jnp.float32),
            pltpu.VMEM(((speeds.shape[0] + ROWS) * 2, LANES), jnp.float32),
        ],
        compiler_params=pltpu.CompilerParams(vmem_limit_bytes=16 * 1024 * 1024),
        cost_estimate=pl.CostEstimate(flops=24 * 60 * 8192, bytes_accessed=2 * state.size * 4, transcendentals=0),
        name="fine_steps",
    )(state, speeds, flags, near, far)


def times(matrix, field):
    out = []
    for row in matrix:
        total = row[0] * field[0]
        for entry, value in zip(row[1:], field[1:]):
            total = total + entry * value
        out.append(total)
    return out


def square(matrix):
    columns = [times(matrix, [matrix[i][j] for i in range(MODES)]) for j in range(MODES)]
    return [[columns[j][i] for j in range(MODES)] for i in range(MODES)]


def added(xs, ys):
    return [x + y for x, y in zip(xs, ys)]


def chosen(test, xs, ys):
    return [jnp.where(test, x, y) for x, y in zip(xs, ys)]


QUAD = 4
CHUNK = 4
HALVES = 2


def place():
    slab = lax.axis_index("tm")
    y, z = slab // (QUAD * QUAD), slab % (QUAD * QUAD)
    return z // QUAD, (z % QUAD) * QUAD + y


def coarse_matrix(speed_ref, chunk):
    rows = [speed_ref[pl.ds(chunk * CHUNK + r, 1), :] for r in range(CHUNK)]
    speed = jnp.concatenate(rows * (ROWS // CHUNK), 0)
    speed2 = 2.0 * speed
    zero, one = jnp.zeros_like(speed), jnp.ones_like(speed)
    columns = [
        three_sections([one if i == j else zero for i in range(MODES)], lambda u: local_rhs(u, speed, speed2), STEPS * STEP)
        for j in range(MODES)
    ]
    return [[columns[j][i] for j in range(MODES)] for i in range(MODES)]


def term_rows(step, half, k):
    return pl.ds((step * QUAD * CHUNK + half * ROWS) * MODES + k, ROWS, stride=MODES)


def carry_rows(half, k):
    return pl.ds((k * HALVES + half) * ROWS, ROWS)


def quad_kernel(term_ref, speed_ref, carry_ref):
    quad, chunk = place()
    matrix = coarse_matrix(speed_ref, chunk)
    row = lax.broadcasted_iota(jnp.int32, (ROWS, LANES), 0)
    for half in range(HALVES):
        terms = [[term_ref[term_rows(step, half, k), :] for k in range(MODES)] for step in range(QUAD)]
        total = terms[0]
        for step in range(1, QUAD):
            total = added(times(matrix, total), terms[step])
        if half == HALVES - 1:
            total = chosen(jnp.logical_and(quad == QUAD - 1, row >= CHUNK), terms[-1], total)
        for k in range(MODES):
            carry_ref[carry_rows(half, k), :] = total[k]


def read_carry(ref, half):
    return [ref[carry_rows(half, k), :] for k in range(MODES)]


def joined(over_quad, quad, own, partner, half, row):
    odd = quad % 2 == 1
    earlier, later = chosen(odd, partner, own), chosen(odd, own, partner)
    both = added(times(over_quad, earlier), later)
    if half < HALVES - 1:
        return both
    return chosen(jnp.logical_and(quad >= 2, row >= CHUNK), later, both)


def pair_kernel(carry_ref, partner_ref, speed_ref, out_ref):
    quad, chunk = place()
    over_quad = square(square(coarse_matrix(speed_ref, chunk)))
    row = lax.broadcasted_iota(jnp.int32, (ROWS, LANES), 0)
    for half in range(HALVES):
        both = joined(over_quad, quad, read_carry(carry_ref, half), read_carry(partner_ref, half), half, row)
        for k in range(MODES):
            out_ref[carry_rows(half, k), :] = both[k]


def slab_kernel(term_ref, carry_ref, partner_ref, far_ref, speed_ref, out_ref):
    quad, chunk = place()
    matrix = coarse_matrix(speed_ref, chunk)
    over_quad = square(square(matrix))
    over_pair = square(over_quad)
    over_y = square(over_pair)
    row = lax.broadcasted_iota(jnp.int32, (ROWS, LANES), 0)
    low = row < CHUNK
    high_pair, odd = quad >= 2, quad % 2 == 1

    def swapped(xs):
        return [pltpu.roll(x, CHUNK, 0) for x in xs]

    here, total = [], []
    for half in range(HALVES):
        own, partner, far = (read_carry(ref, half) for ref in (carry_ref, partner_ref, far_ref))
        both = joined(over_quad, quad, own, partner, half, row)
        before_pair = [jnp.where(high_pair, x, 0.0) for x in far]
        here.append(chosen(odd, added(times(over_quad, before_pair), partner), before_pair))
        first_pair, second_pair = chosen(high_pair, far, both), chosen(high_pair, both, far)
        total.append(added(times(over_pair, first_pair), second_pair))
    first = swapped(second_pair)
    second = swapped(added(times(over_y, first), total[0]))
    pair = chosen(low, first, second)
    third = swapped(added(times(over_y, pair), total[0]))
    fourth = swapped(added(times(over_y, third), total[1]))
    starts = [pair, chosen(low, third, fourth)]
    for half in range(HALVES):
        state = starts[half]
        state = chosen(high_pair, times(over_pair, state), state)
        state = chosen(odd, times(over_quad, state), state)
        state = added(state, here[half])
        for step in range(QUAD):
            for k in range(MODES):
                out_ref[term_rows(step, half, k), :] = state[k]
            if step < QUAD - 1:
                terms = [term_ref[term_rows(step, half, k), :] for k in range(MODES)]
                state = added(times(matrix, state), terms)


def on_device(kernel, name, rows, *operands):
    return pl.pallas_call(
        kernel,
        out_shape=jax.ShapeDtypeStruct((rows, LANES), jnp.float32),
        in_specs=[pl.BlockSpec(memory_space=pltpu.VMEM)] * len(operands),
        out_specs=pl.BlockSpec(memory_space=pltpu.VMEM),
        compiler_params=pltpu.CompilerParams(vmem_limit_bytes=16 * 1024 * 1024),
        name=name,
    )(*operands)


def swap_blocks(x, groups):
    return lax.all_to_all(x.reshape(-1, MODES, LANES), "tm", 0, 0, axis_index_groups=groups, tiled=True).reshape(x.shape)


def body(initial, guess, speeds, flags):
    slabs, blocks = lax.axis_size("tm"), lax.axis_size("space")
    count = initial.shape[1]
    rows = count // LANES

    def by_row(x):
        return x.reshape(MODES, rows, LANES).transpose(1, 0, 2).reshape(rows * MODES, LANES)

    speed_rows, flag_rows = speeds.reshape(rows, LANES), flags.reshape(rows, LANES)
    near, far = strip_part(by_row(guess[0]), by_row(initial), speed_rows, flag_rows, slabs)
    ours, _ = lax.optimization_barrier((guess[0], near))
    far = lax.ppermute(far, "space", [p for i in range(1, blocks - 1, 2) for p in ((i, i + 1), (i + 1, i))])
    near = lax.ppermute(near, "space", [p for i in range(0, blocks, 2) for p in ((i, i + 1), (i + 1, i))])
    state = by_row(jnp.where(lax.axis_index("tm") == slabs - 1, initial, ours))
    terms = fine_part(state, speed_rows, flag_rows, near, far, slabs)
    quads, ys = range(QUAD), range(slabs // QUAD**2)
    of_quad = [[y * QUAD**2 + q * QUAD + step for step in range(QUAD) for y in ys] for q in quads]
    terms = swap_blocks(terms, of_quad)
    size = MODES * HALVES * ROWS
    carry = on_device(quad_kernel, "quad_carry", size, terms, speed_rows)
    partner = lax.ppermute(carry, "tm", [(c, c ^ QUAD) for c in range(slabs)])
    joint = on_device(pair_kernel, "pair_carry", size, carry, partner, speed_rows)
    far = lax.ppermute(joint, "tm", [(c, c ^ (3 * QUAD)) for c in range(slabs)])
    sums = on_device(slab_kernel, "slab_sums", rows * MODES, terms, carry, partner, far, speed_rows)
    sums = swap_blocks(sums, of_quad)
    sums = sums.reshape(rows, MODES, LANES)
    return sums.transpose(1, 0, 2).reshape(1, MODES, count)


def solution(mesh):
    return jax.shard_map(
        body,
        mesh=mesh,
        in_specs=(P(None, "space"), P("tm", None, "space"), P("space"), P("space")),
        out_specs=P("tm", None, "space"),
        check_vma=False,
    )
```

```python
import functools

import jax
import jax.numpy as jnp
from jax import lax
from jax.experimental import pallas as pl
from jax.experimental.pallas import tpu as pltpu
from jax.sharding import PartitionSpec as P

MODES = 4
STEPS = 8
LANES = 128
ROWS = 8
VISCOSITY = 0.02
PENALTY = 10.0
STEP = 0.015625
JACOBIAN = 8.0
INV_MASS = (0.5, 1.5, 2.5, 3.5)


def column_scales(delta):
    return [JACOBIAN * m * delta for m in INV_MASS]


def shifted(xs, step):
    rolled = [pltpu.roll(x, step % LANES, 1) for x in xs]
    lane = lax.broadcasted_iota(jnp.int32, xs[0].shape, 1)
    edge = lane == (0 if step == 1 else LANES - 1)
    return [jnp.where(edge, rolled[(v - step) % len(xs)], x) for v, x in enumerate(rolled)]


def volume_terms(u, speed2, p, q):
    a, b, c, d = u
    vq = (2.0 * VISCOSITY) * q
    m1 = speed2 * a - vq
    m2 = speed2 * b - (6.0 * VISCOSITY) * c
    m3 = speed2 * p - vq - (10.0 * VISCOSITY) * d
    return m1, m2, m3


def local_rhs(u, speed, speed2):
    a, b, c, d = u
    p, q = a + c, b + d
    out = -(speed * (p + q))
    m1, m2, m3 = volume_terms(u, speed2, p, q)
    return out, out + m1, out + m2, out + m3


def traces(u):
    a, b, c, d = u
    p, q = a + c, b + d
    odd, even = b + 6.0 * d, 3.0 * c
    return p + q, p - q, odd + even, odd - even


def full_step(start, now, scale, speed, speed2, inflow, gate, gate_after):
    tr, tl, sr, sl = zip(*(traces(u) for u in now))
    tr_b, sr_b, tl_a, sl_a = shifted(tr, 1), shifted(sr, 1), shifted(tl, -1), shifted(sl, -1)
    result = []
    for v, u in enumerate(now):
        jump = tr_b[v] - tl[v]
        k_l = gate[v] * jump
        g_l = inflow[v] * tr_b[v] - gate[v] * (sr_b[v] + sl[v] - (2.0 * PENALTY) * jump)
        jump = tr[v] - tl_a[v]
        k_r = gate_after[v] * jump
        base = gate_after[v] * (sr[v] + sl_a[v] - (2.0 * PENALTY) * jump) - speed[v] * tr[v]
        plus, minus = base + g_l, base - g_l
        k_sum, k_dif = k_r + k_l, k_r - k_l
        m1, m2, m3 = volume_terms(u, speed2[v], u[0] + u[2], u[1] + u[3])
        rhs = plus, minus + k_sum + m1, plus + 3.0 * k_dif + m2, minus + 6.0 * k_sum + m3
        result.append([x + f * r for x, f, r in zip(start[v], scale, rhs)])
    return result


def three_sections(u, rhs, delta):
    v = u
    for share in (3.0, 2.0, 1.0):
        scale = column_scales(delta / share)
        v = [x + f * r for x, f, r in zip(u, scale, rhs(v))]
    return v


QUAD = 4
CHUNK = 4
HALVES = 2
CHUNKS = 16
WINDOW = (CHUNK + 1) * MODES
ORDER = (4, 1, 2, 3, 0, 5, 6, 7, 15, 9, 10, 11, 12, 13, 14, 8)
BACKWARDS = tuple(CHUNKS - 1 - chunk for chunk in ORDER)


def even_block():
    return lax.axis_index("space") % 2 == 0


def place():
    slab = lax.axis_index("tm")
    y, z = slab // (QUAD * QUAD), slab % (QUAD * QUAD)
    position = (z % QUAD) * QUAD + y
    chunk = position
    for i, there in enumerate(ORDER):
        if i != there:
            chunk = jnp.where(position == i, there, chunk)
    return z // QUAD, jnp.where(even_block(), chunk, CHUNKS - 1 - chunk)


def window_kernel(slabs, guess_ref, initial_ref, out_ref, state, sem):
    last = lax.axis_index("tm") == slabs - 1

    @pl.when(last)
    def _():
        pltpu.make_async_copy(initial_ref, state, sem).start()

    @pl.when(jnp.logical_not(last))
    def _():
        pltpu.make_async_copy(guess_ref, state, sem).start()

    pltpu.make_async_copy(guess_ref, state, sem).wait()
    low = lax.broadcasted_iota(jnp.int32, (MODES, LANES), 1) < LANES // 2
    size = CHUNK * MODES

    def write(chunks):
        for position, chunk in enumerate(chunks):
            at, source = position * WINDOW, chunk * size
            out_ref[pl.ds(at, size), :] = state[pl.ds(source, size), :]
            after = state[pl.ds(min(source + size, (CHUNKS - 1) * size), MODES), :]
            before = state[pl.ds(max(source - MODES, 0), MODES), :]
            out_ref[pl.ds(at + size, MODES), :] = jnp.where(low, after, before)

    @pl.when(even_block())
    def _():
        write(ORDER)

    @pl.when(jnp.logical_not(even_block()))
    def _():
        write(BACKWARDS)


def window_part(guess, initial, slabs):
    return pl.pallas_call(
        functools.partial(window_kernel, slabs),
        out_shape=jax.ShapeDtypeStruct((CHUNKS * WINDOW, LANES), jnp.float32),
        in_specs=[pl.BlockSpec(memory_space=pltpu.HBM)] * 2,
        out_specs=pl.BlockSpec(memory_space=pltpu.VMEM),
        scratch_shapes=[pltpu.VMEM(guess.shape, jnp.float32), pltpu.SemaphoreType.DMA],
        compiler_params=pltpu.CompilerParams(vmem_limit_bytes=16 * 1024 * 1024),
        name="windows",
    )(*(pltpu.with_memory_space_constraint(x, pltpu.HBM) for x in (guess, initial)))


def window_rows(half, r, k):
    return pl.ds((half * ROWS * (CHUNK + 1) + r) * MODES + k, ROWS, stride=WINDOW)


def message_rows(half, k):
    return pl.ds((k * HALVES + half) * ROWS, ROWS)


COEFS = MODES * HALVES * ROWS


def edge_kernel(window_ref, speed_ref, flag_ref, out_ref):
    _, chunk = place()
    tail = chunk == CHUNKS - 1
    rows = speed_ref.shape[0]
    for half in range(HALVES):
        for k in range(MODES):
            first, final = window_ref[window_rows(half, 0, k), :], window_ref[window_rows(half, CHUNK - 1, k), :]
            out_ref[message_rows(half, k), :] = jnp.where(tail, final, first)
    at = jnp.where(tail, rows - 1, 0)
    out_ref[pl.ds(COEFS, 1), :] = speed_ref[pl.ds(at, 1), :]
    out_ref[pl.ds(COEFS + 1, 1), :] = 1.0 - flag_ref[pl.ds(at, 1), :].astype(jnp.float32)
    out_ref[pl.ds(COEFS + 2, ROWS - 2), :] = jnp.zeros((ROWS - 2, LANES), jnp.float32)


def fine_kernel(window_ref, message_ref, speed_ref, flag_ref, out_ref):
    quad, chunk = place()
    first, final = chunk == 0, chunk == CHUNKS - 1
    shape = (ROWS, LANES)
    row = lax.broadcasted_iota(jnp.int32, shape, 0)
    lane = lax.broadcasted_iota(jnp.int32, shape, 1)
    low = lane < LANES // 2
    outside = jnp.logical_or(jnp.logical_and(low, final), jnp.logical_and(lane >= LANES // 2, first))

    def coef(read, k):
        def spread(x):
            return jnp.broadcast_to(x, shape)

        at = chunk * CHUNK
        own = [spread(read(at + r)) for r in range(CHUNK)]
        after = spread(read(jnp.minimum(at + CHUNK, CHUNKS * CHUNK - 1)))
        before = spread(read(jnp.maximum(at - 1, 0)))
        beyond = spread(message_ref[pl.ds(COEFS + k, 1), :])
        return [*own, jnp.where(outside, beyond, jnp.where(low, after, before))]

    speed = coef(lambda i: speed_ref[pl.ds(i, 1), :], 0)
    opened = coef(lambda i: 1.0 - flag_ref[pl.ds(i, 1), :].astype(jnp.float32), 1)
    wall = jnp.logical_and(jnp.logical_and(first, lax.axis_index("space") == 0), lane == 0)
    opened[0] = jnp.where(wall, 0.0, opened[0])
    gate = [(0.5 * VISCOSITY) * x for x in opened]
    gate_after = shifted(gate, -1)
    inflow = [x * y for x, y in zip(opened, shifted(speed, 1))]
    speed2 = [2.0 * x for x in speed]

    starts = []
    for half in range(HALVES):
        start = [[window_ref[window_rows(half, r, k), :] for k in range(MODES)] for r in range(CHUNK + 1)]
        start[CHUNK] = [
            jnp.where(outside, message_ref[message_rows(half, k), :], x) for k, x in enumerate(start[CHUNK])
        ]
        starts.append(start)

    def advance(_, us):
        nows = us
        for share in (3.0, 2.0, 1.0):
            scale = column_scales(STEP / share)
            nows = [full_step(u, now, scale, speed, speed2, inflow, gate, gate_after) for u, now in zip(us, nows)]
        return nows

    finals = lax.fori_loop(0, STEPS, advance, starts, unroll=True)
    for half in range(HALVES):
        for r in range(CHUNK):
            coarse = three_sections(starts[half][r], lambda u: local_rhs(u, speed[r], speed2[r]), STEPS * STEP)
            if half == HALVES - 1:
                last = jnp.logical_and(quad == QUAD - 1, row == ROWS - 1)
                coarse = [jnp.where(last, 0.0, x) for x in coarse]
            for k in range(MODES):
                rows = pl.ds((half * ROWS * CHUNK + r) * MODES + k, ROWS, stride=CHUNK * MODES)
                out_ref[rows, :] = finals[half][r][k] - coarse[k]


def write_kernel(sums_ref, out_ref, sems):
    size = CHUNK * MODES

    def write(chunks):
        copies = []
        for position, chunk in enumerate(chunks):
            source, target = pl.ds(position * size, size), pl.ds(chunk * size, size)
            copies.append(pltpu.make_async_copy(sums_ref.at[source], out_ref.at[target], sems.at[position]))
        for copy in copies:
            copy.start()
        for copy in copies:
            copy.wait()

    @pl.when(even_block())
    def _():
        write(ORDER)

    @pl.when(jnp.logical_not(even_block()))
    def _():
        write(BACKWARDS)


def write_part(sums):
    return pl.pallas_call(
        write_kernel,
        out_shape=jax.ShapeDtypeStruct(sums.shape, jnp.float32),
        in_specs=[pl.BlockSpec(memory_space=pltpu.VMEM)],
        out_specs=pl.BlockSpec(memory_space=pl.ANY),
        scratch_shapes=[pltpu.SemaphoreType.DMA((CHUNKS,))],
        compiler_params=pltpu.CompilerParams(vmem_limit_bytes=16 * 1024 * 1024),
        name="write_out",
    )(sums)


def times(matrix, field):
    out = []
    for row in matrix:
        total = row[0] * field[0]
        for entry, value in zip(row[1:], field[1:]):
            total = total + entry * value
        out.append(total)
    return out


def square(matrix):
    columns = [times(matrix, [matrix[i][j] for i in range(MODES)]) for j in range(MODES)]
    return [[columns[j][i] for j in range(MODES)] for i in range(MODES)]


def added(xs, ys):
    return [x + y for x, y in zip(xs, ys)]


def chosen(test, xs, ys):
    return [jnp.where(test, x, y) for x, y in zip(xs, ys)]


def coarse_matrix(speed_ref, chunk):
    rows = [speed_ref[pl.ds(chunk * CHUNK + r, 1), :] for r in range(CHUNK)]
    speed = jnp.concatenate(rows * (ROWS // CHUNK), 0)
    speed2 = 2.0 * speed
    zero, one = jnp.zeros_like(speed), jnp.ones_like(speed)
    columns = [
        three_sections([one if i == j else zero for i in range(MODES)], lambda u: local_rhs(u, speed, speed2), STEPS * STEP)
        for j in range(MODES)
    ]
    return [[columns[j][i] for j in range(MODES)] for i in range(MODES)]


def term_rows(step, half, k):
    return pl.ds((step * QUAD * CHUNK + half * ROWS) * MODES + k, ROWS, stride=MODES)


def carry_rows(half, k):
    return pl.ds((k * HALVES + half) * ROWS, ROWS)


def quad_kernel(term_ref, speed_ref, carry_ref):
    quad, chunk = place()
    matrix = coarse_matrix(speed_ref, chunk)
    row = lax.broadcasted_iota(jnp.int32, (ROWS, LANES), 0)
    for half in range(HALVES):
        terms = [[term_ref[term_rows(step, half, k), :] for k in range(MODES)] for step in range(QUAD)]
        total = terms[0]
        for step in range(1, QUAD):
            total = added(times(matrix, total), terms[step])
        if half == HALVES - 1:
            total = chosen(jnp.logical_and(quad == QUAD - 1, row >= CHUNK), terms[-1], total)
        for k in range(MODES):
            carry_ref[carry_rows(half, k), :] = total[k]


def read_carry(ref, half):
    return [ref[carry_rows(half, k), :] for k in range(MODES)]


def joined(over_quad, quad, own, partner, half, row):
    odd = quad % 2 == 1
    earlier, later = chosen(odd, partner, own), chosen(odd, own, partner)
    both = added(times(over_quad, earlier), later)
    if half < HALVES - 1:
        return both
    return chosen(jnp.logical_and(quad >= 2, row >= CHUNK), later, both)


def pair_kernel(carry_ref, partner_ref, speed_ref, out_ref):
    quad, chunk = place()
    over_quad = square(square(coarse_matrix(speed_ref, chunk)))
    row = lax.broadcasted_iota(jnp.int32, (ROWS, LANES), 0)
    for half in range(HALVES):
        both = joined(over_quad, quad, read_carry(carry_ref, half), read_carry(partner_ref, half), half, row)
        for k in range(MODES):
            out_ref[carry_rows(half, k), :] = both[k]


def slab_kernel(term_ref, carry_ref, partner_ref, far_ref, speed_ref, out_ref):
    quad, chunk = place()
    matrix = coarse_matrix(speed_ref, chunk)
    over_quad = square(square(matrix))
    over_pair = square(over_quad)
    over_y = square(over_pair)
    row = lax.broadcasted_iota(jnp.int32, (ROWS, LANES), 0)
    low = row < CHUNK
    high_pair, odd = quad >= 2, quad % 2 == 1

    def swapped(xs):
        return [pltpu.roll(x, CHUNK, 0) for x in xs]

    here, total = [], []
    for half in range(HALVES):
        own, partner, far = (read_carry(ref, half) for ref in (carry_ref, partner_ref, far_ref))
        both = joined(over_quad, quad, own, partner, half, row)
        before_pair = [jnp.where(high_pair, x, 0.0) for x in far]
        here.append(chosen(odd, added(times(over_quad, before_pair), partner), before_pair))
        first_pair, second_pair = chosen(high_pair, far, both), chosen(high_pair, both, far)
        total.append(added(times(over_pair, first_pair), second_pair))
    first = swapped(second_pair)
    second = swapped(added(times(over_y, first), total[0]))
    pair = chosen(low, first, second)
    third = swapped(added(times(over_y, pair), total[0]))
    fourth = swapped(added(times(over_y, third), total[1]))
    starts = [pair, chosen(low, third, fourth)]
    for half in range(HALVES):
        state = starts[half]
        state = chosen(high_pair, times(over_pair, state), state)
        state = chosen(odd, times(over_quad, state), state)
        state = added(state, here[half])
        for step in range(QUAD):
            for k in range(MODES):
                out_ref[term_rows(step, half, k), :] = state[k]
            if step < QUAD - 1:
                terms = [term_ref[term_rows(step, half, k), :] for k in range(MODES)]
                state = added(times(matrix, state), terms)


def on_device(kernel, name, rows, *operands):
    return pl.pallas_call(
        kernel,
        out_shape=jax.ShapeDtypeStruct((rows, LANES), jnp.float32),
        in_specs=[pl.BlockSpec(memory_space=pltpu.VMEM)] * len(operands),
        out_specs=pl.BlockSpec(memory_space=pltpu.VMEM),
        compiler_params=pltpu.CompilerParams(vmem_limit_bytes=16 * 1024 * 1024),
        name=name,
    )(*operands)


def swap_blocks(x, groups):
    return lax.all_to_all(x.reshape(-1, MODES, LANES), "tm", 0, 0, axis_index_groups=groups, tiled=True).reshape(x.shape)


def body(initial, guess, speeds, flags):
    slabs, blocks = lax.axis_size("tm"), lax.axis_size("space")
    count = initial.shape[1]
    rows = count // LANES

    def by_row(x):
        return x.reshape(MODES, rows, LANES).transpose(1, 0, 2).reshape(rows * MODES, LANES)

    speed_rows, flag_rows = speeds.reshape(rows, LANES), flags.reshape(rows, LANES)
    quads, ys = range(QUAD), range(slabs // QUAD**2)
    of_quad = [[y * QUAD**2 + q * QUAD + step for step in range(QUAD) for y in ys] for q in quads]
    windows = swap_blocks(window_part(by_row(guess[0]), by_row(initial), slabs), of_quad)
    pairs = []
    for group in of_quad:
        for slab, start in ((group[ORDER.index(CHUNKS - 1)], 0), (group[ORDER.index(0)], 1)):
            for i in range(start, blocks - 1, 2):
                ends = slab * blocks + i, slab * blocks + i + 1
                pairs += [ends, ends[::-1]]
    edge = on_device(edge_kernel, "edge_rows", COEFS + ROWS, windows, speed_rows, flag_rows)
    message = lax.ppermute(edge, ("tm", "space"), pairs)
    terms = on_device(fine_kernel, "fine_steps", rows * MODES, windows, message, speed_rows, flag_rows)
    size = MODES * HALVES * ROWS
    carry = on_device(quad_kernel, "quad_carry", size, terms, speed_rows)
    partner = lax.ppermute(carry, "tm", [(c, c ^ QUAD) for c in range(slabs)])
    joint = on_device(pair_kernel, "pair_carry", size, carry, partner, speed_rows)
    far = lax.ppermute(joint, "tm", [(c, c ^ (3 * QUAD)) for c in range(slabs)])
    sums = on_device(slab_kernel, "slab_sums", rows * MODES, terms, carry, partner, far, speed_rows)
    sums = write_part(swap_blocks(sums, of_quad)).reshape(rows, MODES, LANES)
    return sums.transpose(1, 0, 2).reshape(1, MODES, count)


def solution(mesh):
    return jax.shard_map(
        body,
        mesh=mesh,
        in_specs=(P(None, "space"), P("tm", None, "space"), P("space"), P("space")),
        out_specs=P("tm", None, "space"),
        check_vma=False,
    )
```

```python
import functools

import jax
import jax.numpy as jnp
from jax import lax
from jax.experimental import pallas as pl
from jax.experimental.pallas import tpu as pltpu
from jax.sharding import PartitionSpec as P

MODES = 4
STEPS = 8
LANES = 128
ROWS = 8
VISCOSITY = 0.02
PENALTY = 10.0
STEP = 0.015625
JACOBIAN = 8.0
INV_MASS = (0.5, 1.5, 2.5, 3.5)


def column_scales(delta):
    return [JACOBIAN * m * delta for m in INV_MASS]


def shifted(xs, step):
    rolled = [pltpu.roll(x, step % LANES, 1) for x in xs]
    lane = lax.broadcasted_iota(jnp.int32, xs[0].shape, 1)
    edge = lane == (0 if step == 1 else LANES - 1)
    return [jnp.where(edge, rolled[(v - step) % len(xs)], x) for v, x in enumerate(rolled)]


def volume_terms(u, speed2, p, q):
    a, b, c, d = u
    vq = (2.0 * VISCOSITY) * q
    m1 = speed2 * a - vq
    m2 = speed2 * b - (6.0 * VISCOSITY) * c
    m3 = speed2 * p - vq - (10.0 * VISCOSITY) * d
    return m1, m2, m3


def local_rhs(u, speed, speed2):
    a, b, c, d = u
    p, q = a + c, b + d
    out = -(speed * (p + q))
    m1, m2, m3 = volume_terms(u, speed2, p, q)
    return out, out + m1, out + m2, out + m3


def traces(u):
    a, b, c, d = u
    p, q = a + c, b + d
    odd, even = b + 6.0 * d, 3.0 * c
    return p + q, p - q, odd + even, odd - even


def full_step(start, now, scale, speed, speed2, inflow, gate, gate_after):
    tr, tl, sr, sl = zip(*(traces(u) for u in now))
    tr_b, sr_b, tl_a, sl_a = shifted(tr, 1), shifted(sr, 1), shifted(tl, -1), shifted(sl, -1)
    result = []
    for v, u in enumerate(now):
        jump = tr_b[v] - tl[v]
        k_l = gate[v] * jump
        g_l = inflow[v] * tr_b[v] - gate[v] * (sr_b[v] + sl[v] - (2.0 * PENALTY) * jump)
        jump = tr[v] - tl_a[v]
        k_r = gate_after[v] * jump
        base = gate_after[v] * (sr[v] + sl_a[v] - (2.0 * PENALTY) * jump) - speed[v] * tr[v]
        plus, minus = base + g_l, base - g_l
        k_sum, k_dif = k_r + k_l, k_r - k_l
        m1, m2, m3 = volume_terms(u, speed2[v], u[0] + u[2], u[1] + u[3])
        rhs = plus, minus + k_sum + m1, plus + 3.0 * k_dif + m2, minus + 6.0 * k_sum + m3
        result.append([x + f * r for x, f, r in zip(start[v], scale, rhs)])
    return result


def three_sections(u, rhs, delta):
    v = u
    for share in (3.0, 2.0, 1.0):
        scale = column_scales(delta / share)
        v = [x + f * r for x, f, r in zip(u, scale, rhs(v))]
    return v


QUAD = 4
CHUNK = 4
HALVES = 2
CHUNKS = 16
WINDOW = (CHUNK + 1) * MODES
ORDER = (1, 2, 3, 4, 0, 15, 5, 6, 7, 8, 9, 10, 11, 12, 13, 14)
BACKWARDS = tuple(CHUNKS - 1 - chunk for chunk in ORDER)


def even_block():
    return lax.axis_index("space") % 2 == 0


def place():
    slab = lax.axis_index("tm")
    y, z = slab // (QUAD * QUAD), slab % (QUAD * QUAD)
    position = (z % QUAD) * QUAD + y
    chunk = position
    for i, there in enumerate(ORDER):
        if i != there:
            chunk = jnp.where(position == i, there, chunk)
    return z // QUAD, jnp.where(even_block(), chunk, CHUNKS - 1 - chunk)


COPIES = 4


def window_kernel(slabs, guess_ref, initial_ref, out_ref, state, sems):
    last = lax.axis_index("tm") == slabs - 1
    rows = state.shape[0] // COPIES

    def copies(source):
        parts = [pl.ds(i * rows, rows) for i in range(COPIES)]
        return [pltpu.make_async_copy(source.at[part], state.at[part], sems.at[i]) for i, part in enumerate(parts)]

    @pl.when(last)
    def _():
        for copy in copies(initial_ref):
            copy.start()

    @pl.when(jnp.logical_not(last))
    def _():
        for copy in copies(guess_ref):
            copy.start()

    for copy in copies(guess_ref):
        copy.wait()
    low = lax.broadcasted_iota(jnp.int32, (MODES, LANES), 1) < LANES // 2
    size = CHUNK * MODES

    def write(chunks):
        for position, chunk in enumerate(chunks):
            at, source = position * WINDOW, chunk * size
            out_ref[pl.ds(at, size), :] = state[pl.ds(source, size), :]
            after = state[pl.ds(min(source + size, (CHUNKS - 1) * size), MODES), :]
            before = state[pl.ds(max(source - MODES, 0), MODES), :]
            out_ref[pl.ds(at + size, MODES), :] = jnp.where(low, after, before)

    @pl.when(even_block())
    def _():
        write(ORDER)

    @pl.when(jnp.logical_not(even_block()))
    def _():
        write(BACKWARDS)


def window_part(guess, initial, slabs):
    return pl.pallas_call(
        functools.partial(window_kernel, slabs),
        out_shape=jax.ShapeDtypeStruct((CHUNKS * WINDOW, LANES), jnp.float32),
        in_specs=[pl.BlockSpec(memory_space=pltpu.HBM)] * 2,
        out_specs=pl.BlockSpec(memory_space=pltpu.VMEM),
        scratch_shapes=[pltpu.VMEM(guess.shape, jnp.float32), pltpu.SemaphoreType.DMA((COPIES,))],
        compiler_params=pltpu.CompilerParams(vmem_limit_bytes=16 * 1024 * 1024),
        name="windows",
    )(*(pltpu.with_memory_space_constraint(x, pltpu.HBM) for x in (guess, initial)))


def window_rows(half, r, k):
    return pl.ds((half * ROWS * (CHUNK + 1) + r) * MODES + k, ROWS, stride=WINDOW)


SHARE = LANES // MODES
COEFS = HALVES * ROWS


def edge_kernel(window_ref, speed_ref, flag_ref, out_ref):
    _, chunk = place()
    tail = chunk == CHUNKS - 1
    rows = speed_ref.shape[0]
    group = lax.broadcasted_iota(jnp.int32, (ROWS, LANES), 1) // SHARE
    for half in range(HALVES):
        packed = jnp.zeros((ROWS, LANES), jnp.float32)
        for k in range(MODES):
            first, final = window_ref[window_rows(half, 0, k), :], window_ref[window_rows(half, CHUNK - 1, k), :]
            moved = jnp.where(tail, pltpu.roll(final, (k + 1) * SHARE % LANES, 1), pltpu.roll(first, k * SHARE, 1))
            packed = jnp.where(group == k, moved, packed)
        out_ref[pl.ds(half * ROWS, ROWS), :] = packed
    at = jnp.where(tail, rows - 1, 0)
    out_ref[pl.ds(COEFS, 1), :] = speed_ref[pl.ds(at, 1), :]
    out_ref[pl.ds(COEFS + 1, 1), :] = 1.0 - flag_ref[pl.ds(at, 1), :].astype(jnp.float32)
    out_ref[pl.ds(COEFS + 2, ROWS - 2), :] = jnp.zeros((ROWS - 2, LANES), jnp.float32)


def coarse_kernel(window_ref, speed_ref, out_ref):
    quad, chunk = place()
    shape = (ROWS, LANES)
    last = jnp.logical_and(quad == QUAD - 1, lax.broadcasted_iota(jnp.int32, shape, 0) == ROWS - 1)
    for r in range(CHUNK):
        speed = jnp.broadcast_to(speed_ref[pl.ds(chunk * CHUNK + r, 1), :], shape)
        speed2 = 2.0 * speed
        for half in range(HALVES):
            start = [window_ref[window_rows(half, r, k), :] for k in range(MODES)]
            coarse = three_sections(start, lambda u: local_rhs(u, speed, speed2), STEPS * STEP)
            if half == HALVES - 1:
                coarse = [jnp.where(last, 0.0, x) for x in coarse]
            for k in range(MODES):
                out_ref[slab_rows(half, r, k), :] = coarse[k]


def slab_rows(half, r, k):
    return pl.ds((half * ROWS * CHUNK + r) * MODES + k, ROWS, stride=CHUNK * MODES)


def derived(speed, opened):
    gate = [(0.5 * VISCOSITY) * x for x in opened]
    inflow = [x * y for x, y in zip(opened, shifted(speed, 1))]
    return speed, [2.0 * x for x in speed], inflow, gate, shifted(gate, -1)


def fine_steps(starts, coefs):
    def advance(_, us):
        nows = us
        for share in (3.0, 2.0, 1.0):
            scale = column_scales(STEP / share)
            nows = [full_step(u, now, scale, *coefs) for u, now in zip(us, nows)]
        return nows

    return lax.fori_loop(0, STEPS, advance, starts, unroll=True)


def fine_kernel(window_ref, coarse_ref, speed_ref, flag_ref, out_ref):
    _, chunk = place()
    first, final = chunk == 0, chunk == CHUNKS - 1
    shape = (ROWS, LANES)
    lane = lax.broadcasted_iota(jnp.int32, shape, 1)
    low = lane < LANES // 2
    outside = jnp.logical_or(jnp.logical_and(low, final), jnp.logical_and(lane >= LANES // 2, first))

    def coef(read):
        at = chunk * CHUNK
        own = [jnp.broadcast_to(read(at + r), shape) for r in range(CHUNK)]
        after = jnp.broadcast_to(read(jnp.minimum(at + CHUNK, CHUNKS * CHUNK - 1)), shape)
        before = jnp.broadcast_to(read(jnp.maximum(at - 1, 0)), shape)
        return [*own, jnp.where(outside, 0.0, jnp.where(low, after, before))]

    speed = coef(lambda i: speed_ref[pl.ds(i, 1), :])
    opened = coef(lambda i: 1.0 - flag_ref[pl.ds(i, 1), :].astype(jnp.float32))
    wall = jnp.logical_and(jnp.logical_and(first, lax.axis_index("space") == 0), lane == 0)
    opened[0] = jnp.where(wall, 0.0, opened[0])
    coefs = derived(speed, opened)
    starts = []
    for half in range(HALVES):
        start = [[window_ref[window_rows(half, r, k), :] for k in range(MODES)] for r in range(CHUNK + 1)]
        start[CHUNK] = [jnp.where(outside, 0.0, x) for x in start[CHUNK]]
        starts.append(start)
    finals = fine_steps(starts, coefs)
    for half in range(HALVES):
        for r in range(CHUNK):
            for k in range(MODES):
                rows = slab_rows(half, r, k)
                out_ref[rows, :] = finals[half][r][k] - coarse_ref[rows, :]


def end_kernel(term_ref, window_ref, coarse_ref, message_ref, speed_ref, flag_ref, out_ref):
    _, chunk = place()
    first, final = chunk == 0, chunk == CHUNKS - 1
    out_ref[...] = term_ref[...]

    @pl.when(jnp.logical_or(first, final))
    def _():
        shape = (ROWS, LANES)
        lane = lax.broadcasted_iota(jnp.int32, shape, 1)
        low = lane < LANES // 2
        own_side = jnp.logical_xor(low, final)
        at = jnp.where(first, 0, CHUNKS * CHUNK - 1)

        def joined_row(own, other):
            return pltpu.roll(jnp.where(own_side, own, other), LANES // 2, 1)

        opened = 1.0 - flag_ref[pl.ds(at, 1), :].astype(jnp.float32)
        wall = jnp.logical_and(jnp.logical_and(first, lax.axis_index("space") == 0), lane == 0)
        opened = jnp.where(wall, 0.0, jnp.broadcast_to(opened, shape))
        beyond = [jnp.broadcast_to(message_ref[pl.ds(COEFS + i, 1), :], shape) for i in range(2)]
        speed = joined_row(jnp.broadcast_to(speed_ref[pl.ds(at, 1), :], shape), beyond[0])
        coefs = derived([speed], [joined_row(opened, beyond[1])])
        starts = []
        for half in range(HALVES):
            packed = message_ref[pl.ds(half * ROWS, ROWS), :]
            start = []
            for k in range(MODES):
                own = jnp.where(first, window_ref[window_rows(half, 0, k), :], window_ref[window_rows(half, CHUNK - 1, k), :])
                after, before = pltpu.roll(packed, -k * SHARE % LANES, 1), pltpu.roll(packed, (MODES - 1 - k) * SHARE, 1)
                start.append(joined_row(own, jnp.where(final, after, before)))
            starts.append([start])
        finals = fine_steps(starts, coefs)
        near_end = jnp.logical_or(jnp.logical_and(first, lane < SHARE), jnp.logical_and(final, lane >= LANES - SHARE))
        for r, here in ((0, first), (CHUNK - 1, final)):

            @pl.when(here)
            def _(r=r):
                for half in range(HALVES):
                    for k in range(MODES):
                        rows = slab_rows(half, r, k)
                        made = pltpu.roll(finals[half][0][k], LANES // 2, 1) - coarse_ref[rows, :]
                        out_ref[rows, :] = jnp.where(near_end, made, term_ref[rows, :])


def write_kernel(sums_ref, out_ref, sems):
    size = CHUNK * MODES

    def write(chunks):
        starts = [i for i in range(CHUNKS) if i == 0 or chunks[i] != chunks[i - 1] + 1]
        copies = []
        for position, end in zip(starts, [*starts[1:], CHUNKS]):
            count = (end - position) * size
            source, target = pl.ds(position * size, count), pl.ds(chunks[position] * size, count)
            copies.append(pltpu.make_async_copy(sums_ref.at[source], out_ref.at[target], sems.at[position]))
        for copy in copies:
            copy.start()
        for copy in copies:
            copy.wait()

    @pl.when(even_block())
    def _():
        write(ORDER)

    @pl.when(jnp.logical_not(even_block()))
    def _():
        write(BACKWARDS)


def write_part(sums):
    return pl.pallas_call(
        write_kernel,
        out_shape=jax.ShapeDtypeStruct(sums.shape, jnp.float32),
        in_specs=[pl.BlockSpec(memory_space=pltpu.VMEM)],
        out_specs=pl.BlockSpec(memory_space=pl.ANY),
        scratch_shapes=[pltpu.SemaphoreType.DMA((CHUNKS,))],
        compiler_params=pltpu.CompilerParams(vmem_limit_bytes=16 * 1024 * 1024),
        name="write_out",
    )(sums)


def times(matrix, field):
    out = []
    for row in matrix:
        total = row[0] * field[0]
        for entry, value in zip(row[1:], field[1:]):
            total = total + entry * value
        out.append(total)
    return out


def square(matrix):
    columns = [times(matrix, [matrix[i][j] for i in range(MODES)]) for j in range(MODES)]
    return [[columns[j][i] for j in range(MODES)] for i in range(MODES)]


def added(xs, ys):
    return [x + y for x, y in zip(xs, ys)]


def chosen(test, xs, ys):
    return [jnp.where(test, x, y) for x, y in zip(xs, ys)]


def coarse_matrix(speed_ref, chunk):
    rows = [speed_ref[pl.ds(chunk * CHUNK + r, 1), :] for r in range(CHUNK)]
    speed = jnp.concatenate(rows * (ROWS // CHUNK), 0)
    speed2 = 2.0 * speed
    zero, one = jnp.zeros_like(speed), jnp.ones_like(speed)
    columns = [
        three_sections([one if i == j else zero for i in range(MODES)], lambda u: local_rhs(u, speed, speed2), STEPS * STEP)
        for j in range(MODES)
    ]
    return [[columns[j][i] for j in range(MODES)] for i in range(MODES)]


def term_rows(step, half, k):
    return pl.ds((step * QUAD * CHUNK + half * ROWS) * MODES + k, ROWS, stride=MODES)


def carry_rows(half, k):
    return pl.ds((k * HALVES + half) * ROWS, ROWS)


def quad_kernel(term_ref, speed_ref, carry_ref):
    quad, chunk = place()
    matrix = coarse_matrix(speed_ref, chunk)
    row = lax.broadcasted_iota(jnp.int32, (ROWS, LANES), 0)
    for half in range(HALVES):
        terms = [[term_ref[term_rows(step, half, k), :] for k in range(MODES)] for step in range(QUAD)]
        total = terms[0]
        for step in range(1, QUAD):
            total = added(times(matrix, total), terms[step])
        if half == HALVES - 1:
            total = chosen(jnp.logical_and(quad == QUAD - 1, row >= CHUNK), terms[-1], total)
        for k in range(MODES):
            carry_ref[carry_rows(half, k), :] = total[k]


def read_carry(ref, half):
    return [ref[carry_rows(half, k), :] for k in range(MODES)]


def joined(over_quad, quad, own, partner, half, row):
    odd = quad % 2 == 1
    earlier, later = chosen(odd, partner, own), chosen(odd, own, partner)
    both = added(times(over_quad, earlier), later)
    if half < HALVES - 1:
        return both
    return chosen(jnp.logical_and(quad >= 2, row >= CHUNK), later, both)


def pair_kernel(carry_ref, partner_ref, speed_ref, out_ref):
    quad, chunk = place()
    over_quad = square(square(coarse_matrix(speed_ref, chunk)))
    row = lax.broadcasted_iota(jnp.int32, (ROWS, LANES), 0)
    for half in range(HALVES):
        both = joined(over_quad, quad, read_carry(carry_ref, half), read_carry(partner_ref, half), half, row)
        for k in range(MODES):
            out_ref[carry_rows(half, k), :] = both[k]


def slab_kernel(term_ref, carry_ref, partner_ref, far_ref, speed_ref, out_ref):
    quad, chunk = place()
    matrix = coarse_matrix(speed_ref, chunk)
    over_quad = square(square(matrix))
    over_pair = square(over_quad)
    over_y = square(over_pair)
    row = lax.broadcasted_iota(jnp.int32, (ROWS, LANES), 0)
    low = row < CHUNK
    high_pair, odd = quad >= 2, quad % 2 == 1

    def swapped(xs):
        return [pltpu.roll(x, CHUNK, 0) for x in xs]

    here, total = [], []
    for half in range(HALVES):
        own, partner, far = (read_carry(ref, half) for ref in (carry_ref, partner_ref, far_ref))
        both = joined(over_quad, quad, own, partner, half, row)
        before_pair = [jnp.where(high_pair, x, 0.0) for x in far]
        here.append(chosen(odd, added(times(over_quad, before_pair), partner), before_pair))
        first_pair, second_pair = chosen(high_pair, far, both), chosen(high_pair, both, far)
        total.append(added(times(over_pair, first_pair), second_pair))
    first = swapped(second_pair)
    second = swapped(added(times(over_y, first), total[0]))
    pair = chosen(low, first, second)
    third = swapped(added(times(over_y, pair), total[0]))
    fourth = swapped(added(times(over_y, third), total[1]))
    starts = [pair, chosen(low, third, fourth)]
    for half in range(HALVES):
        state = starts[half]
        state = chosen(high_pair, times(over_pair, state), state)
        state = chosen(odd, times(over_quad, state), state)
        state = added(state, here[half])
        for step in range(QUAD):
            for k in range(MODES):
                out_ref[term_rows(step, half, k), :] = state[k]
            if step < QUAD - 1:
                terms = [term_ref[term_rows(step, half, k), :] for k in range(MODES)]
                state = added(times(matrix, state), terms)


def on_device(kernel, name, rows, *operands):
    return pl.pallas_call(
        kernel,
        out_shape=jax.ShapeDtypeStruct((rows, LANES), jnp.float32),
        in_specs=[pl.BlockSpec(memory_space=pltpu.VMEM)] * len(operands),
        out_specs=pl.BlockSpec(memory_space=pltpu.VMEM),
        compiler_params=pltpu.CompilerParams(vmem_limit_bytes=16 * 1024 * 1024),
        name=name,
    )(*operands)


def swap_blocks(x, groups):
    return lax.all_to_all(x.reshape(-1, MODES, LANES), "tm", 0, 0, axis_index_groups=groups, tiled=True).reshape(x.shape)


def body(initial, guess, speeds, flags):
    slabs, blocks = lax.axis_size("tm"), lax.axis_size("space")
    count = initial.shape[1]
    rows = count // LANES

    def by_row(x):
        return x.reshape(MODES, rows, LANES).transpose(1, 0, 2).reshape(rows * MODES, LANES)

    speed_rows, flag_rows = speeds.reshape(rows, LANES), flags.reshape(rows, LANES)
    quads, ys = range(QUAD), range(slabs // QUAD**2)
    of_quad = [[y * QUAD**2 + q * QUAD + step for step in range(QUAD) for y in ys] for q in quads]
    windows = swap_blocks(window_part(by_row(guess[0]), by_row(initial), slabs), of_quad)
    pairs = []
    for group in of_quad:
        for slab, start in ((group[ORDER.index(CHUNKS - 1)], 0), (group[ORDER.index(0)], 1)):
            for i in range(start, blocks - 1, 2):
                ends = slab * blocks + i, slab * blocks + i + 1
                pairs += [ends, ends[::-1]]
    edge = on_device(edge_kernel, "edge_rows", COEFS + ROWS, windows, speed_rows, flag_rows)
    message = lax.ppermute(edge, ("tm", "space"), pairs)
    coarse = on_device(coarse_kernel, "coarse_steps", rows * MODES, windows, speed_rows)
    terms = on_device(fine_kernel, "fine_steps", rows * MODES, windows, coarse, speed_rows, flag_rows)
    terms = on_device(end_kernel, "block_ends", rows * MODES, terms, windows, coarse, message, speed_rows, flag_rows)
    size = MODES * HALVES * ROWS
    carry = on_device(quad_kernel, "quad_carry", size, terms, speed_rows)
    partner = lax.ppermute(carry, "tm", [(c, c ^ QUAD) for c in range(slabs)])
    joint = on_device(pair_kernel, "pair_carry", size, carry, partner, speed_rows)
    far = lax.ppermute(joint, "tm", [(c, c ^ (3 * QUAD)) for c in range(slabs)])
    sums = on_device(slab_kernel, "slab_sums", rows * MODES, terms, carry, partner, far, speed_rows)
    sums = write_part(swap_blocks(sums, of_quad)).reshape(rows, MODES, LANES)
    return sums.transpose(1, 0, 2).reshape(1, MODES, count)


def solution(mesh):
    return jax.shard_map(
        body,
        mesh=mesh,
        in_specs=(P(None, "space"), P("tm", None, "space"), P("space"), P("space")),
        out_specs=P("tm", None, "space"),
        check_vma=False,
    )
```

```python
import functools

import jax
import jax.numpy as jnp
from jax import lax
from jax.experimental import pallas as pl
from jax.experimental.pallas import tpu as pltpu
from jax.sharding import PartitionSpec as P

MODES = 4
STEPS = 8
LANES = 128
ROWS = 8
VISCOSITY = 0.02
PENALTY = 10.0
STEP = 0.015625
JACOBIAN = 8.0
INV_MASS = (0.5, 1.5, 2.5, 3.5)


def column_scales(delta):
    return [JACOBIAN * m * delta for m in INV_MASS]


def shifted(xs, step):
    rolled = [pltpu.roll(x, step % LANES, 1) for x in xs]
    lane = lax.broadcasted_iota(jnp.int32, xs[0].shape, 1)
    edge = lane == (0 if step == 1 else LANES - 1)
    return [jnp.where(edge, rolled[(v - step) % len(xs)], x) for v, x in enumerate(rolled)]


def volume_terms(u, speed2, p, q):
    a, b, c, d = u
    vq = (2.0 * VISCOSITY) * q
    m1 = speed2 * a - vq
    m2 = speed2 * b - (6.0 * VISCOSITY) * c
    m3 = speed2 * p - vq - (10.0 * VISCOSITY) * d
    return m1, m2, m3


def local_rhs(u, speed, speed2):
    a, b, c, d = u
    p, q = a + c, b + d
    out = -(speed * (p + q))
    m1, m2, m3 = volume_terms(u, speed2, p, q)
    return out, out + m1, out + m2, out + m3


def traces(u):
    a, b, c, d = u
    p, q = a + c, b + d
    odd, even = b + 6.0 * d, 3.0 * c
    return p + q, p - q, odd + even, odd - even


def full_step(start, now, scale, speed, speed2, inflow, gate, gate_after):
    tr, tl, sr, sl = zip(*(traces(u) for u in now))
    tr_b, sr_b, tl_a, sl_a = shifted(tr, 1), shifted(sr, 1), shifted(tl, -1), shifted(sl, -1)
    result = []
    for v, u in enumerate(now):
        jump = tr_b[v] - tl[v]
        k_l = gate[v] * jump
        g_l = inflow[v] * tr_b[v] - gate[v] * (sr_b[v] + sl[v] - (2.0 * PENALTY) * jump)
        jump = tr[v] - tl_a[v]
        k_r = gate_after[v] * jump
        base = gate_after[v] * (sr[v] + sl_a[v] - (2.0 * PENALTY) * jump) - speed[v] * tr[v]
        plus, minus = base + g_l, base - g_l
        k_sum, k_dif = k_r + k_l, k_r - k_l
        m1, m2, m3 = volume_terms(u, speed2[v], u[0] + u[2], u[1] + u[3])
        rhs = plus, minus + k_sum + m1, plus + 3.0 * k_dif + m2, minus + 6.0 * k_sum + m3
        result.append([x + f * r for x, f, r in zip(start[v], scale, rhs)])
    return result


def three_sections(u, rhs, delta):
    v = u
    for share in (3.0, 2.0, 1.0):
        scale = column_scales(delta / share)
        v = [x + f * r for x, f, r in zip(u, scale, rhs(v))]
    return v


QUAD = 4
CHUNK = 4
HALVES = 2
CHUNKS = 16
WINDOW = CHUNK * MODES + 2
SHARE = LANES // MODES
ORDER = (1, 2, 3, 4, 0, 15, 5, 6, 7, 8, 9, 10, 11, 12, 13, 14)
BACKWARDS = tuple(CHUNKS - 1 - chunk for chunk in ORDER)


def even_block():
    return lax.axis_index("space") % 2 == 0


def place():
    slab = lax.axis_index("tm")
    y, z = slab // (QUAD * QUAD), slab % (QUAD * QUAD)
    position = (z % QUAD) * QUAD + y
    chunk = position
    for i, there in enumerate(ORDER):
        if i != there:
            chunk = jnp.where(position == i, there, chunk)
    return z // QUAD, jnp.where(even_block(), chunk, CHUNKS - 1 - chunk)


COPIES = 4


def window_kernel(slabs, guess_ref, initial_ref, out_ref, state, sems):
    last = lax.axis_index("tm") == slabs - 1
    rows = state.shape[0] // COPIES

    def copies(source):
        parts = [pl.ds(i * rows, rows) for i in range(COPIES)]
        return [pltpu.make_async_copy(source.at[part], state.at[part], sems.at[i]) for i, part in enumerate(parts)]

    @pl.when(last)
    def _():
        for copy in copies(initial_ref):
            copy.start()

    @pl.when(jnp.logical_not(last))
    def _():
        for copy in copies(guess_ref):
            copy.start()

    for copy in copies(guess_ref):
        copy.wait()
    size = CHUNK * MODES
    group = lax.broadcasted_iota(jnp.int32, (ROWS, LANES), 1) // SHARE

    def packed(row, shift):
        vectors = []
        for i in range(CHUNKS // ROWS):
            total = jnp.zeros((ROWS, LANES), jnp.float32)
            for k in range(MODES):
                read = state[pl.ds(i * ROWS * size + row * MODES + k, ROWS, stride=size), :]
                total = jnp.where(group == k, pltpu.roll(read, (k * SHARE + shift) % LANES, 1), total)
            vectors.append(total)
        return [vectors[n // ROWS][n % ROWS : n % ROWS + 1] for n in range(CHUNKS)]

    heads, tails = packed(0, 0), packed(CHUNK - 1, SHARE)
    none = jnp.zeros((1, LANES), jnp.float32)

    def write(chunks):
        for position, chunk in enumerate(chunks):
            at = position * WINDOW
            out_ref[pl.ds(at, size), :] = state[pl.ds(chunk * size, size), :]
            out_ref[pl.ds(at + size, 1), :] = heads[chunk + 1] if chunk < CHUNKS - 1 else none
            out_ref[pl.ds(at + size + 1, 1), :] = tails[chunk - 1] if chunk else none

    @pl.when(even_block())
    def _():
        write(ORDER)

    @pl.when(jnp.logical_not(even_block()))
    def _():
        write(BACKWARDS)


def window_part(guess, initial, slabs):
    return pl.pallas_call(
        functools.partial(window_kernel, slabs),
        out_shape=jax.ShapeDtypeStruct((CHUNKS * WINDOW, LANES), jnp.float32),
        in_specs=[pl.BlockSpec(memory_space=pltpu.HBM)] * 2,
        out_specs=pl.BlockSpec(memory_space=pltpu.VMEM),
        scratch_shapes=[pltpu.VMEM(guess.shape, jnp.float32), pltpu.SemaphoreType.DMA((COPIES,))],
        compiler_params=pltpu.CompilerParams(vmem_limit_bytes=16 * 1024 * 1024),
        name="windows",
    )(*(pltpu.with_memory_space_constraint(x, pltpu.HBM) for x in (guess, initial)))


def window_rows(half, r, k):
    return pl.ds(half * ROWS * WINDOW + r * MODES + k, ROWS, stride=WINDOW)


def unpacked(after, before, k, low):
    return jnp.where(low, pltpu.roll(after, -k * SHARE % LANES, 1), pltpu.roll(before, (MODES - 1 - k) * SHARE, 1))


COEFS = HALVES * ROWS


def edge_kernel(window_ref, speed_ref, flag_ref, out_ref):
    _, chunk = place()
    tail = chunk == CHUNKS - 1
    rows = speed_ref.shape[0]
    group = lax.broadcasted_iota(jnp.int32, (ROWS, LANES), 1) // SHARE
    for half in range(HALVES):
        packed = jnp.zeros((ROWS, LANES), jnp.float32)
        for k in range(MODES):
            first, final = window_ref[window_rows(half, 0, k), :], window_ref[window_rows(half, CHUNK - 1, k), :]
            moved = jnp.where(tail, pltpu.roll(final, (k + 1) * SHARE % LANES, 1), pltpu.roll(first, k * SHARE, 1))
            packed = jnp.where(group == k, moved, packed)
        out_ref[pl.ds(half * ROWS, ROWS), :] = packed
    at = jnp.where(tail, rows - 1, 0)
    out_ref[pl.ds(COEFS, 1), :] = speed_ref[pl.ds(at, 1), :]
    out_ref[pl.ds(COEFS + 1, 1), :] = 1.0 - flag_ref[pl.ds(at, 1), :].astype(jnp.float32)
    out_ref[pl.ds(COEFS + 2, ROWS - 2), :] = jnp.zeros((ROWS - 2, LANES), jnp.float32)


def coarse_kernel(window_ref, speed_ref, out_ref):
    quad, chunk = place()
    shape = (ROWS, LANES)
    last = jnp.logical_and(quad == QUAD - 1, lax.broadcasted_iota(jnp.int32, shape, 0) == ROWS - 1)
    for r in range(CHUNK):
        speed = jnp.broadcast_to(speed_ref[pl.ds(chunk * CHUNK + r, 1), :], shape)
        speed2 = 2.0 * speed
        for half in range(HALVES):
            start = [window_ref[window_rows(half, r, k), :] for k in range(MODES)]
            coarse = three_sections(start, lambda u: local_rhs(u, speed, speed2), STEPS * STEP)
            if half == HALVES - 1:
                coarse = [jnp.where(last, 0.0, x) for x in coarse]
            for k in range(MODES):
                out_ref[slab_rows(half, r, k), :] = coarse[k]


def slab_rows(half, r, k):
    return pl.ds((half * ROWS * CHUNK + r) * MODES + k, ROWS, stride=CHUNK * MODES)


def derived(speed, opened):
    gate = [(0.5 * VISCOSITY) * x for x in opened]
    inflow = [x * y for x, y in zip(opened, shifted(speed, 1))]
    return speed, [2.0 * x for x in speed], inflow, gate, shifted(gate, -1)


def fine_steps(starts, coefs):
    def advance(_, us):
        nows = us
        for share in (3.0, 2.0, 1.0):
            scale = column_scales(STEP / share)
            nows = [full_step(u, now, scale, *coefs) for u, now in zip(us, nows)]
        return nows

    return lax.fori_loop(0, STEPS, advance, starts, unroll=True)


def fine_kernel(window_ref, coarse_ref, speed_ref, flag_ref, out_ref):
    _, chunk = place()
    first, final = chunk == 0, chunk == CHUNKS - 1
    shape = (ROWS, LANES)
    lane = lax.broadcasted_iota(jnp.int32, shape, 1)
    low = lane < LANES // 2
    outside = jnp.logical_or(jnp.logical_and(low, final), jnp.logical_and(lane >= LANES // 2, first))

    def coef(read):
        at = chunk * CHUNK
        own = [jnp.broadcast_to(read(at + r), shape) for r in range(CHUNK)]
        after = jnp.broadcast_to(read(jnp.minimum(at + CHUNK, CHUNKS * CHUNK - 1)), shape)
        before = jnp.broadcast_to(read(jnp.maximum(at - 1, 0)), shape)
        return [*own, jnp.where(outside, 0.0, jnp.where(low, after, before))]

    speed = coef(lambda i: speed_ref[pl.ds(i, 1), :])
    opened = coef(lambda i: 1.0 - flag_ref[pl.ds(i, 1), :].astype(jnp.float32))
    wall = jnp.logical_and(jnp.logical_and(first, lax.axis_index("space") == 0), lane == 0)
    opened[0] = jnp.where(wall, 0.0, opened[0])
    coefs = derived(speed, opened)
    starts = []
    for half in range(HALVES):
        start = [[window_ref[window_rows(half, r, k), :] for k in range(MODES)] for r in range(CHUNK)]
        after, before = (window_ref[window_rows(half, CHUNK, i), :] for i in range(2))
        start.append([jnp.where(outside, 0.0, unpacked(after, before, k, low)) for k in range(MODES)])
        starts.append(start)
    finals = fine_steps(starts, coefs)
    for half in range(HALVES):
        for r in range(CHUNK):
            for k in range(MODES):
                rows = slab_rows(half, r, k)
                out_ref[rows, :] = finals[half][r][k] - coarse_ref[rows, :]


def end_kernel(term_ref, window_ref, coarse_ref, message_ref, speed_ref, flag_ref, out_ref):
    _, chunk = place()
    first, final = chunk == 0, chunk == CHUNKS - 1
    out_ref[...] = term_ref[...]

    @pl.when(jnp.logical_or(first, final))
    def _():
        shape = (ROWS, LANES)
        lane = lax.broadcasted_iota(jnp.int32, shape, 1)
        low = lane < LANES // 2
        own_side = jnp.logical_xor(low, final)
        at = jnp.where(first, 0, CHUNKS * CHUNK - 1)

        def joined_row(own, other):
            return pltpu.roll(jnp.where(own_side, own, other), LANES // 2, 1)

        opened = 1.0 - flag_ref[pl.ds(at, 1), :].astype(jnp.float32)
        wall = jnp.logical_and(jnp.logical_and(first, lax.axis_index("space") == 0), lane == 0)
        opened = jnp.where(wall, 0.0, jnp.broadcast_to(opened, shape))
        beyond = [jnp.broadcast_to(message_ref[pl.ds(COEFS + i, 1), :], shape) for i in range(2)]
        speed = joined_row(jnp.broadcast_to(speed_ref[pl.ds(at, 1), :], shape), beyond[0])
        coefs = derived([speed], [joined_row(opened, beyond[1])])
        starts = []
        for half in range(HALVES):
            packed = message_ref[pl.ds(half * ROWS, ROWS), :]
            start = []
            for k in range(MODES):
                own = jnp.where(first, window_ref[window_rows(half, 0, k), :], window_ref[window_rows(half, CHUNK - 1, k), :])
                start.append(joined_row(own, unpacked(packed, packed, k, low)))
            starts.append([start])
        finals = fine_steps(starts, coefs)
        near_end = jnp.logical_or(jnp.logical_and(first, lane < SHARE), jnp.logical_and(final, lane >= LANES - SHARE))
        for r, here in ((0, first), (CHUNK - 1, final)):

            @pl.when(here)
            def _(r=r):
                for half in range(HALVES):
                    for k in range(MODES):
                        rows = slab_rows(half, r, k)
                        made = pltpu.roll(finals[half][0][k], LANES // 2, 1) - coarse_ref[rows, :]
                        out_ref[rows, :] = jnp.where(near_end, made, term_ref[rows, :])


def write_kernel(sums_ref, out_ref, sems):
    size = CHUNK * MODES

    def write(pairs, count):
        copies = []
        for i, (source, target) in enumerate(pairs):
            source, target = pl.ds(source * size, count * size), pl.ds(target * size, count * size)
            copies.append(pltpu.make_async_copy(sums_ref.at[source], out_ref.at[target], sems.at[i]))
        for copy in copies:
            copy.start()
        for copy in copies:
            copy.wait()

    @pl.when(even_block())
    def _():
        write([(i, i) for i in range(0, CHUNKS, CHUNKS // COPIES)], CHUNKS // COPIES)

    @pl.when(jnp.logical_not(even_block()))
    def _():
        write([(i, CHUNKS - 1 - i) for i in range(CHUNKS)], 1)


def write_part(sums):
    return pl.pallas_call(
        write_kernel,
        out_shape=jax.ShapeDtypeStruct(sums.shape, jnp.float32),
        in_specs=[pl.BlockSpec(memory_space=pltpu.VMEM)],
        out_specs=pl.BlockSpec(memory_space=pl.ANY),
        scratch_shapes=[pltpu.SemaphoreType.DMA((CHUNKS,))],
        compiler_params=pltpu.CompilerParams(vmem_limit_bytes=16 * 1024 * 1024),
        name="write_out",
    )(sums)


def times(matrix, field):
    out = []
    for row in matrix:
        total = row[0] * field[0]
        for entry, value in zip(row[1:], field[1:]):
            total = total + entry * value
        out.append(total)
    return out


def square(matrix):
    columns = [times(matrix, [matrix[i][j] for i in range(MODES)]) for j in range(MODES)]
    return [[columns[j][i] for j in range(MODES)] for i in range(MODES)]


def added(xs, ys):
    return [x + y for x, y in zip(xs, ys)]


def chosen(test, xs, ys):
    return [jnp.where(test, x, y) for x, y in zip(xs, ys)]


def coarse_matrix(speed_ref, chunk):
    rows = [speed_ref[pl.ds(chunk * CHUNK + r, 1), :] for r in range(CHUNK)]
    speed = jnp.concatenate(rows * (ROWS // CHUNK), 0)
    speed2 = 2.0 * speed
    zero, one = jnp.zeros_like(speed), jnp.ones_like(speed)
    columns = [
        three_sections([one if i == j else zero for i in range(MODES)], lambda u: local_rhs(u, speed, speed2), STEPS * STEP)
        for j in range(MODES)
    ]
    return [[columns[j][i] for j in range(MODES)] for i in range(MODES)]


def term_rows(step, half, k):
    return pl.ds((step * QUAD * CHUNK + half * ROWS) * MODES + k, ROWS, stride=MODES)


def carry_rows(half, k):
    return pl.ds((k * HALVES + half) * ROWS, ROWS)


def quad_kernel(term_ref, speed_ref, carry_ref):
    quad, chunk = place()
    matrix = coarse_matrix(speed_ref, chunk)
    row = lax.broadcasted_iota(jnp.int32, (ROWS, LANES), 0)
    for half in range(HALVES):
        terms = [[term_ref[term_rows(step, half, k), :] for k in range(MODES)] for step in range(QUAD)]
        total = terms[0]
        for step in range(1, QUAD):
            total = added(times(matrix, total), terms[step])
        if half == HALVES - 1:
            total = chosen(jnp.logical_and(quad == QUAD - 1, row >= CHUNK), terms[-1], total)
        for k in range(MODES):
            carry_ref[carry_rows(half, k), :] = total[k]


def read_carry(ref, half):
    return [ref[carry_rows(half, k), :] for k in range(MODES)]


def joined(over_quad, quad, own, partner, half, row):
    odd = quad % 2 == 1
    earlier, later = chosen(odd, partner, own), chosen(odd, own, partner)
    both = added(times(over_quad, earlier), later)
    if half < HALVES - 1:
        return both
    return chosen(jnp.logical_and(quad >= 2, row >= CHUNK), later, both)


def pair_kernel(carry_ref, partner_ref, speed_ref, out_ref):
    quad, chunk = place()
    over_quad = square(square(coarse_matrix(speed_ref, chunk)))
    row = lax.broadcasted_iota(jnp.int32, (ROWS, LANES), 0)
    for half in range(HALVES):
        both = joined(over_quad, quad, read_carry(carry_ref, half), read_carry(partner_ref, half), half, row)
        for k in range(MODES):
            out_ref[carry_rows(half, k), :] = both[k]


def slab_kernel(term_ref, carry_ref, partner_ref, far_ref, speed_ref, out_ref):
    quad, chunk = place()
    matrix = coarse_matrix(speed_ref, chunk)
    over_quad = square(square(matrix))
    over_pair = square(over_quad)
    over_y = square(over_pair)
    row = lax.broadcasted_iota(jnp.int32, (ROWS, LANES), 0)
    low = row < CHUNK
    high_pair, odd = quad >= 2, quad % 2 == 1

    def swapped(xs):
        return [pltpu.roll(x, CHUNK, 0) for x in xs]

    here, total = [], []
    for half in range(HALVES):
        own, partner, far = (read_carry(ref, half) for ref in (carry_ref, partner_ref, far_ref))
        both = joined(over_quad, quad, own, partner, half, row)
        before_pair = [jnp.where(high_pair, x, 0.0) for x in far]
        here.append(chosen(odd, added(times(over_quad, before_pair), partner), before_pair))
        first_pair, second_pair = chosen(high_pair, far, both), chosen(high_pair, both, far)
        total.append(added(times(over_pair, first_pair), second_pair))
    first = swapped(second_pair)
    second = swapped(added(times(over_y, first), total[0]))
    pair = chosen(low, first, second)
    third = swapped(added(times(over_y, pair), total[0]))
    fourth = swapped(added(times(over_y, third), total[1]))
    starts = [pair, chosen(low, third, fourth)]
    for half in range(HALVES):
        state = starts[half]
        state = chosen(high_pair, times(over_pair, state), state)
        state = chosen(odd, times(over_quad, state), state)
        state = added(state, here[half])
        for step in range(QUAD):
            for i in range(HALVES):
                block = ORDER[step * QUAD + half * HALVES + i] * CHUNK * MODES
                for k in range(MODES):
                    out_ref[pl.ds(block + k, CHUNK, stride=MODES), :] = state[k][i * CHUNK : (i + 1) * CHUNK]
            if step < QUAD - 1:
                terms = [term_ref[term_rows(step, half, k), :] for k in range(MODES)]
                state = added(times(matrix, state), terms)


def on_device(kernel, name, rows, *operands):
    return pl.pallas_call(
        kernel,
        out_shape=jax.ShapeDtypeStruct((rows, LANES), jnp.float32),
        in_specs=[pl.BlockSpec(memory_space=pltpu.VMEM)] * len(operands),
        out_specs=pl.BlockSpec(memory_space=pltpu.VMEM),
        compiler_params=pltpu.CompilerParams(vmem_limit_bytes=16 * 1024 * 1024),
        name=name,
    )(*operands)


def swap_blocks(x, groups, rows=MODES):
    return lax.all_to_all(x.reshape(-1, rows, LANES), "tm", 0, 0, axis_index_groups=groups, tiled=True).reshape(x.shape)


def body(initial, guess, speeds, flags):
    slabs, blocks = lax.axis_size("tm"), lax.axis_size("space")
    count = initial.shape[1]
    rows = count // LANES

    def by_row(x):
        return x.reshape(MODES, rows, LANES).transpose(1, 0, 2).reshape(rows * MODES, LANES)

    speed_rows, flag_rows = speeds.reshape(rows, LANES), flags.reshape(rows, LANES)
    quads, ys = range(QUAD), range(slabs // QUAD**2)
    of_quad = [[y * QUAD**2 + q * QUAD + step for step in range(QUAD) for y in ys] for q in quads]
    windows = swap_blocks(window_part(by_row(guess[0]), by_row(initial), slabs), of_quad, 2)
    pairs = []
    for group in of_quad:
        for slab, start in ((group[ORDER.index(CHUNKS - 1)], 0), (group[ORDER.index(0)], 1)):
            for i in range(start, blocks - 1, 2):
                ends = slab * blocks + i, slab * blocks + i + 1
                pairs += [ends, ends[::-1]]
    edge = on_device(edge_kernel, "edge_rows", COEFS + ROWS, windows, speed_rows, flag_rows)
    message = lax.ppermute(edge, ("tm", "space"), pairs)
    coarse = on_device(coarse_kernel, "coarse_steps", rows * MODES, windows, speed_rows)
    terms = on_device(fine_kernel, "fine_steps", rows * MODES, windows, coarse, speed_rows, flag_rows)
    terms = on_device(end_kernel, "block_ends", rows * MODES, terms, windows, coarse, message, speed_rows, flag_rows)
    size = MODES * HALVES * ROWS
    carry = on_device(quad_kernel, "quad_carry", size, terms, speed_rows)
    partner = lax.ppermute(carry, "tm", [(c, c ^ QUAD) for c in range(slabs)])
    joint = on_device(pair_kernel, "pair_carry", size, carry, partner, speed_rows)
    far = lax.ppermute(joint, "tm", [(c, c ^ (3 * QUAD)) for c in range(slabs)])
    sums = on_device(slab_kernel, "slab_sums", rows * MODES, terms, carry, partner, far, speed_rows)
    by_chunk = [[group[ORDER.index(i)] for i in range(CHUNKS)] for group in of_quad]
    sums = write_part(swap_blocks(sums, by_chunk)).reshape(rows, MODES, LANES)
    return sums.transpose(1, 0, 2).reshape(1, MODES, count)


def solution(mesh):
    return jax.shard_map(
        body,
        mesh=mesh,
        in_specs=(P(None, "space"), P("tm", None, "space"), P("space"), P("space")),
        out_specs=P("tm", None, "space"),
        check_vma=False,
    )
```

```python
import functools

import jax
import jax.numpy as jnp
from jax import lax
from jax.experimental import pallas as pl
from jax.experimental.pallas import tpu as pltpu
from jax.sharding import PartitionSpec as P

MODES = 4
STEPS = 8
LANES = 128
ROWS = 8
VISCOSITY = 0.02
PENALTY = 10.0
STEP = 0.015625
JACOBIAN = 8.0
INV_MASS = (0.5, 1.5, 2.5, 3.5)


def column_scales(delta):
    return [JACOBIAN * m * delta for m in INV_MASS]


def shifted(xs, step):
    rolled = [pltpu.roll(x, step % LANES, 1) for x in xs]
    lane = lax.broadcasted_iota(jnp.int32, xs[0].shape, 1)
    edge = lane == (0 if step == 1 else LANES - 1)
    return [jnp.where(edge, rolled[(v - step) % len(xs)], x) for v, x in enumerate(rolled)]


def volume_terms(u, speed2, p, q):
    a, b, c, d = u
    vq = (2.0 * VISCOSITY) * q
    m1 = speed2 * a - vq
    m2 = speed2 * b - (6.0 * VISCOSITY) * c
    m3 = speed2 * p - vq - (10.0 * VISCOSITY) * d
    return m1, m2, m3


def local_rhs(u, speed, speed2):
    a, b, c, d = u
    p, q = a + c, b + d
    out = -(speed * (p + q))
    m1, m2, m3 = volume_terms(u, speed2, p, q)
    return out, out + m1, out + m2, out + m3


def traces(u):
    a, b, c, d = u
    p, q = a + c, b + d
    odd, even = b + 6.0 * d, 3.0 * c
    return p + q, p - q, odd + even, odd - even


def full_step(start, now, scale, speed, speed2, inflow, gate, gate_after):
    tr, tl, sr, sl = zip(*(traces(u) for u in now))
    tr_b, sr_b, tl_a, sl_a = shifted(tr, 1), shifted(sr, 1), shifted(tl, -1), shifted(sl, -1)
    result = []
    for v, u in enumerate(now):
        jump = tr_b[v] - tl[v]
        k_l = gate[v] * jump
        g_l = inflow[v] * tr_b[v] - gate[v] * (sr_b[v] + sl[v] - (2.0 * PENALTY) * jump)
        jump = tr[v] - tl_a[v]
        k_r = gate_after[v] * jump
        base = gate_after[v] * (sr[v] + sl_a[v] - (2.0 * PENALTY) * jump) - speed[v] * tr[v]
        plus, minus = base + g_l, base - g_l
        k_sum, k_dif = k_r + k_l, k_r - k_l
        m1, m2, m3 = volume_terms(u, speed2[v], u[0] + u[2], u[1] + u[3])
        rhs = plus, minus + k_sum + m1, plus + 3.0 * k_dif + m2, minus + 6.0 * k_sum + m3
        result.append([x + f * r for x, f, r in zip(start[v], scale, rhs)])
    return result


def three_sections(u, rhs, delta):
    v = u
    for share in (3.0, 2.0, 1.0):
        scale = column_scales(delta / share)
        v = [x + f * r for x, f, r in zip(u, scale, rhs(v))]
    return v


QUAD = 4
CHUNK = 4
HALVES = 2
CHUNKS = 16
WINDOW = CHUNK * MODES + 2
SHARE = LANES // MODES
ORDER = (1, 2, 3, 4, 0, 15, 5, 6, 7, 8, 9, 10, 11, 12, 13, 14)
LISTED = (4, 5, 2, 3, 0, 1, 6, 7, 8, 9, 10, 11, 12, 13, 14, 15)
BACKWARDS = tuple(CHUNKS - 1 - chunk for chunk in ORDER)


def even_block():
    return lax.axis_index("space") % 2 == 0


def place():
    slab = lax.axis_index("tm")
    y, z = slab // (QUAD * QUAD), slab % (QUAD * QUAD)
    position = (z % QUAD) * QUAD + y
    chunk = position
    for i, there in enumerate(ORDER):
        if i != there:
            chunk = jnp.where(position == i, there, chunk)
    return z // QUAD, jnp.where(even_block(), chunk, CHUNKS - 1 - chunk)


COPIES = 4


def window_kernel(slabs, guess_ref, initial_ref, out_ref, state, sems):
    last = lax.axis_index("tm") == slabs - 1
    rows = state.shape[0] // COPIES

    def copies(source):
        parts = [pl.ds(i * rows, rows) for i in range(COPIES)]
        return [pltpu.make_async_copy(source.at[part], state.at[part], sems.at[i]) for i, part in enumerate(parts)]

    @pl.when(last)
    def _():
        for copy in copies(initial_ref):
            copy.start()

    @pl.when(jnp.logical_not(last))
    def _():
        for copy in copies(guess_ref):
            copy.start()

    for copy in copies(guess_ref):
        copy.wait()
    size = CHUNK * MODES
    group = lax.broadcasted_iota(jnp.int32, (ROWS, LANES), 1) // SHARE

    def packed(row, shift):
        vectors = []
        for i in range(CHUNKS // ROWS):
            total = jnp.zeros((ROWS, LANES), jnp.float32)
            for k in range(MODES):
                read = state[pl.ds(i * ROWS * size + row * MODES + k, ROWS, stride=size), :]
                total = jnp.where(group == k, pltpu.roll(read, (k * SHARE + shift) % LANES, 1), total)
            vectors.append(total)
        return [vectors[n // ROWS][n % ROWS : n % ROWS + 1] for n in range(CHUNKS)]

    heads, tails = packed(0, 0), packed(CHUNK - 1, SHARE)
    none = jnp.zeros((1, LANES), jnp.float32)

    def write(chunks):
        for position, place_there in enumerate(LISTED):
            at, chunk = position * WINDOW, chunks[place_there]
            out_ref[pl.ds(at, size), :] = state[pl.ds(chunk * size, size), :]
            out_ref[pl.ds(at + size, 1), :] = heads[chunk + 1] if chunk < CHUNKS - 1 else none
            out_ref[pl.ds(at + size + 1, 1), :] = tails[chunk - 1] if chunk else none

    @pl.when(even_block())
    def _():
        write(ORDER)

    @pl.when(jnp.logical_not(even_block()))
    def _():
        write(BACKWARDS)


def window_part(guess, initial, slabs):
    return pl.pallas_call(
        functools.partial(window_kernel, slabs),
        out_shape=jax.ShapeDtypeStruct((CHUNKS * WINDOW, LANES), jnp.float32),
        in_specs=[pl.BlockSpec(memory_space=pltpu.HBM)] * 2,
        out_specs=pl.BlockSpec(memory_space=pltpu.VMEM),
        scratch_shapes=[pltpu.VMEM(guess.shape, jnp.float32), pltpu.SemaphoreType.DMA((COPIES,))],
        compiler_params=pltpu.CompilerParams(vmem_limit_bytes=16 * 1024 * 1024),
        name="windows",
    )(*(pltpu.with_memory_space_constraint(x, pltpu.HBM) for x in (guess, initial)))


def window_rows(half, r, k):
    return pl.ds(half * ROWS * WINDOW + r * MODES + k, ROWS, stride=WINDOW)


def unpacked(after, before, k, low):
    return jnp.where(low, pltpu.roll(after, -k * SHARE % LANES, 1), pltpu.roll(before, (MODES - 1 - k) * SHARE, 1))


COEFS = HALVES * ROWS


def edge_kernel(window_ref, speed_ref, flag_ref, out_ref):
    _, chunk = place()
    tail = chunk == CHUNKS - 1
    rows = speed_ref.shape[0]
    group = lax.broadcasted_iota(jnp.int32, (ROWS, LANES), 1) // SHARE
    for half in range(HALVES):
        packed = jnp.zeros((ROWS, LANES), jnp.float32)
        for k in range(MODES):
            first, final = window_ref[window_rows(half, 0, k), :], window_ref[window_rows(half, CHUNK - 1, k), :]
            moved = jnp.where(tail, pltpu.roll(final, (k + 1) * SHARE % LANES, 1), pltpu.roll(first, k * SHARE, 1))
            packed = jnp.where(group == k, moved, packed)
        out_ref[pl.ds(half * ROWS, ROWS), :] = packed
    at = jnp.where(tail, rows - 1, 0)
    out_ref[pl.ds(COEFS, 1), :] = speed_ref[pl.ds(at, 1), :]
    out_ref[pl.ds(COEFS + 1, 1), :] = 1.0 - flag_ref[pl.ds(at, 1), :].astype(jnp.float32)
    out_ref[pl.ds(COEFS + 2, ROWS - 2), :] = jnp.zeros((ROWS - 2, LANES), jnp.float32)


def coarse_kernel(window_ref, speed_ref, out_ref):
    quad, chunk = place()
    shape = (ROWS, LANES)
    last = jnp.logical_and(quad == QUAD - 1, lax.broadcasted_iota(jnp.int32, shape, 0) == ROWS - 1)
    for r in range(CHUNK):
        speed = jnp.broadcast_to(speed_ref[pl.ds(chunk * CHUNK + r, 1), :], shape)
        speed2 = 2.0 * speed
        for half in range(HALVES):
            start = [window_ref[window_rows(half, r, k), :] for k in range(MODES)]
            coarse = three_sections(start, lambda u: local_rhs(u, speed, speed2), STEPS * STEP)
            if half == HALVES - 1:
                coarse = [jnp.where(last, 0.0, x) for x in coarse]
            for k in range(MODES):
                out_ref[slab_rows(half, r, k), :] = coarse[k]


def by_place(half, x):
    row = lax.broadcasted_iota(jnp.int32, x.shape, 0)
    return jnp.where(row % QUAD < QUAD // 2, pltpu.roll(x, QUAD, 0), x) if half == 0 else x


def slab_rows(half, r, k):
    return pl.ds((half * ROWS * CHUNK + r) * MODES + k, ROWS, stride=CHUNK * MODES)


def derived(speed, opened):
    gate = [(0.5 * VISCOSITY) * x for x in opened]
    inflow = [x * y for x, y in zip(opened, shifted(speed, 1))]
    return speed, [2.0 * x for x in speed], inflow, gate, shifted(gate, -1)


def fine_steps(starts, coefs):
    def advance(_, us):
        nows = us
        for share in (3.0, 2.0, 1.0):
            scale = column_scales(STEP / share)
            nows = [full_step(u, now, scale, *coefs) for u, now in zip(us, nows)]
        return nows

    return lax.fori_loop(0, STEPS, advance, starts, unroll=True)


def fine_kernel(window_ref, coarse_ref, speed_ref, flag_ref, out_ref):
    _, chunk = place()
    first, final = chunk == 0, chunk == CHUNKS - 1
    shape = (ROWS, LANES)
    lane = lax.broadcasted_iota(jnp.int32, shape, 1)
    low = lane < LANES // 2
    outside = jnp.logical_or(jnp.logical_and(low, final), jnp.logical_and(lane >= LANES // 2, first))

    def coef(read):
        at = chunk * CHUNK
        own = [jnp.broadcast_to(read(at + r), shape) for r in range(CHUNK)]
        after = jnp.broadcast_to(read(jnp.minimum(at + CHUNK, CHUNKS * CHUNK - 1)), shape)
        before = jnp.broadcast_to(read(jnp.maximum(at - 1, 0)), shape)
        return [*own, jnp.where(outside, 0.0, jnp.where(low, after, before))]

    speed = coef(lambda i: speed_ref[pl.ds(i, 1), :])
    opened = coef(lambda i: 1.0 - flag_ref[pl.ds(i, 1), :].astype(jnp.float32))
    wall = jnp.logical_and(jnp.logical_and(first, lax.axis_index("space") == 0), lane == 0)
    opened[0] = jnp.where(wall, 0.0, opened[0])
    coefs = derived(speed, opened)
    starts = []
    for half in range(HALVES):
        start = [[window_ref[window_rows(half, r, k), :] for k in range(MODES)] for r in range(CHUNK)]
        after, before = (window_ref[window_rows(half, CHUNK, i), :] for i in range(2))
        start.append([jnp.where(outside, 0.0, unpacked(after, before, k, low)) for k in range(MODES)])
        starts.append(start)
    finals = fine_steps(starts, coefs)
    for half in range(HALVES):
        for r in range(CHUNK):
            for k in range(MODES):
                rows = slab_rows(half, r, k)
                out_ref[rows, :] = by_place(half, finals[half][r][k] - coarse_ref[rows, :])


def end_kernel(term_ref, window_ref, coarse_ref, message_ref, speed_ref, flag_ref, out_ref):
    _, chunk = place()
    first, final = chunk == 0, chunk == CHUNKS - 1
    out_ref[...] = term_ref[...]

    @pl.when(jnp.logical_or(first, final))
    def _():
        shape = (ROWS, LANES)
        lane = lax.broadcasted_iota(jnp.int32, shape, 1)
        low = lane < LANES // 2
        own_side = jnp.logical_xor(low, final)
        at = jnp.where(first, 0, CHUNKS * CHUNK - 1)

        def joined_row(own, other):
            return pltpu.roll(jnp.where(own_side, own, other), LANES // 2, 1)

        opened = 1.0 - flag_ref[pl.ds(at, 1), :].astype(jnp.float32)
        wall = jnp.logical_and(jnp.logical_and(first, lax.axis_index("space") == 0), lane == 0)
        opened = jnp.where(wall, 0.0, jnp.broadcast_to(opened, shape))
        beyond = [jnp.broadcast_to(message_ref[pl.ds(COEFS + i, 1), :], shape) for i in range(2)]
        speed = joined_row(jnp.broadcast_to(speed_ref[pl.ds(at, 1), :], shape), beyond[0])
        coefs = derived([speed], [joined_row(opened, beyond[1])])
        starts = []
        for half in range(HALVES):
            packed = message_ref[pl.ds(half * ROWS, ROWS), :]
            start = []
            for k in range(MODES):
                own = jnp.where(first, window_ref[window_rows(half, 0, k), :], window_ref[window_rows(half, CHUNK - 1, k), :])
                start.append(joined_row(own, unpacked(packed, packed, k, low)))
            starts.append([start])
        finals = fine_steps(starts, coefs)
        near_end = jnp.logical_or(jnp.logical_and(first, lane < SHARE), jnp.logical_and(final, lane >= LANES - SHARE))
        for r, here in ((0, first), (CHUNK - 1, final)):

            @pl.when(here)
            def _(r=r):
                for half in range(HALVES):
                    for k in range(MODES):
                        rows = slab_rows(half, r, k)
                        made = pltpu.roll(finals[half][0][k], LANES // 2, 1) - coarse_ref[rows, :]
                        out_ref[rows, :] = jnp.where(near_end, by_place(half, made), term_ref[rows, :])


def write_kernel(sums_ref, out_ref, sems):
    size = CHUNK * MODES

    def write(pairs, count):
        copies = []
        for i, (source, target) in enumerate(pairs):
            source, target = pl.ds(source * size, count * size), pl.ds(target * size, count * size)
            copies.append(pltpu.make_async_copy(sums_ref.at[source], out_ref.at[target], sems.at[i]))
        for copy in copies:
            copy.start()
        for copy in copies:
            copy.wait()

    @pl.when(even_block())
    def _():
        write([(i, i) for i in range(0, CHUNKS, CHUNKS // COPIES)], CHUNKS // COPIES)

    @pl.when(jnp.logical_not(even_block()))
    def _():
        write([(i, CHUNKS - 1 - i) for i in range(CHUNKS)], 1)


def write_part(sums):
    return pl.pallas_call(
        write_kernel,
        out_shape=jax.ShapeDtypeStruct(sums.shape, jnp.float32),
        in_specs=[pl.BlockSpec(memory_space=pltpu.VMEM)],
        out_specs=pl.BlockSpec(memory_space=pl.ANY),
        scratch_shapes=[pltpu.SemaphoreType.DMA((CHUNKS,))],
        compiler_params=pltpu.CompilerParams(vmem_limit_bytes=16 * 1024 * 1024),
        name="write_out",
    )(sums)


def times(matrix, field):
    out = []
    for row in matrix:
        total = row[0] * field[0]
        for entry, value in zip(row[1:], field[1:]):
            total = total + entry * value
        out.append(total)
    return out


def square(matrix):
    columns = [times(matrix, [matrix[i][j] for i in range(MODES)]) for j in range(MODES)]
    return [[columns[j][i] for j in range(MODES)] for i in range(MODES)]


def added(xs, ys):
    return [x + y for x, y in zip(xs, ys)]


def chosen(test, xs, ys):
    return [jnp.where(test, x, y) for x, y in zip(xs, ys)]


def coarse_matrix(speed_ref, chunk):
    rows = [speed_ref[pl.ds(chunk * CHUNK + r, 1), :] for r in range(CHUNK)]
    speed = jnp.concatenate(rows * (ROWS // CHUNK), 0)
    speed2 = 2.0 * speed
    zero, one = jnp.zeros_like(speed), jnp.ones_like(speed)
    columns = [
        three_sections([one if i == j else zero for i in range(MODES)], lambda u: local_rhs(u, speed, speed2), STEPS * STEP)
        for j in range(MODES)
    ]
    return [[columns[j][i] for j in range(MODES)] for i in range(MODES)]


def term_rows(step, half, k):
    return pl.ds((step * QUAD * CHUNK + half * ROWS) * MODES + k, ROWS, stride=MODES)


def carry_rows(half, k):
    return pl.ds((k * HALVES + half) * ROWS, ROWS)


def quad_kernel(term_ref, speed_ref, carry_ref):
    quad, chunk = place()
    matrix = coarse_matrix(speed_ref, chunk)
    row = lax.broadcasted_iota(jnp.int32, (ROWS, LANES), 0)
    for half in range(HALVES):
        terms = [[term_ref[term_rows(step, half, k), :] for k in range(MODES)] for step in range(QUAD)]
        total = terms[0]
        for step in range(1, QUAD):
            total = added(times(matrix, total), terms[step])
        if half == HALVES - 1:
            total = chosen(jnp.logical_and(quad == QUAD - 1, row >= CHUNK), terms[-1], total)
        for k in range(MODES):
            carry_ref[carry_rows(half, k), :] = total[k]


def read_carry(ref, half):
    return [ref[carry_rows(half, k), :] for k in range(MODES)]


def joined(over_quad, quad, own, partner, half, row):
    odd = quad % 2 == 1
    earlier, later = chosen(odd, partner, own), chosen(odd, own, partner)
    both = added(times(over_quad, earlier), later)
    if half < HALVES - 1:
        return both
    return chosen(jnp.logical_and(quad >= 2, row >= CHUNK), later, both)


def pair_kernel(carry_ref, partner_ref, speed_ref, out_ref):
    quad, chunk = place()
    over_quad = square(square(coarse_matrix(speed_ref, chunk)))
    row = lax.broadcasted_iota(jnp.int32, (ROWS, LANES), 0)
    for half in range(HALVES):
        both = joined(over_quad, quad, read_carry(carry_ref, half), read_carry(partner_ref, half), half, row)
        for k in range(MODES):
            out_ref[carry_rows(half, k), :] = both[k]


def slab_kernel(term_ref, carry_ref, partner_ref, far_ref, speed_ref, out_ref):
    quad, chunk = place()
    matrix = coarse_matrix(speed_ref, chunk)
    over_quad = square(square(matrix))
    over_pair = square(over_quad)
    over_y = square(over_pair)
    row = lax.broadcasted_iota(jnp.int32, (ROWS, LANES), 0)
    low = row < CHUNK
    high_pair, odd = quad >= 2, quad % 2 == 1

    def swapped(xs):
        return [pltpu.roll(x, CHUNK, 0) for x in xs]

    here, total = [], []
    for half in range(HALVES):
        own, partner, far = (read_carry(ref, half) for ref in (carry_ref, partner_ref, far_ref))
        both = joined(over_quad, quad, own, partner, half, row)
        before_pair = [jnp.where(high_pair, x, 0.0) for x in far]
        here.append(chosen(odd, added(times(over_quad, before_pair), partner), before_pair))
        first_pair, second_pair = chosen(high_pair, far, both), chosen(high_pair, both, far)
        total.append(added(times(over_pair, first_pair), second_pair))
    first = swapped(second_pair)
    second = swapped(added(times(over_y, first), total[0]))
    pair = chosen(low, first, second)
    third = swapped(added(times(over_y, pair), total[0]))
    fourth = swapped(added(times(over_y, third), total[1]))
    starts = [pair, chosen(low, third, fourth)]
    for half in range(HALVES):
        state = starts[half]
        state = chosen(high_pair, times(over_pair, state), state)
        state = chosen(odd, times(over_quad, state), state)
        state = added(state, here[half])
        for step in range(QUAD):
            for i in range(HALVES):
                block = ORDER[step * QUAD + half * HALVES + i] * CHUNK * MODES
                for k in range(MODES):
                    out_ref[pl.ds(block + k, CHUNK, stride=MODES), :] = state[k][i * CHUNK : (i + 1) * CHUNK]
            if step < QUAD - 1:
                terms = [term_ref[term_rows(step, half, k), :] for k in range(MODES)]
                state = added(times(matrix, state), terms)


def on_device(kernel, name, rows, *operands):
    return pl.pallas_call(
        kernel,
        out_shape=jax.ShapeDtypeStruct((rows, LANES), jnp.float32),
        in_specs=[pl.BlockSpec(memory_space=pltpu.VMEM)] * len(operands),
        out_specs=pl.BlockSpec(memory_space=pltpu.VMEM),
        compiler_params=pltpu.CompilerParams(vmem_limit_bytes=16 * 1024 * 1024),
        name=name,
    )(*operands)


def swap_blocks(x, groups, rows=MODES):
    return lax.all_to_all(x.reshape(-1, rows, LANES), "tm", 0, 0, axis_index_groups=groups, tiled=True).reshape(x.shape)


def body(initial, guess, speeds, flags):
    slabs, blocks = lax.axis_size("tm"), lax.axis_size("space")
    count = initial.shape[1]
    rows = count // LANES

    def by_row(x):
        return x.reshape(MODES, rows, LANES).transpose(1, 0, 2).reshape(rows * MODES, LANES)

    speed_rows, flag_rows = speeds.reshape(rows, LANES), flags.reshape(rows, LANES)
    quads, ys = range(QUAD), range(slabs // QUAD**2)
    of_quad = [[y * QUAD**2 + q * QUAD + step for step in range(QUAD) for y in ys] for q in quads]
    listed = [[group[p] for p in LISTED] for group in of_quad]
    windows = swap_blocks(window_part(by_row(guess[0]), by_row(initial), slabs), listed, 2)
    pairs = []
    for group in of_quad:
        for slab, start in ((group[ORDER.index(CHUNKS - 1)], 0), (group[ORDER.index(0)], 1)):
            for i in range(start, blocks - 1, 2):
                ends = slab * blocks + i, slab * blocks + i + 1
                pairs += [ends, ends[::-1]]
    edge = on_device(edge_kernel, "edge_rows", COEFS + ROWS, windows, speed_rows, flag_rows)
    message = lax.ppermute(edge, ("tm", "space"), pairs)
    coarse = on_device(coarse_kernel, "coarse_steps", rows * MODES, windows, speed_rows)
    terms = on_device(fine_kernel, "fine_steps", rows * MODES, windows, coarse, speed_rows, flag_rows)
    terms = on_device(end_kernel, "block_ends", rows * MODES, terms, windows, coarse, message, speed_rows, flag_rows)
    size = MODES * HALVES * ROWS
    carry = on_device(quad_kernel, "quad_carry", size, terms, speed_rows)
    partner = lax.ppermute(carry, "tm", [(c, c ^ QUAD) for c in range(slabs)])
    joint = on_device(pair_kernel, "pair_carry", size, carry, partner, speed_rows)
    far = lax.ppermute(joint, "tm", [(c, c ^ (3 * QUAD)) for c in range(slabs)])
    sums = on_device(slab_kernel, "slab_sums", rows * MODES, terms, carry, partner, far, speed_rows)
    by_chunk = [[group[ORDER.index(i)] for i in range(CHUNKS)] for group in of_quad]
    sums = write_part(swap_blocks(sums, by_chunk)).reshape(rows, MODES, LANES)
    return sums.transpose(1, 0, 2).reshape(1, MODES, count)


def solution(mesh):
    return jax.shard_map(
        body,
        mesh=mesh,
        in_specs=(P(None, "space"), P("tm", None, "space"), P("space"), P("space")),
        out_specs=P("tm", None, "space"),
        check_vma=False,
    )
```

```python
import functools

import jax
import jax.numpy as jnp
from jax import lax
from jax.experimental import pallas as pl
from jax.experimental.pallas import tpu as pltpu
from jax.sharding import PartitionSpec as P

MODES = 4
STEPS = 8
LANES = 128
ROWS = 8
VISCOSITY = 0.02
PENALTY = 10.0
STEP = 0.015625
JACOBIAN = 8.0
INV_MASS = (0.5, 1.5, 2.5, 3.5)


def column_scales(delta):
    return [JACOBIAN * m * delta for m in INV_MASS]


def shifted(xs, step):
    rolled = [pltpu.roll(x, step % LANES, 1) for x in xs]
    if len(xs) == 1:
        return rolled
    lane = lax.broadcasted_iota(jnp.int32, xs[0].shape, 1)
    edge = lane == (0 if step == 1 else LANES - 1)
    return [jnp.where(edge, rolled[(v - step) % len(xs)], x) for v, x in enumerate(rolled)]


def volume_terms(u, speed2, p, q):
    a, b, c, d = u
    vq = (2.0 * VISCOSITY) * q
    m1 = speed2 * a - vq
    m2 = speed2 * b - (6.0 * VISCOSITY) * c
    m3 = speed2 * p - vq - (10.0 * VISCOSITY) * d
    return m1, m2, m3


def local_rhs(u, speed, speed2):
    a, b, c, d = u
    p, q = a + c, b + d
    out = -(speed * (p + q))
    m1, m2, m3 = volume_terms(u, speed2, p, q)
    return out, out + m1, out + m2, out + m3


def traces(u):
    a, b, c, d = u
    p, q = a + c, b + d
    odd, even = b + 6.0 * d, 3.0 * c
    return p + q, p - q, odd + even, odd - even


def full_step(start, now, scale, speed, speed2, inflow, gate, gate_after):
    tr, tl, sr, sl = zip(*(traces(u) for u in now))
    tr_b, sr_b, tl_a, sl_a = shifted(tr, 1), shifted(sr, 1), shifted(tl, -1), shifted(sl, -1)
    result = []
    for v, u in enumerate(now):
        jump = tr_b[v] - tl[v]
        k_l = gate[v] * jump
        g_l = inflow[v] * tr_b[v] - gate[v] * (sr_b[v] + sl[v] - (2.0 * PENALTY) * jump)
        jump = tr[v] - tl_a[v]
        k_r = gate_after[v] * jump
        base = gate_after[v] * (sr[v] + sl_a[v] - (2.0 * PENALTY) * jump) - speed[v] * tr[v]
        plus, minus = base + g_l, base - g_l
        k_sum, k_dif = k_r + k_l, k_r - k_l
        m1, m2, m3 = volume_terms(u, speed2[v], u[0] + u[2], u[1] + u[3])
        rhs = plus, minus + k_sum + m1, plus + 3.0 * k_dif + m2, minus + 6.0 * k_sum + m3
        result.append([x + f * r for x, f, r in zip(start[v], scale, rhs)])
    return result


def three_sections(u, rhs, delta):
    v = u
    for share in (3.0, 2.0, 1.0):
        scale = column_scales(delta / share)
        v = [x + f * r for x, f, r in zip(u, scale, rhs(v))]
    return v


QUAD = 4
CHUNK = 4
HALVES = 2
CHUNKS = 16
WINDOW = CHUNK * MODES + 2
SHARE = LANES // MODES
ORDER = (1, 2, 3, 4, 0, 15, 5, 6, 7, 8, 9, 10, 11, 12, 13, 14)
LISTED = (4, 5, 2, 3, 0, 1, 6, 7, 8, 9, 10, 11, 12, 13, 14, 15)
BACKWARDS = tuple(CHUNKS - 1 - chunk for chunk in ORDER)


def even_block():
    return lax.axis_index("space") % 2 == 0


def place():
    slab = lax.axis_index("tm")
    y, z = slab // (QUAD * QUAD), slab % (QUAD * QUAD)
    position = (z % QUAD) * QUAD + y
    chunk = position
    for i, there in enumerate(ORDER):
        if i != there:
            chunk = jnp.where(position == i, there, chunk)
    return z // QUAD, jnp.where(even_block(), chunk, CHUNKS - 1 - chunk)


COPIES = 4


def window_kernel(slabs, guess_ref, initial_ref, out_ref, state, sems):
    last = lax.axis_index("tm") == slabs - 1
    rows = state.shape[0] // COPIES

    def copies(source):
        parts = [pl.ds(i * rows, rows) for i in range(COPIES)]
        return [pltpu.make_async_copy(source.at[part], state.at[part], sems.at[i]) for i, part in enumerate(parts)]

    @pl.when(last)
    def _():
        for copy in copies(initial_ref):
            copy.start()

    @pl.when(jnp.logical_not(last))
    def _():
        for copy in copies(guess_ref):
            copy.start()

    for copy in copies(guess_ref):
        copy.wait()
    size = CHUNK * MODES
    group = lax.broadcasted_iota(jnp.int32, (ROWS, LANES), 1) // SHARE

    def packed(row, shift):
        vectors = []
        for i in range(CHUNKS // ROWS):
            total = jnp.zeros((ROWS, LANES), jnp.float32)
            for k in range(MODES):
                read = state[pl.ds(i * ROWS * size + row * MODES + k, ROWS, stride=size), :]
                total = jnp.where(group == k, pltpu.roll(read, (k * SHARE + shift) % LANES, 1), total)
            vectors.append(total)
        return [vectors[n // ROWS][n % ROWS : n % ROWS + 1] for n in range(CHUNKS)]

    heads, tails = packed(0, 0), packed(CHUNK - 1, SHARE)
    none = jnp.zeros((1, LANES), jnp.float32)

    def write(chunks):
        for position, place_there in enumerate(LISTED):
            at, chunk = position * WINDOW, chunks[place_there]
            out_ref[pl.ds(at, size), :] = state[pl.ds(chunk * size, size), :]
            out_ref[pl.ds(at + size, 1), :] = heads[chunk + 1] if chunk < CHUNKS - 1 else none
            out_ref[pl.ds(at + size + 1, 1), :] = tails[chunk - 1] if chunk else none

    @pl.when(even_block())
    def _():
        write(ORDER)

    @pl.when(jnp.logical_not(even_block()))
    def _():
        write(BACKWARDS)


def window_part(guess, initial, slabs):
    return pl.pallas_call(
        functools.partial(window_kernel, slabs),
        out_shape=jax.ShapeDtypeStruct((CHUNKS * WINDOW, LANES), jnp.float32),
        in_specs=[pl.BlockSpec(memory_space=pltpu.HBM)] * 2,
        out_specs=pl.BlockSpec(memory_space=pltpu.VMEM),
        scratch_shapes=[pltpu.VMEM(guess.shape, jnp.float32), pltpu.SemaphoreType.DMA((COPIES,))],
        compiler_params=pltpu.CompilerParams(vmem_limit_bytes=16 * 1024 * 1024),
        name="windows",
    )(*(pltpu.with_memory_space_constraint(x, pltpu.HBM) for x in (guess, initial)))


def window_rows(half, r, k):
    return pl.ds(half * ROWS * WINDOW + r * MODES + k, ROWS, stride=WINDOW)


def unpacked(after, before, k, low):
    return jnp.where(low, pltpu.roll(after, -k * SHARE % LANES, 1), pltpu.roll(before, (MODES - 1 - k) * SHARE, 1))


COEFS = HALVES * ROWS


def edge_kernel(window_ref, speed_ref, flag_ref, out_ref):
    _, chunk = place()
    tail = chunk == CHUNKS - 1
    rows = speed_ref.shape[0]
    group = lax.broadcasted_iota(jnp.int32, (ROWS, LANES), 1) // SHARE
    for half in range(HALVES):
        packed = jnp.zeros((ROWS, LANES), jnp.float32)
        for k in range(MODES):
            first, final = window_ref[window_rows(half, 0, k), :], window_ref[window_rows(half, CHUNK - 1, k), :]
            moved = jnp.where(tail, pltpu.roll(final, (k + 1) * SHARE % LANES, 1), pltpu.roll(first, k * SHARE, 1))
            packed = jnp.where(group == k, moved, packed)
        out_ref[pl.ds(half * ROWS, ROWS), :] = packed
    at = jnp.where(tail, rows - 1, 0)
    out_ref[pl.ds(COEFS, 1), :] = speed_ref[pl.ds(at, 1), :]
    out_ref[pl.ds(COEFS + 1, 1), :] = 1.0 - flag_ref[pl.ds(at, 1), :].astype(jnp.float32)
    out_ref[pl.ds(COEFS + 2, ROWS - 2), :] = jnp.zeros((ROWS - 2, LANES), jnp.float32)


def coarse_step(start, speed, half, quad):
    speed2 = 2.0 * speed
    coarse = three_sections(start, lambda u: local_rhs(u, speed, speed2), STEPS * STEP)
    if half < HALVES - 1:
        return coarse
    last = jnp.logical_and(quad == QUAD - 1, lax.broadcasted_iota(jnp.int32, speed.shape, 0) == ROWS - 1)
    return [jnp.where(last, 0.0, x) for x in coarse]


def by_place(half, x):
    row = lax.broadcasted_iota(jnp.int32, x.shape, 0)
    return jnp.where(row % QUAD < QUAD // 2, pltpu.roll(x, QUAD, 0), x) if half == 0 else x


def slab_rows(half, r, k):
    return pl.ds((half * ROWS * CHUNK + r) * MODES + k, ROWS, stride=CHUNK * MODES)


def derived(speed, opened):
    gate = [(0.5 * VISCOSITY) * x for x in opened]
    inflow = [x * y for x, y in zip(opened, shifted(speed, 1))]
    return speed, [2.0 * x for x in speed], inflow, gate, shifted(gate, -1)


def fine_steps(starts, coefs):
    def advance(_, us):
        nows = us
        for share in (3.0, 2.0, 1.0):
            scale = column_scales(STEP / share)
            nows = [full_step(u, now, scale, *coefs) for u, now in zip(us, nows)]
        return nows

    return lax.fori_loop(0, STEPS, advance, starts, unroll=True)


def fine_kernel(window_ref, speed_ref, flag_ref, out_ref):
    quad, chunk = place()
    first, final = chunk == 0, chunk == CHUNKS - 1
    shape = (ROWS, LANES)
    lane = lax.broadcasted_iota(jnp.int32, shape, 1)
    low = lane < LANES // 2
    outside = jnp.logical_or(jnp.logical_and(low, final), jnp.logical_and(lane >= LANES // 2, first))

    def coef(read):
        at = chunk * CHUNK
        own = [jnp.broadcast_to(read(at + r), shape) for r in range(CHUNK)]
        after = jnp.broadcast_to(read(jnp.minimum(at + CHUNK, CHUNKS * CHUNK - 1)), shape)
        before = jnp.broadcast_to(read(jnp.maximum(at - 1, 0)), shape)
        return [*own, jnp.where(outside, 0.0, jnp.where(low, after, before))]

    speed = coef(lambda i: speed_ref[pl.ds(i, 1), :])
    opened = coef(lambda i: 1.0 - flag_ref[pl.ds(i, 1), :].astype(jnp.float32))
    wall = jnp.logical_and(jnp.logical_and(first, lax.axis_index("space") == 0), lane == 0)
    opened[0] = jnp.where(wall, 0.0, opened[0])
    coefs = derived(speed, opened)
    starts = []
    for half in range(HALVES):
        start = [[window_ref[window_rows(half, r, k), :] for k in range(MODES)] for r in range(CHUNK)]
        after, before = (window_ref[window_rows(half, CHUNK, i), :] for i in range(2))
        start.append([jnp.where(outside, 0.0, unpacked(after, before, k, low)) for k in range(MODES)])
        starts.append(start)
    finals = fine_steps(starts, coefs)
    for half in range(HALVES):
        for r in range(CHUNK):
            coarse = coarse_step(starts[half][r], speed[r], half, quad)
            for k in range(MODES):
                out_ref[slab_rows(half, r, k), :] = by_place(half, finals[half][r][k] - coarse[k])


def end_kernel(term_ref, window_ref, message_ref, speed_ref, flag_ref, out_ref):
    quad, chunk = place()
    first, final = chunk == 0, chunk == CHUNKS - 1
    out_ref[...] = term_ref[...]

    @pl.when(jnp.logical_or(first, final))
    def _():
        shape = (ROWS, LANES)
        lane = lax.broadcasted_iota(jnp.int32, shape, 1)
        low = lane < LANES // 2
        own_side = jnp.logical_xor(low, final)
        at = jnp.where(first, 0, CHUNKS * CHUNK - 1)

        def joined_row(own, other):
            return pltpu.roll(jnp.where(own_side, own, other), LANES // 2, 1)

        opened = 1.0 - flag_ref[pl.ds(at, 1), :].astype(jnp.float32)
        wall = jnp.logical_and(jnp.logical_and(first, lax.axis_index("space") == 0), lane == 0)
        opened = jnp.where(wall, 0.0, jnp.broadcast_to(opened, shape))
        beyond = [jnp.broadcast_to(message_ref[pl.ds(COEFS + i, 1), :], shape) for i in range(2)]
        own_speed = jnp.broadcast_to(speed_ref[pl.ds(at, 1), :], shape)
        coefs = derived([joined_row(own_speed, beyond[0])], [joined_row(opened, beyond[1])])
        starts, coarse = [], []
        for half in range(HALVES):
            packed = message_ref[pl.ds(half * ROWS, ROWS), :]
            start, owns = [], []
            for k in range(MODES):
                own = jnp.where(first, window_ref[window_rows(half, 0, k), :], window_ref[window_rows(half, CHUNK - 1, k), :])
                owns.append(own)
                start.append(joined_row(own, unpacked(packed, packed, k, low)))
            starts.append([start])
            coarse.append(coarse_step(owns, own_speed, half, quad))
        finals = fine_steps(starts, coefs)
        near_end = jnp.logical_or(jnp.logical_and(first, lane < SHARE), jnp.logical_and(final, lane >= LANES - SHARE))
        for r, here in ((0, first), (CHUNK - 1, final)):

            @pl.when(here)
            def _(r=r):
                for half in range(HALVES):
                    for k in range(MODES):
                        rows = slab_rows(half, r, k)
                        made = pltpu.roll(finals[half][0][k], LANES // 2, 1) - coarse[half][k]
                        out_ref[rows, :] = jnp.where(near_end, by_place(half, made), term_ref[rows, :])


def write_kernel(sums_ref, out_ref, sems):
    size = CHUNK * MODES

    def write(pairs, count):
        copies = []
        for i, (source, target) in enumerate(pairs):
            source, target = pl.ds(source * size, count * size), pl.ds(target * size, count * size)
            copies.append(pltpu.make_async_copy(sums_ref.at[source], out_ref.at[target], sems.at[i]))
        for copy in copies:
            copy.start()
        for copy in copies:
            copy.wait()

    @pl.when(even_block())
    def _():
        write([(i, i) for i in range(0, CHUNKS, CHUNKS // COPIES)], CHUNKS // COPIES)

    @pl.when(jnp.logical_not(even_block()))
    def _():
        write([(i, CHUNKS - 1 - i) for i in range(CHUNKS)], 1)


def write_part(sums):
    return pl.pallas_call(
        write_kernel,
        out_shape=jax.ShapeDtypeStruct(sums.shape, jnp.float32),
        in_specs=[pl.BlockSpec(memory_space=pltpu.VMEM)],
        out_specs=pl.BlockSpec(memory_space=pl.ANY),
        scratch_shapes=[pltpu.SemaphoreType.DMA((CHUNKS,))],
        compiler_params=pltpu.CompilerParams(vmem_limit_bytes=16 * 1024 * 1024),
        name="write_out",
    )(sums)


def times(matrix, field):
    out = []
    for row in matrix:
        total = row[0] * field[0]
        for entry, value in zip(row[1:], field[1:]):
            total = total + entry * value
        out.append(total)
    return out


def square(matrix):
    columns = [times(matrix, [matrix[i][j] for i in range(MODES)]) for j in range(MODES)]
    return [[columns[j][i] for j in range(MODES)] for i in range(MODES)]


def added(xs, ys):
    return [x + y for x, y in zip(xs, ys)]


def chosen(test, xs, ys):
    return [jnp.where(test, x, y) for x, y in zip(xs, ys)]


def coarse_matrix(speed_ref, chunk):
    rows = [speed_ref[pl.ds(chunk * CHUNK + r, 1), :] for r in range(CHUNK)]
    speed = jnp.concatenate(rows * (ROWS // CHUNK), 0)
    speed2 = 2.0 * speed
    zero, one = jnp.zeros_like(speed), jnp.ones_like(speed)
    columns = [
        three_sections([one if i == j else zero for i in range(MODES)], lambda u: local_rhs(u, speed, speed2), STEPS * STEP)
        for j in range(MODES)
    ]
    return [[columns[j][i] for j in range(MODES)] for i in range(MODES)]


def term_rows(step, half, k):
    return pl.ds((step * QUAD * CHUNK + half * ROWS) * MODES + k, ROWS, stride=MODES)


def carry_rows(half, k):
    return pl.ds((k * HALVES + half) * ROWS, ROWS)


def quad_kernel(term_ref, speed_ref, carry_ref):
    quad, chunk = place()
    matrix = coarse_matrix(speed_ref, chunk)
    row = lax.broadcasted_iota(jnp.int32, (ROWS, LANES), 0)
    for half in range(HALVES):
        terms = [[term_ref[term_rows(step, half, k), :] for k in range(MODES)] for step in range(QUAD)]
        total = terms[0]
        for step in range(1, QUAD):
            total = added(times(matrix, total), terms[step])
        if half == HALVES - 1:
            total = chosen(jnp.logical_and(quad == QUAD - 1, row >= CHUNK), terms[-1], total)
        for k in range(MODES):
            carry_ref[carry_rows(half, k), :] = total[k]


def read_carry(ref, half):
    return [ref[carry_rows(half, k), :] for k in range(MODES)]


def joined(over_quad, quad, own, partner, half, row):
    odd = quad % 2 == 1
    earlier, later = chosen(odd, partner, own), chosen(odd, own, partner)
    both = added(times(over_quad, earlier), later)
    if half < HALVES - 1:
        return both
    return chosen(jnp.logical_and(quad >= 2, row >= CHUNK), later, both)


def pair_kernel(carry_ref, partner_ref, speed_ref, out_ref):
    quad, chunk = place()
    over_quad = square(square(coarse_matrix(speed_ref, chunk)))
    row = lax.broadcasted_iota(jnp.int32, (ROWS, LANES), 0)
    for half in range(HALVES):
        both = joined(over_quad, quad, read_carry(carry_ref, half), read_carry(partner_ref, half), half, row)
        for k in range(MODES):
            out_ref[carry_rows(half, k), :] = both[k]


def slab_kernel(term_ref, carry_ref, partner_ref, far_ref, speed_ref, out_ref):
    quad, chunk = place()
    matrix = coarse_matrix(speed_ref, chunk)
    over_quad = square(square(matrix))
    over_pair = square(over_quad)
    over_y = square(over_pair)
    row = lax.broadcasted_iota(jnp.int32, (ROWS, LANES), 0)
    low = row < CHUNK
    high_pair, odd = quad >= 2, quad % 2 == 1

    def swapped(xs):
        return [pltpu.roll(x, CHUNK, 0) for x in xs]

    here, total = [], []
    for half in range(HALVES):
        own, partner, far = (read_carry(ref, half) for ref in (carry_ref, partner_ref, far_ref))
        both = joined(over_quad, quad, own, partner, half, row)
        before_pair = [jnp.where(high_pair, x, 0.0) for x in far]
        here.append(chosen(odd, added(times(over_quad, before_pair), partner), before_pair))
        first_pair, second_pair = chosen(high_pair, far, both), chosen(high_pair, both, far)
        total.append(added(times(over_pair, first_pair), second_pair))
    first = swapped(second_pair)
    second = swapped(added(times(over_y, first), total[0]))
    pair = chosen(low, first, second)
    third = swapped(added(times(over_y, pair), total[0]))
    fourth = swapped(added(times(over_y, third), total[1]))
    starts = [pair, chosen(low, third, fourth)]
    for half in range(HALVES):
        state = starts[half]
        state = chosen(high_pair, times(over_pair, state), state)
        state = chosen(odd, times(over_quad, state), state)
        state = added(state, here[half])
        for step in range(QUAD):
            for i in range(HALVES):
                block = ORDER[step * QUAD + half * HALVES + i] * CHUNK * MODES
                for k in range(MODES):
                    out_ref[pl.ds(block + k, CHUNK, stride=MODES), :] = state[k][i * CHUNK : (i + 1) * CHUNK]
            if step < QUAD - 1:
                terms = [term_ref[term_rows(step, half, k), :] for k in range(MODES)]
                state = added(times(matrix, state), terms)


def on_device(kernel, name, rows, *operands):
    return pl.pallas_call(
        kernel,
        out_shape=jax.ShapeDtypeStruct((rows, LANES), jnp.float32),
        in_specs=[pl.BlockSpec(memory_space=pltpu.VMEM)] * len(operands),
        out_specs=pl.BlockSpec(memory_space=pltpu.VMEM),
        compiler_params=pltpu.CompilerParams(vmem_limit_bytes=16 * 1024 * 1024),
        name=name,
    )(*operands)


def swap_blocks(x, groups, rows=MODES):
    return lax.all_to_all(x.reshape(-1, rows, LANES), "tm", 0, 0, axis_index_groups=groups, tiled=True).reshape(x.shape)


def body(initial, guess, speeds, flags):
    slabs, blocks = lax.axis_size("tm"), lax.axis_size("space")
    count = initial.shape[1]
    rows = count // LANES

    def by_row(x):
        return x.reshape(MODES, rows, LANES).transpose(1, 0, 2).reshape(rows * MODES, LANES)

    speed_rows, flag_rows = speeds.reshape(rows, LANES), flags.reshape(rows, LANES)
    quads, ys = range(QUAD), range(slabs // QUAD**2)
    of_quad = [[y * QUAD**2 + q * QUAD + step for step in range(QUAD) for y in ys] for q in quads]
    listed = [[group[p] for p in LISTED] for group in of_quad]
    windows = swap_blocks(window_part(by_row(guess[0]), by_row(initial), slabs), listed, 2)
    pairs = []
    for group in of_quad:
        for slab, start in ((group[ORDER.index(CHUNKS - 1)], 0), (group[ORDER.index(0)], 1)):
            for i in range(start, blocks - 1, 2):
                ends = slab * blocks + i, slab * blocks + i + 1
                pairs += [ends, ends[::-1]]
    edge = on_device(edge_kernel, "edge_rows", COEFS + ROWS, windows, speed_rows, flag_rows)
    message = lax.ppermute(edge, ("tm", "space"), pairs)
    terms = on_device(fine_kernel, "fine_steps", rows * MODES, windows, speed_rows, flag_rows)
    terms = on_device(end_kernel, "block_ends", rows * MODES, terms, windows, message, speed_rows, flag_rows)
    size = MODES * HALVES * ROWS
    carry = on_device(quad_kernel, "quad_carry", size, terms, speed_rows)
    partner = lax.ppermute(carry, "tm", [(c, c ^ QUAD) for c in range(slabs)])
    joint = on_device(pair_kernel, "pair_carry", size, carry, partner, speed_rows)
    far = lax.ppermute(joint, "tm", [(c, c ^ (3 * QUAD)) for c in range(slabs)])
    sums = on_device(slab_kernel, "slab_sums", rows * MODES, terms, carry, partner, far, speed_rows)
    by_chunk = [[group[ORDER.index(i)] for i in range(CHUNKS)] for group in of_quad]
    sums = write_part(swap_blocks(sums, by_chunk)).reshape(rows, MODES, LANES)
    return sums.transpose(1, 0, 2).reshape(1, MODES, count)


def solution(mesh):
    return jax.shard_map(
        body,
        mesh=mesh,
        in_specs=(P(None, "space"), P("tm", None, "space"), P("space"), P("space")),
        out_specs=P("tm", None, "space"),
        check_vma=False,
    )
```

```python
import functools

import jax
import jax.numpy as jnp
from jax import lax
from jax.experimental import pallas as pl
from jax.experimental.pallas import tpu as pltpu
from jax.sharding import PartitionSpec as P

MODES = 4
STEPS = 8
LANES = 128
ROWS = 8
VISCOSITY = 0.02
PENALTY = 10.0
STEP = 0.015625
JACOBIAN = 8.0
INV_MASS = (0.5, 1.5, 2.5, 3.5)


def column_scales(delta):
    return [JACOBIAN * m * delta for m in INV_MASS]


def shifted(xs, step):
    rolled = [pltpu.roll(x, step % LANES, 1) for x in xs]
    if len(xs) == 1:
        return rolled
    lane = lax.broadcasted_iota(jnp.int32, xs[0].shape, 1)
    edge = lane == (0 if step == 1 else LANES - 1)
    return [jnp.where(edge, rolled[(v - step) % len(xs)], x) for v, x in enumerate(rolled)]


def volume_terms(u, speed2, p, q):
    a, b, c, d = u
    vq = (2.0 * VISCOSITY) * q
    m1 = speed2 * a - vq
    m2 = speed2 * b - (6.0 * VISCOSITY) * c
    m3 = speed2 * p - vq - (10.0 * VISCOSITY) * d
    return m1, m2, m3


def local_rhs(u, speed, speed2):
    a, b, c, d = u
    p, q = a + c, b + d
    out = -(speed * (p + q))
    m1, m2, m3 = volume_terms(u, speed2, p, q)
    return out, out + m1, out + m2, out + m3


def traces(u):
    a, b, c, d = u
    p, q = a + c, b + d
    odd, even = b + 6.0 * d, 3.0 * c
    return p + q, p - q, odd + even, odd - even


def full_step(start, now, scale, speed, speed2, inflow, gate, gate_after):
    tr, tl, sr, sl = zip(*(traces(u) for u in now))
    tr_b, sr_b, tl_a, sl_a = shifted(tr, 1), shifted(sr, 1), shifted(tl, -1), shifted(sl, -1)
    result = []
    for v, u in enumerate(now):
        jump = tr_b[v] - tl[v]
        k_l = gate[v] * jump
        g_l = inflow[v] * tr_b[v] - gate[v] * (sr_b[v] + sl[v] - (2.0 * PENALTY) * jump)
        jump = tr[v] - tl_a[v]
        k_r = gate_after[v] * jump
        base = gate_after[v] * (sr[v] + sl_a[v] - (2.0 * PENALTY) * jump) - speed[v] * tr[v]
        plus, minus = base + g_l, base - g_l
        k_sum, k_dif = k_r + k_l, k_r - k_l
        m1, m2, m3 = volume_terms(u, speed2[v], u[0] + u[2], u[1] + u[3])
        rhs = plus, minus + k_sum + m1, plus + 3.0 * k_dif + m2, minus + 6.0 * k_sum + m3
        result.append([x + f * r for x, f, r in zip(start[v], scale, rhs)])
    return result


def three_sections(u, rhs, delta):
    v = u
    for share in (3.0, 2.0, 1.0):
        scale = column_scales(delta / share)
        v = [x + f * r for x, f, r in zip(u, scale, rhs(v))]
    return v


QUAD = 4
CHUNK = 4
HALVES = 2
CHUNKS = 16
WINDOW = CHUNK * MODES + 2
SHARE = LANES // MODES
ORDER = (1, 2, 3, 4, 0, 15, 5, 6, 7, 8, 9, 10, 11, 12, 13, 14)
LISTED = (4, 5, 2, 3, 0, 1, 6, 7, 8, 9, 10, 11, 12, 13, 14, 15)
BACKWARDS = tuple(CHUNKS - 1 - chunk for chunk in ORDER)


def even_block():
    return lax.axis_index("space") % 2 == 0


def place():
    slab = lax.axis_index("tm")
    y, z = slab // (QUAD * QUAD), slab % (QUAD * QUAD)
    position = (z % QUAD) * QUAD + y
    chunk = position
    for i, there in enumerate(ORDER):
        if i != there:
            chunk = jnp.where(position == i, there, chunk)
    return z // QUAD, jnp.where(even_block(), chunk, CHUNKS - 1 - chunk)


COPIES = 4


def window_kernel(slabs, guess_ref, initial_ref, out_ref, state, sems):
    last = lax.axis_index("tm") == slabs - 1
    rows = state.shape[0] // COPIES

    def copies(source):
        parts = [pl.ds(i * rows, rows) for i in range(COPIES)]
        return [pltpu.make_async_copy(source.at[part], state.at[part], sems.at[i]) for i, part in enumerate(parts)]

    @pl.when(last)
    def _():
        for copy in copies(initial_ref):
            copy.start()

    @pl.when(jnp.logical_not(last))
    def _():
        for copy in copies(guess_ref):
            copy.start()

    for copy in copies(guess_ref):
        copy.wait()
    size = CHUNK * MODES
    group = lax.broadcasted_iota(jnp.int32, (ROWS, LANES), 1) // SHARE

    def packed(row, shift):
        vectors = []
        for i in range(CHUNKS // ROWS):
            total = jnp.zeros((ROWS, LANES), jnp.float32)
            for k in range(MODES):
                read = state[pl.ds(i * ROWS * size + row * MODES + k, ROWS, stride=size), :]
                total = jnp.where(group == k, pltpu.roll(read, (k * SHARE + shift) % LANES, 1), total)
            vectors.append(total)
        return [vectors[n // ROWS][n % ROWS : n % ROWS + 1] for n in range(CHUNKS)]

    heads, tails = packed(0, 0), packed(CHUNK - 1, SHARE)
    none = jnp.zeros((1, LANES), jnp.float32)

    def write(chunks):
        for position, place_there in enumerate(LISTED):
            at, chunk = position * WINDOW, chunks[place_there]
            out_ref[pl.ds(at, size), :] = state[pl.ds(chunk * size, size), :]
            out_ref[pl.ds(at + size, 1), :] = heads[chunk + 1] if chunk < CHUNKS - 1 else none
            out_ref[pl.ds(at + size + 1, 1), :] = tails[chunk - 1] if chunk else none

    @pl.when(even_block())
    def _():
        write(ORDER)

    @pl.when(jnp.logical_not(even_block()))
    def _():
        write(BACKWARDS)


def window_part(guess, initial, slabs):
    return pl.pallas_call(
        functools.partial(window_kernel, slabs),
        out_shape=jax.ShapeDtypeStruct((CHUNKS * WINDOW, LANES), jnp.float32),
        in_specs=[pl.BlockSpec(memory_space=pltpu.HBM)] * 2,
        out_specs=pl.BlockSpec(memory_space=pltpu.VMEM),
        scratch_shapes=[pltpu.VMEM(guess.shape, jnp.float32), pltpu.SemaphoreType.DMA((COPIES,))],
        compiler_params=pltpu.CompilerParams(vmem_limit_bytes=16 * 1024 * 1024),
        name="windows",
    )(*(pltpu.with_memory_space_constraint(x, pltpu.HBM) for x in (guess, initial)))


def window_rows(half, r, k):
    return pl.ds(half * ROWS * WINDOW + r * MODES + k, ROWS, stride=WINDOW)


def unpacked(after, before, k, low):
    return jnp.where(low, pltpu.roll(after, -k * SHARE % LANES, 1), pltpu.roll(before, (MODES - 1 - k) * SHARE, 1))


COEFS = HALVES * ROWS


def edge_kernel(window_ref, speed_ref, flag_ref, out_ref):
    _, chunk = place()
    tail = chunk == CHUNKS - 1
    rows = speed_ref.shape[0]
    group = lax.broadcasted_iota(jnp.int32, (ROWS, LANES), 1) // SHARE
    for half in range(HALVES):
        packed = jnp.zeros((ROWS, LANES), jnp.float32)
        for k in range(MODES):
            first, final = window_ref[window_rows(half, 0, k), :], window_ref[window_rows(half, CHUNK - 1, k), :]
            moved = jnp.where(tail, pltpu.roll(final, (k + 1) * SHARE % LANES, 1), pltpu.roll(first, k * SHARE, 1))
            packed = jnp.where(group == k, moved, packed)
        out_ref[pl.ds(half * ROWS, ROWS), :] = packed
    at = jnp.where(tail, rows - 1, 0)
    out_ref[pl.ds(COEFS, 1), :] = speed_ref[pl.ds(at, 1), :]
    out_ref[pl.ds(COEFS + 1, 1), :] = 1.0 - flag_ref[pl.ds(at, 1), :].astype(jnp.float32)
    out_ref[pl.ds(COEFS + 2, ROWS - 2), :] = jnp.zeros((ROWS - 2, LANES), jnp.float32)


def coarse_step(start, speed, half, quad):
    speed2 = 2.0 * speed
    coarse = three_sections(start, lambda u: local_rhs(u, speed, speed2), STEPS * STEP)
    if half < HALVES - 1:
        return coarse
    last = jnp.logical_and(quad == QUAD - 1, lax.broadcasted_iota(jnp.int32, speed.shape, 0) == ROWS - 1)
    return [jnp.where(last, 0.0, x) for x in coarse]


def by_place(half, x):
    row = lax.broadcasted_iota(jnp.int32, x.shape, 0)
    return jnp.where(row % QUAD < QUAD // 2, pltpu.roll(x, QUAD, 0), x) if half == 0 else x


def slab_rows(half, r, k):
    return pl.ds((half * ROWS * CHUNK + r) * MODES + k, ROWS, stride=CHUNK * MODES)


def derived(speed, opened):
    gate = [(0.5 * VISCOSITY) * x for x in opened]
    inflow = [x * y for x, y in zip(opened, shifted(speed, 1))]
    return speed, [2.0 * x for x in speed], inflow, gate, shifted(gate, -1)


def fine_steps(starts, coefs):
    def advance(_, us):
        nows = us
        for share in (3.0, 2.0, 1.0):
            scale = column_scales(STEP / share)
            nows = [full_step(u, now, scale, *coefs) for u, now in zip(us, nows)]
        return nows

    return lax.fori_loop(0, STEPS, advance, starts, unroll=True)


def fine_kernel(window_ref, speed_ref, flag_ref, out_ref):
    quad, chunk = place()
    first, final = chunk == 0, chunk == CHUNKS - 1
    shape = (ROWS, LANES)
    lane = lax.broadcasted_iota(jnp.int32, shape, 1)
    low = lane < LANES // 2
    outside = jnp.logical_or(jnp.logical_and(low, final), jnp.logical_and(lane >= LANES // 2, first))

    def coef(read):
        at = chunk * CHUNK
        own = [jnp.broadcast_to(read(at + r), shape) for r in range(CHUNK)]
        after = jnp.broadcast_to(read(jnp.minimum(at + CHUNK, CHUNKS * CHUNK - 1)), shape)
        before = jnp.broadcast_to(read(jnp.maximum(at - 1, 0)), shape)
        return [*own, jnp.where(outside, 0.0, jnp.where(low, after, before))]

    speed = coef(lambda i: speed_ref[pl.ds(i, 1), :])
    opened = coef(lambda i: 1.0 - flag_ref[pl.ds(i, 1), :].astype(jnp.float32))
    wall = jnp.logical_and(jnp.logical_and(first, lax.axis_index("space") == 0), lane == 0)
    opened[0] = jnp.where(wall, 0.0, opened[0])
    coefs = derived(speed, opened)
    starts = []
    for half in range(HALVES):
        start = [[window_ref[window_rows(half, r, k), :] for k in range(MODES)] for r in range(CHUNK)]
        after, before = (window_ref[window_rows(half, CHUNK, i), :] for i in range(2))
        start.append([jnp.where(outside, 0.0, unpacked(after, before, k, low)) for k in range(MODES)])
        starts.append(start)
    finals = fine_steps(starts, coefs)
    for half in range(HALVES):
        for r in range(CHUNK):
            coarse = coarse_step(starts[half][r], speed[r], half, quad)
            for k in range(MODES):
                out_ref[slab_rows(half, r, k), :] = by_place(half, finals[half][r][k] - coarse[k])


def end_kernel(term_ref, window_ref, message_ref, speed_ref, flag_ref, out_ref, carry_ref):
    quad, chunk = place()
    first, final = chunk == 0, chunk == CHUNKS - 1
    out_ref[...] = term_ref[...]

    @pl.when(jnp.logical_or(first, final))
    def _():
        shape = (ROWS, LANES)
        lane = lax.broadcasted_iota(jnp.int32, shape, 1)
        low = lane < LANES // 2
        own_side = jnp.logical_xor(low, final)
        at = jnp.where(first, 0, CHUNKS * CHUNK - 1)

        def joined_row(own, other):
            return pltpu.roll(jnp.where(own_side, own, other), LANES // 2, 1)

        opened = 1.0 - flag_ref[pl.ds(at, 1), :].astype(jnp.float32)
        wall = jnp.logical_and(jnp.logical_and(first, lax.axis_index("space") == 0), lane == 0)
        opened = jnp.where(wall, 0.0, jnp.broadcast_to(opened, shape))
        beyond = [jnp.broadcast_to(message_ref[pl.ds(COEFS + i, 1), :], shape) for i in range(2)]
        own_speed = jnp.broadcast_to(speed_ref[pl.ds(at, 1), :], shape)
        coefs = derived([joined_row(own_speed, beyond[0])], [joined_row(opened, beyond[1])])
        starts, coarse = [], []
        for half in range(HALVES):
            packed = message_ref[pl.ds(half * ROWS, ROWS), :]
            start, owns = [], []
            for k in range(MODES):
                own = jnp.where(first, window_ref[window_rows(half, 0, k), :], window_ref[window_rows(half, CHUNK - 1, k), :])
                owns.append(own)
                start.append(joined_row(own, unpacked(packed, packed, k, low)))
            starts.append([start])
            coarse.append(coarse_step(owns, own_speed, half, quad))
        finals = fine_steps(starts, coefs)
        near_end = jnp.logical_or(jnp.logical_and(first, lane < SHARE), jnp.logical_and(final, lane >= LANES - SHARE))
        for r, here in ((0, first), (CHUNK - 1, final)):

            @pl.when(here)
            def _(r=r):
                for half in range(HALVES):
                    for k in range(MODES):
                        rows = slab_rows(half, r, k)
                        made = pltpu.roll(finals[half][0][k], LANES // 2, 1) - coarse[half][k]
                        out_ref[rows, :] = jnp.where(near_end, by_place(half, made), term_ref[rows, :])

    quad_carry(out_ref, speed_ref, carry_ref)


def write_kernel(sums_ref, out_ref, sems):
    size = CHUNK * MODES

    def write(pairs, count):
        copies = []
        for i, (source, target) in enumerate(pairs):
            source, target = pl.ds(source * size, count * size), pl.ds(target * size, count * size)
            copies.append(pltpu.make_async_copy(sums_ref.at[source], out_ref.at[target], sems.at[i]))
        for copy in copies:
            copy.start()
        for copy in copies:
            copy.wait()

    @pl.when(even_block())
    def _():
        write([(i, i) for i in range(0, CHUNKS, CHUNKS // COPIES)], CHUNKS // COPIES)

    @pl.when(jnp.logical_not(even_block()))
    def _():
        write([(i, CHUNKS - 1 - i) for i in range(CHUNKS)], 1)


def write_part(sums):
    return pl.pallas_call(
        write_kernel,
        out_shape=jax.ShapeDtypeStruct(sums.shape, jnp.float32),
        in_specs=[pl.BlockSpec(memory_space=pltpu.VMEM)],
        out_specs=pl.BlockSpec(memory_space=pl.ANY),
        scratch_shapes=[pltpu.SemaphoreType.DMA((CHUNKS,))],
        compiler_params=pltpu.CompilerParams(vmem_limit_bytes=16 * 1024 * 1024),
        name="write_out",
    )(sums)


def times(matrix, field):
    out = []
    for row in matrix:
        total = row[0] * field[0]
        for entry, value in zip(row[1:], field[1:]):
            total = total + entry * value
        out.append(total)
    return out


def square(matrix):
    columns = [times(matrix, [matrix[i][j] for i in range(MODES)]) for j in range(MODES)]
    return [[columns[j][i] for j in range(MODES)] for i in range(MODES)]


def added(xs, ys):
    return [x + y for x, y in zip(xs, ys)]


def chosen(test, xs, ys):
    return [jnp.where(test, x, y) for x, y in zip(xs, ys)]


def coarse_matrix(speed_ref, chunk):
    rows = [speed_ref[pl.ds(chunk * CHUNK + r, 1), :] for r in range(CHUNK)]
    speed = jnp.concatenate(rows * (ROWS // CHUNK), 0)
    speed2 = 2.0 * speed
    zero, one = jnp.zeros_like(speed), jnp.ones_like(speed)
    columns = [
        three_sections([one if i == j else zero for i in range(MODES)], lambda u: local_rhs(u, speed, speed2), STEPS * STEP)
        for j in range(MODES)
    ]
    return [[columns[j][i] for j in range(MODES)] for i in range(MODES)]


def term_rows(step, half, k):
    return pl.ds((step * QUAD * CHUNK + half * ROWS) * MODES + k, ROWS, stride=MODES)


def carry_rows(half, k):
    return pl.ds((k * HALVES + half) * ROWS, ROWS)


def quad_carry(term_ref, speed_ref, carry_ref):
    quad, chunk = place()
    matrix = coarse_matrix(speed_ref, chunk)
    row = lax.broadcasted_iota(jnp.int32, (ROWS, LANES), 0)
    for half in range(HALVES):
        terms = [[term_ref[term_rows(step, half, k), :] for k in range(MODES)] for step in range(QUAD)]
        total = terms[0]
        for step in range(1, QUAD):
            total = added(times(matrix, total), terms[step])
        if half == HALVES - 1:
            total = chosen(jnp.logical_and(quad == QUAD - 1, row >= CHUNK), terms[-1], total)
        for k in range(MODES):
            carry_ref[carry_rows(half, k), :] = total[k]


def read_carry(ref, half):
    return [ref[carry_rows(half, k), :] for k in range(MODES)]


def joined(over_quad, quad, own, partner, half, row):
    odd = quad % 2 == 1
    earlier, later = chosen(odd, partner, own), chosen(odd, own, partner)
    both = added(times(over_quad, earlier), later)
    if half < HALVES - 1:
        return both
    return chosen(jnp.logical_and(quad >= 2, row >= CHUNK), later, both)


def pair_kernel(carry_ref, partner_ref, speed_ref, out_ref):
    quad, chunk = place()
    over_quad = square(square(coarse_matrix(speed_ref, chunk)))
    row = lax.broadcasted_iota(jnp.int32, (ROWS, LANES), 0)
    for half in range(HALVES):
        both = joined(over_quad, quad, read_carry(carry_ref, half), read_carry(partner_ref, half), half, row)
        for k in range(MODES):
            out_ref[carry_rows(half, k), :] = both[k]


def slab_kernel(term_ref, carry_ref, partner_ref, far_ref, speed_ref, out_ref):
    quad, chunk = place()
    matrix = coarse_matrix(speed_ref, chunk)
    over_quad = square(square(matrix))
    over_pair = square(over_quad)
    over_y = square(over_pair)
    row = lax.broadcasted_iota(jnp.int32, (ROWS, LANES), 0)
    low = row < CHUNK
    high_pair, odd = quad >= 2, quad % 2 == 1

    def swapped(xs):
        return [pltpu.roll(x, CHUNK, 0) for x in xs]

    here, total = [], []
    for half in range(HALVES):
        own, partner, far = (read_carry(ref, half) for ref in (carry_ref, partner_ref, far_ref))
        both = joined(over_quad, quad, own, partner, half, row)
        before_pair = [jnp.where(high_pair, x, 0.0) for x in far]
        here.append(chosen(odd, added(times(over_quad, before_pair), partner), before_pair))
        first_pair, second_pair = chosen(high_pair, far, both), chosen(high_pair, both, far)
        total.append(added(times(over_pair, first_pair), second_pair))
    first = swapped(second_pair)
    second = swapped(added(times(over_y, first), total[0]))
    pair = chosen(low, first, second)
    third = swapped(added(times(over_y, pair), total[0]))
    fourth = swapped(added(times(over_y, third), total[1]))
    starts = [pair, chosen(low, third, fourth)]
    for half in range(HALVES):
        state = starts[half]
        state = chosen(high_pair, times(over_pair, state), state)
        state = chosen(odd, times(over_quad, state), state)
        state = added(state, here[half])
        for step in range(QUAD):
            for i in range(HALVES):
                block = ORDER[step * QUAD + half * HALVES + i] * CHUNK * MODES
                for k in range(MODES):
                    out_ref[pl.ds(block + k, CHUNK, stride=MODES), :] = state[k][i * CHUNK : (i + 1) * CHUNK]
            if step < QUAD - 1:
                terms = [term_ref[term_rows(step, half, k), :] for k in range(MODES)]
                state = added(times(matrix, state), terms)


def on_device(kernel, name, rows, *operands):
    whole = pl.BlockSpec(memory_space=pltpu.VMEM)
    outs = [jax.ShapeDtypeStruct((n, LANES), jnp.float32) for n in (rows if isinstance(rows, tuple) else (rows,))]
    return pl.pallas_call(
        kernel,
        out_shape=outs if isinstance(rows, tuple) else outs[0],
        in_specs=[whole] * len(operands),
        out_specs=[whole] * len(outs) if isinstance(rows, tuple) else whole,
        compiler_params=pltpu.CompilerParams(vmem_limit_bytes=16 * 1024 * 1024),
        name=name,
    )(*operands)


def swap_blocks(x, groups, rows=MODES):
    return lax.all_to_all(x.reshape(-1, rows, LANES), "tm", 0, 0, axis_index_groups=groups, tiled=True).reshape(x.shape)


def body(initial, guess, speeds, flags):
    slabs, blocks = lax.axis_size("tm"), lax.axis_size("space")
    count = initial.shape[1]
    rows = count // LANES

    def by_row(x):
        return x.reshape(MODES, rows, LANES).transpose(1, 0, 2).reshape(rows * MODES, LANES)

    speed_rows, flag_rows = speeds.reshape(rows, LANES), flags.reshape(rows, LANES)
    quads, ys = range(QUAD), range(slabs // QUAD**2)
    of_quad = [[y * QUAD**2 + q * QUAD + step for step in range(QUAD) for y in ys] for q in quads]
    listed = [[group[p] for p in LISTED] for group in of_quad]
    windows = swap_blocks(window_part(by_row(guess[0]), by_row(initial), slabs), listed, 2)
    pairs = []
    for group in of_quad:
        for slab, start in ((group[ORDER.index(CHUNKS - 1)], 0), (group[ORDER.index(0)], 1)):
            for i in range(start, blocks - 1, 2):
                ends = slab * blocks + i, slab * blocks + i + 1
                pairs += [ends, ends[::-1]]
    edge = on_device(edge_kernel, "edge_rows", COEFS + ROWS, windows, speed_rows, flag_rows)
    message = lax.ppermute(edge, ("tm", "space"), pairs)
    terms = on_device(fine_kernel, "fine_steps", rows * MODES, windows, speed_rows, flag_rows)
    size = MODES * HALVES * ROWS
    terms, carry = on_device(end_kernel, "block_ends", (rows * MODES, size), terms, windows, message, speed_rows, flag_rows)
    partner = lax.ppermute(carry, "tm", [(c, c ^ QUAD) for c in range(slabs)])
    joint = on_device(pair_kernel, "pair_carry", size, carry, partner, speed_rows)
    far = lax.ppermute(joint, "tm", [(c, c ^ (3 * QUAD)) for c in range(slabs)])
    sums = on_device(slab_kernel, "slab_sums", rows * MODES, terms, carry, partner, far, speed_rows)
    by_chunk = [[group[ORDER.index(i)] for i in range(CHUNKS)] for group in of_quad]
    sums = write_part(swap_blocks(sums, by_chunk)).reshape(rows, MODES, LANES)
    return sums.transpose(1, 0, 2).reshape(1, MODES, count)


def solution(mesh):
    return jax.shard_map(
        body,
        mesh=mesh,
        in_specs=(P(None, "space"), P("tm", None, "space"), P("space"), P("space")),
        out_specs=P("tm", None, "space"),
        check_vma=False,
    )
```

```python
import functools

import jax
import jax.numpy as jnp
from jax import lax
from jax.experimental import pallas as pl
from jax.experimental.pallas import tpu as pltpu
from jax.sharding import PartitionSpec as P

MODES = 4
STEPS = 8
LANES = 128
ROWS = 8
VISCOSITY = 0.02
PENALTY = 10.0
STEP = 0.015625
JACOBIAN = 8.0
INV_MASS = (0.5, 1.5, 2.5, 3.5)


def column_scales(delta):
    return [JACOBIAN * m * delta for m in INV_MASS]


def shifted(xs, step):
    rolled = [pltpu.roll(x, step % LANES, 1) for x in xs]
    if len(xs) == 1:
        return rolled
    lane = lax.broadcasted_iota(jnp.int32, xs[0].shape, 1)
    edge = lane == (0 if step == 1 else LANES - 1)
    return [jnp.where(edge, rolled[(v - step) % len(xs)], x) for v, x in enumerate(rolled)]


def volume_terms(u, speed2, p, q):
    a, b, c, d = u
    vq = (2.0 * VISCOSITY) * q
    m1 = speed2 * a - vq
    m2 = speed2 * b - (6.0 * VISCOSITY) * c
    m3 = speed2 * p - vq - (10.0 * VISCOSITY) * d
    return m1, m2, m3


def local_rhs(u, speed, speed2):
    a, b, c, d = u
    p, q = a + c, b + d
    out = -(speed * (p + q))
    m1, m2, m3 = volume_terms(u, speed2, p, q)
    return out, out + m1, out + m2, out + m3


def traces(u):
    a, b, c, d = u
    p, q = a + c, b + d
    odd, even = b + 6.0 * d, 3.0 * c
    return p + q, p - q, odd + even, odd - even


def full_step(start, now, scale, speed, speed2, inflow, gate, gate_after):
    tr, tl, sr, sl = zip(*(traces(u) for u in now))
    tr_b, sr_b, tl_a, sl_a = shifted(tr, 1), shifted(sr, 1), shifted(tl, -1), shifted(sl, -1)
    result = []
    for v, u in enumerate(now):
        jump = tr_b[v] - tl[v]
        k_l = gate[v] * jump
        g_l = inflow[v] * tr_b[v] - gate[v] * (sr_b[v] + sl[v] - (2.0 * PENALTY) * jump)
        jump = tr[v] - tl_a[v]
        k_r = gate_after[v] * jump
        base = gate_after[v] * (sr[v] + sl_a[v] - (2.0 * PENALTY) * jump) - speed[v] * tr[v]
        plus, minus = base + g_l, base - g_l
        k_sum, k_dif = k_r + k_l, k_r - k_l
        m1, m2, m3 = volume_terms(u, speed2[v], u[0] + u[2], u[1] + u[3])
        rhs = plus, minus + k_sum + m1, plus + 3.0 * k_dif + m2, minus + 6.0 * k_sum + m3
        result.append([x + f * r for x, f, r in zip(start[v], scale, rhs)])
    return result


def three_sections(u, rhs, delta):
    v = u
    for share in (3.0, 2.0, 1.0):
        scale = column_scales(delta / share)
        v = [x + f * r for x, f, r in zip(u, scale, rhs(v))]
    return v


QUAD = 4
CHUNK = 4
HALVES = 2
CHUNKS = 16
WINDOW = CHUNK * MODES + 2
SHARE = LANES // MODES
ORDER = (1, 2, 3, 4, 0, 15, 5, 6, 7, 8, 9, 10, 11, 12, 13, 14)
LISTED = (4, 5, 2, 3, 0, 1, 6, 7, 8, 9, 10, 11, 12, 13, 14, 15)
BACKWARDS = tuple(CHUNKS - 1 - chunk for chunk in ORDER)


def even_block():
    return lax.axis_index("space") % 2 == 0


def place():
    slab = lax.axis_index("tm")
    y, z = slab // (QUAD * QUAD), slab % (QUAD * QUAD)
    position = (z % QUAD) * QUAD + y
    chunk = position
    for i, there in enumerate(ORDER):
        if i != there:
            chunk = jnp.where(position == i, there, chunk)
    return z // QUAD, jnp.where(even_block(), chunk, CHUNKS - 1 - chunk)


COPIES = 8


def window_kernel(slabs, guess_ref, initial_ref, out_ref, state, sems):
    last = lax.axis_index("tm") == slabs - 1
    rows = state.shape[0] // COPIES

    def copies(source):
        parts = [pl.ds(i * rows, rows) for i in range(COPIES)]
        return [pltpu.make_async_copy(source.at[part], state.at[part], sems.at[i]) for i, part in enumerate(parts)]

    @pl.when(last)
    def _():
        for copy in copies(initial_ref):
            copy.start()

    @pl.when(jnp.logical_not(last))
    def _():
        for copy in copies(guess_ref):
            copy.start()

    for copy in copies(guess_ref):
        copy.wait()
    size = CHUNK * MODES
    group = lax.broadcasted_iota(jnp.int32, (ROWS, LANES), 1) // SHARE

    def packed(row, shift):
        vectors = []
        for i in range(CHUNKS // ROWS):
            total = jnp.zeros((ROWS, LANES), jnp.float32)
            for k in range(MODES):
                read = state[pl.ds(i * ROWS * size + row * MODES + k, ROWS, stride=size), :]
                total = jnp.where(group == k, pltpu.roll(read, (k * SHARE + shift) % LANES, 1), total)
            vectors.append(total)
        return [vectors[n // ROWS][n % ROWS : n % ROWS + 1] for n in range(CHUNKS)]

    heads, tails = packed(0, 0), packed(CHUNK - 1, SHARE)
    none = jnp.zeros((1, LANES), jnp.float32)

    def write(chunks):
        for position, place_there in enumerate(LISTED):
            at, chunk = position * WINDOW, chunks[place_there]
            out_ref[pl.ds(at, size), :] = state[pl.ds(chunk * size, size), :]
            out_ref[pl.ds(at + size, 1), :] = heads[chunk + 1] if chunk < CHUNKS - 1 else none
            out_ref[pl.ds(at + size + 1, 1), :] = tails[chunk - 1] if chunk else none

    @pl.when(even_block())
    def _():
        write(ORDER)

    @pl.when(jnp.logical_not(even_block()))
    def _():
        write(BACKWARDS)


def window_part(guess, initial, slabs):
    return pl.pallas_call(
        functools.partial(window_kernel, slabs),
        out_shape=jax.ShapeDtypeStruct((CHUNKS * WINDOW, LANES), jnp.float32),
        in_specs=[pl.BlockSpec(memory_space=pltpu.HBM)] * 2,
        out_specs=pl.BlockSpec(memory_space=pltpu.VMEM),
        scratch_shapes=[pltpu.VMEM(guess.shape, jnp.float32), pltpu.SemaphoreType.DMA((COPIES,))],
        compiler_params=pltpu.CompilerParams(vmem_limit_bytes=16 * 1024 * 1024),
        name="windows",
    )(*(pltpu.with_memory_space_constraint(x, pltpu.HBM) for x in (guess, initial)))


def window_rows(half, r, k):
    return pl.ds(half * ROWS * WINDOW + r * MODES + k, ROWS, stride=WINDOW)


def unpacked(after, before, k, low):
    return jnp.where(low, pltpu.roll(after, -k * SHARE % LANES, 1), pltpu.roll(before, (MODES - 1 - k) * SHARE, 1))


COEFS = HALVES * ROWS


def edge_kernel(window_ref, speed_ref, flag_ref, out_ref):
    _, chunk = place()
    tail = chunk == CHUNKS - 1
    rows = speed_ref.shape[0]
    group = lax.broadcasted_iota(jnp.int32, (ROWS, LANES), 1) // SHARE
    for half in range(HALVES):
        packed = jnp.zeros((ROWS, LANES), jnp.float32)
        for k in range(MODES):
            first, final = window_ref[window_rows(half, 0, k), :], window_ref[window_rows(half, CHUNK - 1, k), :]
            moved = jnp.where(tail, pltpu.roll(final, (k + 1) * SHARE % LANES, 1), pltpu.roll(first, k * SHARE, 1))
            packed = jnp.where(group == k, moved, packed)
        out_ref[pl.ds(half * ROWS, ROWS), :] = packed
    at = jnp.where(tail, rows - 1, 0)
    out_ref[pl.ds(COEFS, 1), :] = speed_ref[pl.ds(at, 1), :]
    out_ref[pl.ds(COEFS + 1, 1), :] = 1.0 - flag_ref[pl.ds(at, 1), :].astype(jnp.float32)
    out_ref[pl.ds(COEFS + 2, ROWS - 2), :] = jnp.zeros((ROWS - 2, LANES), jnp.float32)


def coarse_step(start, speed, half, quad):
    speed2 = 2.0 * speed
    coarse = three_sections(start, lambda u: local_rhs(u, speed, speed2), STEPS * STEP)
    if half < HALVES - 1:
        return coarse
    last = jnp.logical_and(quad == QUAD - 1, lax.broadcasted_iota(jnp.int32, speed.shape, 0) == ROWS - 1)
    return [jnp.where(last, 0.0, x) for x in coarse]


def by_place(half, x):
    row = lax.broadcasted_iota(jnp.int32, x.shape, 0)
    return jnp.where(row % QUAD < QUAD // 2, pltpu.roll(x, QUAD, 0), x) if half == 0 else x


def slab_rows(half, r, k):
    return pl.ds((half * ROWS * CHUNK + r) * MODES + k, ROWS, stride=CHUNK * MODES)


def derived(speed, opened):
    gate = [(0.5 * VISCOSITY) * x for x in opened]
    inflow = [x * y for x, y in zip(opened, shifted(speed, 1))]
    return speed, [2.0 * x for x in speed], inflow, gate, shifted(gate, -1)


def fine_steps(starts, coefs):
    def advance(_, us):
        nows = us
        for share in (3.0, 2.0, 1.0):
            scale = column_scales(STEP / share)
            nows = [full_step(u, now, scale, *coefs) for u, now in zip(us, nows)]
        return nows

    return lax.fori_loop(0, STEPS, advance, starts, unroll=True)


def fine_kernel(window_ref, speed_ref, flag_ref, out_ref):
    quad, chunk = place()
    first, final = chunk == 0, chunk == CHUNKS - 1
    shape = (ROWS, LANES)
    lane = lax.broadcasted_iota(jnp.int32, shape, 1)
    low = lane < LANES // 2
    outside = jnp.logical_or(jnp.logical_and(low, final), jnp.logical_and(lane >= LANES // 2, first))

    def coef(read):
        at = chunk * CHUNK
        own = [jnp.broadcast_to(read(at + r), shape) for r in range(CHUNK)]
        after = jnp.broadcast_to(read(jnp.minimum(at + CHUNK, CHUNKS * CHUNK - 1)), shape)
        before = jnp.broadcast_to(read(jnp.maximum(at - 1, 0)), shape)
        return [*own, jnp.where(outside, 0.0, jnp.where(low, after, before))]

    speed = coef(lambda i: speed_ref[pl.ds(i, 1), :])
    opened = coef(lambda i: 1.0 - flag_ref[pl.ds(i, 1), :].astype(jnp.float32))
    wall = jnp.logical_and(jnp.logical_and(first, lax.axis_index("space") == 0), lane == 0)
    opened[0] = jnp.where(wall, 0.0, opened[0])
    coefs = derived(speed, opened)
    starts = []
    for half in range(HALVES):
        start = [[window_ref[window_rows(half, r, k), :] for k in range(MODES)] for r in range(CHUNK)]
        after, before = (window_ref[window_rows(half, CHUNK, i), :] for i in range(2))
        start.append([jnp.where(outside, 0.0, unpacked(after, before, k, low)) for k in range(MODES)])
        starts.append(start)
    finals = fine_steps(starts, coefs)
    for half in range(HALVES):
        for r in range(CHUNK):
            coarse = coarse_step(starts[half][r], speed[r], half, quad)
            for k in range(MODES):
                out_ref[slab_rows(half, r, k), :] = by_place(half, finals[half][r][k] - coarse[k])


def end_kernel(term_ref, window_ref, message_ref, speed_ref, flag_ref, out_ref):
    quad, chunk = place()
    first, final = chunk == 0, chunk == CHUNKS - 1
    out_ref[...] = term_ref[...]

    @pl.when(jnp.logical_or(first, final))
    def _():
        shape = (ROWS, LANES)
        lane = lax.broadcasted_iota(jnp.int32, shape, 1)
        low = lane < LANES // 2
        own_side = jnp.logical_xor(low, final)
        at = jnp.where(first, 0, CHUNKS * CHUNK - 1)

        def joined_row(own, other):
            return pltpu.roll(jnp.where(own_side, own, other), LANES // 2, 1)

        opened = 1.0 - flag_ref[pl.ds(at, 1), :].astype(jnp.float32)
        wall = jnp.logical_and(jnp.logical_and(first, lax.axis_index("space") == 0), lane == 0)
        opened = jnp.where(wall, 0.0, jnp.broadcast_to(opened, shape))
        beyond = [jnp.broadcast_to(message_ref[pl.ds(COEFS + i, 1), :], shape) for i in range(2)]
        own_speed = jnp.broadcast_to(speed_ref[pl.ds(at, 1), :], shape)
        coefs = derived([joined_row(own_speed, beyond[0])], [joined_row(opened, beyond[1])])
        starts, coarse = [], []
        for half in range(HALVES):
            packed = message_ref[pl.ds(half * ROWS, ROWS), :]
            start, owns = [], []
            for k in range(MODES):
                own = jnp.where(first, window_ref[window_rows(half, 0, k), :], window_ref[window_rows(half, CHUNK - 1, k), :])
                owns.append(own)
                start.append(joined_row(own, unpacked(packed, packed, k, low)))
            starts.append([start])
            coarse.append(coarse_step(owns, own_speed, half, quad))
        finals = fine_steps(starts, coefs)
        near_end = jnp.logical_or(jnp.logical_and(first, lane < SHARE), jnp.logical_and(final, lane >= LANES - SHARE))
        for r, here in ((0, first), (CHUNK - 1, final)):

            @pl.when(here)
            def _(r=r):
                for half in range(HALVES):
                    for k in range(MODES):
                        rows = slab_rows(half, r, k)
                        made = pltpu.roll(finals[half][0][k], LANES // 2, 1) - coarse[half][k]
                        out_ref[rows, :] = jnp.where(near_end, by_place(half, made), term_ref[rows, :])


def write_kernel(sums_ref, out_ref, sems):
    size = CHUNK * MODES

    def write(pairs, count):
        copies = []
        for i, (source, target) in enumerate(pairs):
            source, target = pl.ds(source * size, count * size), pl.ds(target * size, count * size)
            copies.append(pltpu.make_async_copy(sums_ref.at[source], out_ref.at[target], sems.at[i]))
        for copy in copies:
            copy.start()
        for copy in copies:
            copy.wait()

    @pl.when(even_block())
    def _():
        write([(i, i) for i in range(0, CHUNKS, CHUNKS // COPIES)], CHUNKS // COPIES)

    @pl.when(jnp.logical_not(even_block()))
    def _():
        write([(i, CHUNKS - 1 - i) for i in range(CHUNKS)], 1)


def write_part(sums):
    return pl.pallas_call(
        write_kernel,
        out_shape=jax.ShapeDtypeStruct(sums.shape, jnp.float32),
        in_specs=[pl.BlockSpec(memory_space=pltpu.VMEM)],
        out_specs=pl.BlockSpec(memory_space=pl.ANY),
        scratch_shapes=[pltpu.SemaphoreType.DMA((CHUNKS,))],
        compiler_params=pltpu.CompilerParams(vmem_limit_bytes=16 * 1024 * 1024),
        name="write_out",
    )(sums)


def times(matrix, field):
    out = []
    for row in matrix:
        total = row[0] * field[0]
        for entry, value in zip(row[1:], field[1:]):
            total = total + entry * value
        out.append(total)
    return out


def square(matrix):
    columns = [times(matrix, [matrix[i][j] for i in range(MODES)]) for j in range(MODES)]
    return [[columns[j][i] for j in range(MODES)] for i in range(MODES)]


def added(xs, ys):
    return [x + y for x, y in zip(xs, ys)]


def chosen(test, xs, ys):
    return [jnp.where(test, x, y) for x, y in zip(xs, ys)]


def coarse_matrix(speed_ref, chunk):
    rows = [speed_ref[pl.ds(chunk * CHUNK + r, 1), :] for r in range(CHUNK)]
    speed = jnp.concatenate(rows * (ROWS // CHUNK), 0)
    speed2 = 2.0 * speed
    zero, one = jnp.zeros_like(speed), jnp.ones_like(speed)
    columns = [
        three_sections([one if i == j else zero for i in range(MODES)], lambda u: local_rhs(u, speed, speed2), STEPS * STEP)
        for j in range(MODES)
    ]
    return [[columns[j][i] for j in range(MODES)] for i in range(MODES)]


def term_rows(step, half, k):
    return pl.ds((step * QUAD * CHUNK + half * ROWS) * MODES + k, ROWS, stride=MODES)


def carry_rows(half, k):
    return pl.ds((k * HALVES + half) * ROWS, ROWS)


def quad_kernel(term_ref, speed_ref, carry_ref):
    quad, chunk = place()
    matrix = coarse_matrix(speed_ref, chunk)
    row = lax.broadcasted_iota(jnp.int32, (ROWS, LANES), 0)
    for half in range(HALVES):
        terms = [[term_ref[term_rows(step, half, k), :] for k in range(MODES)] for step in range(QUAD)]
        total = terms[0]
        for step in range(1, QUAD):
            total = added(times(matrix, total), terms[step])
        if half == HALVES - 1:
            total = chosen(jnp.logical_and(quad == QUAD - 1, row >= CHUNK), terms[-1], total)
        for k in range(MODES):
            carry_ref[carry_rows(half, k), :] = total[k]


def read_carry(ref, half):
    return [ref[carry_rows(half, k), :] for k in range(MODES)]


def joined(over_quad, quad, own, partner, half, row):
    odd = quad % 2 == 1
    earlier, later = chosen(odd, partner, own), chosen(odd, own, partner)
    both = added(times(over_quad, earlier), later)
    if half < HALVES - 1:
        return both
    return chosen(jnp.logical_and(quad >= 2, row >= CHUNK), later, both)


def pair_kernel(carry_ref, partner_ref, speed_ref, out_ref):
    quad, chunk = place()
    over_quad = square(square(coarse_matrix(speed_ref, chunk)))
    row = lax.broadcasted_iota(jnp.int32, (ROWS, LANES), 0)
    for half in range(HALVES):
        both = joined(over_quad, quad, read_carry(carry_ref, half), read_carry(partner_ref, half), half, row)
        for k in range(MODES):
            out_ref[carry_rows(half, k), :] = both[k]


def slab_kernel(term_ref, carry_ref, partner_ref, far_ref, speed_ref, out_ref):
    quad, chunk = place()
    matrix = coarse_matrix(speed_ref, chunk)
    over_quad = square(square(matrix))
    over_pair = square(over_quad)
    over_y = square(over_pair)
    row = lax.broadcasted_iota(jnp.int32, (ROWS, LANES), 0)
    low = row < CHUNK
    high_pair, odd = quad >= 2, quad % 2 == 1

    def swapped(xs):
        return [pltpu.roll(x, CHUNK, 0) for x in xs]

    here, total = [], []
    for half in range(HALVES):
        own, partner, far = (read_carry(ref, half) for ref in (carry_ref, partner_ref, far_ref))
        both = joined(over_quad, quad, own, partner, half, row)
        before_pair = [jnp.where(high_pair, x, 0.0) for x in far]
        here.append(chosen(odd, added(times(over_quad, before_pair), partner), before_pair))
        first_pair, second_pair = chosen(high_pair, far, both), chosen(high_pair, both, far)
        total.append(added(times(over_pair, first_pair), second_pair))
    first = swapped(second_pair)
    second = swapped(added(times(over_y, first), total[0]))
    pair = chosen(low, first, second)
    third = swapped(added(times(over_y, pair), total[0]))
    fourth = swapped(added(times(over_y, third), total[1]))
    starts = [pair, chosen(low, third, fourth)]
    for half in range(HALVES):
        state = starts[half]
        state = chosen(high_pair, times(over_pair, state), state)
        state = chosen(odd, times(over_quad, state), state)
        state = added(state, here[half])
        for step in range(QUAD):
            for i in range(HALVES):
                block = ORDER[step * QUAD + half * HALVES + i] * CHUNK * MODES
                for k in range(MODES):
                    out_ref[pl.ds(block + k, CHUNK, stride=MODES), :] = state[k][i * CHUNK : (i + 1) * CHUNK]
            if step < QUAD - 1:
                terms = [term_ref[term_rows(step, half, k), :] for k in range(MODES)]
                state = added(times(matrix, state), terms)


def on_device(kernel, name, rows, *operands):
    return pl.pallas_call(
        kernel,
        out_shape=jax.ShapeDtypeStruct((rows, LANES), jnp.float32),
        in_specs=[pl.BlockSpec(memory_space=pltpu.VMEM)] * len(operands),
        out_specs=pl.BlockSpec(memory_space=pltpu.VMEM),
        compiler_params=pltpu.CompilerParams(vmem_limit_bytes=16 * 1024 * 1024),
        name=name,
    )(*operands)


def swap_blocks(x, groups, rows=MODES):
    return lax.all_to_all(x.reshape(-1, rows, LANES), "tm", 0, 0, axis_index_groups=groups, tiled=True).reshape(x.shape)


def body(initial, guess, speeds, flags):
    slabs, blocks = lax.axis_size("tm"), lax.axis_size("space")
    count = initial.shape[1]
    rows = count // LANES

    def by_row(x):
        return x.reshape(MODES, rows, LANES).transpose(1, 0, 2).reshape(rows * MODES, LANES)

    speed_rows, flag_rows = speeds.reshape(rows, LANES), flags.reshape(rows, LANES)
    quads, ys = range(QUAD), range(slabs // QUAD**2)
    of_quad = [[y * QUAD**2 + q * QUAD + step for step in range(QUAD) for y in ys] for q in quads]
    listed = [[group[p] for p in LISTED] for group in of_quad]
    windows = swap_blocks(window_part(by_row(guess[0]), by_row(initial), slabs), listed, 2)
    pairs = []
    for group in of_quad:
        for slab, start in ((group[ORDER.index(CHUNKS - 1)], 0), (group[ORDER.index(0)], 1)):
            for i in range(start, blocks - 1, 2):
                ends = slab * blocks + i, slab * blocks + i + 1
                pairs += [ends, ends[::-1]]
    edge = on_device(edge_kernel, "edge_rows", COEFS + ROWS, windows, speed_rows, flag_rows)
    message = lax.ppermute(edge, ("tm", "space"), pairs)
    terms = on_device(fine_kernel, "fine_steps", rows * MODES, windows, speed_rows, flag_rows)
    terms = on_device(end_kernel, "block_ends", rows * MODES, terms, windows, message, speed_rows, flag_rows)
    size = MODES * HALVES * ROWS
    carry = on_device(quad_kernel, "quad_carry", size, terms, speed_rows)
    partner = lax.ppermute(carry, "tm", [(c, c ^ QUAD) for c in range(slabs)])
    joint = on_device(pair_kernel, "pair_carry", size, carry, partner, speed_rows)
    far = lax.ppermute(joint, "tm", [(c, c ^ (3 * QUAD)) for c in range(slabs)])
    sums = on_device(slab_kernel, "slab_sums", rows * MODES, terms, carry, partner, far, speed_rows)
    by_chunk = [[group[ORDER.index(i)] for i in range(CHUNKS)] for group in of_quad]
    sums = write_part(swap_blocks(sums, by_chunk)).reshape(rows, MODES, LANES)
    return sums.transpose(1, 0, 2).reshape(1, MODES, count)


def solution(mesh):
    return jax.shard_map(
        body,
        mesh=mesh,
        in_specs=(P(None, "space"), P("tm", None, "space"), P("space"), P("space")),
        out_specs=P("tm", None, "space"),
        check_vma=False,
    )
```
